32 devices in a mesh: dp: 8 (over z, core), tensor: 4 (over y, x).
Axes of the slice: x: 2, y: 2, z: 4, core: 2. Of those that a mesh axis runs over, the one named last changes fastest.
Arguments:
- block_in: bfloat16 [16384, 1536], P(('dp', 'tensor')), may hold values from -6 to 6
- cond_tokens: bfloat16 [16, 130, 768], P('dp'), may hold values from -6 to 6
- cond_count: int32 [16], P('dp'), may hold values from 65 to 130, as said below
- norm1_gain: bfloat16 [1536], P('dp'), may hold values from 0.25 to 1.75
- norm2_gain: bfloat16 [1536], P('dp'), may hold values from 0.25 to 1.75
- norm3_gain: bfloat16 [1536], P('dp'), may hold values from 0.25 to 1.75
- qkv_weight: bfloat16 [1536, 3, 1536], P('dp', None, 'tensor'), may hold values from -0.15625 to 0.15625
- attn_out_weight: bfloat16 [1536, 1536], P('tensor', 'dp'), may hold values from -0.625 to 0.625
- cross_q_weight: bfloat16 [1536, 1536], P('dp', 'tensor'), may hold values from -0.15625 to 0.15625
- cross_kv_weight: bfloat16 [768, 2, 1536], P('dp', None, 'tensor'), may hold values from -0.21875 to 0.21875
- cross_out_weight: bfloat16 [1536, 1536], P('tensor', 'dp'), may hold values from -0.4375 to 0.4375
- gate_up_weight: bfloat16 [1536, 2, 6144], P('dp', None, 'tensor'), may hold values from -0.15625 to 0.15625
- down_weight: bfloat16 [6144, 1536], P('tensor', 'dp'), may hold values from -0.15625 to 0.15625
- out_cotangent: bfloat16 [16384, 1536], P(('dp', 'tensor')), may hold values from -6 to 6
Outputs:
- block_out: bfloat16 [16384, 1536], P(('dp', 'tensor'))
- grad_in: float32 [16384, 1536], P(('dp', 'tensor'))
- grad_cond: float32 [16, 130, 768], P('dp', None, 'tensor')
- grad_norm1: float32 [1536], P('dp')
- grad_norm2: float32 [1536], P('dp')
- grad_norm3: float32 [1536], P('dp')
- grad_qkv: float32 [1536, 3, 1536], P('dp', None, 'tensor')
- grad_attn_out: float32 [1536, 1536], P('tensor', 'dp')
- grad_cross_q: float32 [1536, 1536], P('dp', 'tensor')
- grad_cross_kv: float32 [768, 2, 1536], P('dp', None, 'tensor')
- grad_cross_out: float32 [1536, 1536], P('tensor', 'dp')
- grad_gate_up: float32 [1536, 2, 6144], P('dp', None, 'tensor')
- grad_down: float32 [6144, 1536], P('tensor', 'dp')
The draws below stay inside these ranges and needn't reach their ends.
Inputs may be any that keep to these rules, and one draw needn't show every extreme that they name: `cond_count`: in every draw one sequence has all 130 slots valid and another exactly 65.
All inputs are finite; a program needn't handle non-finite values.
Results may differ from the reference program's by a relative error of at most 0.024.
Values may be sent and summed in bfloat16 or wider, within the bound.
A program may use at most 320 MiB of HBM per device.

```python
import jax
import jax.numpy as jnp
from jax import lax

D = 1536
H = 24
HD = 64
FF = 6144
DC = 768
COND = 130
SEQ = 1024
NSEQ = 16
TOKENS = 16384


def draw_cond_count(key, part):
    key = jax.random.fold_in(key, 7)
    length_key, select_key = jax.random.split(key)
    lengths = jax.random.randint(length_key, (NSEQ,), COND // 2, COND + 1)
    chosen = jax.random.randint(select_key, (), 0, NSEQ)
    indices = jnp.arange(NSEQ)
    lengths = jnp.where(indices == chosen, COND, lengths)
    lengths = jnp.where(indices == (chosen + 1) % NSEQ, COND // 2, lengths)
    return lengths.astype(jnp.int32)


def levels(rng, shape, pieces, low, top_value):
    def one(axis_at, blocks):
        steps = jax.random.uniform(jax.random.fold_in(jax.random.fold_in(rng, 6), axis_at), (blocks,), jnp.float32, low / len(pieces), top_value / len(pieces))
        return jnp.repeat(jnp.exp(steps), shape[axis_at] // blocks).reshape((-1,) + (1,) * (len(shape) - axis_at - 1))

    loudness = one(*pieces[0])
    for cut in pieces[1:]:
        loudness = loudness * one(*cut)
    return loudness


def scatter_about(key, extent, scale, most, cuts=(), held_as=jnp.bfloat16):
    result = jax.random.normal(key, extent, jnp.float32) * scale
    if len(cuts) > 0:
        result = levels(key, extent, cuts, -0.22, 0.18) * result
    return jnp.clip(result, min=-most, max=most).astype(held_as)


def setup_inputs(seed: int = 0) -> dict:
    keys = jax.random.split(jax.random.key(seed), 15)
    block_in = scatter_about(keys[0], (TOKENS, D), 1.0, 6.0, ((0, 32),))
    cond_tokens = scatter_about(keys[1], (NSEQ, COND, DC), 1.0, 6.0, ((0, 8),))
    cond_count = draw_cond_count(jax.random.fold_in(keys[14], 71), 0)
    norm1_gain = jnp.clip(1.0 + 0.15 * jax.random.normal(keys[3], (D,), jnp.float32), 0.25, 1.75).astype(jnp.bfloat16)
    norm2_gain = jnp.clip(1.0 + 0.15 * jax.random.normal(keys[4], (D,), jnp.float32), 0.25, 1.75).astype(jnp.bfloat16)
    norm3_gain = jnp.clip(1.0 + 0.15 * jax.random.normal(keys[5], (D,), jnp.float32), 0.25, 1.75).astype(jnp.bfloat16)
    qkv_weight = scatter_about(keys[6], (D, 3, D), D ** -0.5, 0.15625, ((0, 8), (2, 4)))
    attn_out_weight = scatter_about(keys[7], (D, D), (D // 16) ** -0.5, 0.625, ((0, 4), (1, 8)))
    cross_q_weight = scatter_about(keys[8], (D, D), D ** -0.5, 0.15625, ((0, 8), (1, 4)))
    cross_kv_weight = scatter_about(keys[9], (DC, 2, D), DC ** -0.5, 0.21875, ((0, 8), (2, 4)))
    cross_out_weight = scatter_about(keys[10], (D, D), (D // 8) ** -0.5, 0.4375, ((0, 4), (1, 8)))
    gate_up_weight = scatter_about(keys[11], (D, 2, FF), D ** -0.5, 0.15625, ((0, 8), (2, 4)))
    down_weight = scatter_about(keys[12], (FF, D), (FF // 4) ** -0.5, 0.15625, ((0, 4), (1, 8)))
    out_cotangent = scatter_about(keys[13], (TOKENS, D), 1.0, 6.0, ((0, 32),))
    return dict(block_in=block_in, cond_tokens=cond_tokens, cond_count=cond_count, norm1_gain=norm1_gain, norm2_gain=norm2_gain, norm3_gain=norm3_gain, qkv_weight=qkv_weight, attn_out_weight=attn_out_weight, cross_q_weight=cross_q_weight, cross_kv_weight=cross_kv_weight, cross_out_weight=cross_out_weight, gate_up_weight=gate_up_weight, down_weight=down_weight, out_cotangent=out_cotangent)


@jax.custom_vjp
def low(v):
    return lax.optimization_barrier(v.astype(jnp.bfloat16)).astype(jnp.float32)

@jax.custom_vjp
def low_back(v):
    return v

def low_keep(v):
    return (low(v), None)

def low_pass(kept, grad):
    return (grad,)

def back_keep(v):
    return (v, None)

def back_low(kept, grad):
    return (low(grad),)
low.defvjp(low_keep, low_pass)
low_back.defvjp(back_keep, back_low)
EPSILON = 1e-05
MASKED_SCORE = -1e+30
PRECISE = lax.Precision.HIGHEST

def matmul_high(left, right):
    return jnp.dot(left, right, precision=PRECISE, preferred_element_type=jnp.float32)

def layer_norm(values, gain):
    centre = values - lax.optimization_barrier(jnp.mean(values, axis=-1, keepdims=True))
    spread = lax.optimization_barrier(jnp.mean(centre * centre, axis=-1, keepdims=True))
    return centre * lax.rsqrt(spread + EPSILON) * gain

def rotary_tables(length):
    quarter = HD // 4
    positions = jnp.arange(length).astype(jnp.float32)
    inverse = 10000.0 ** (-jnp.arange(quarter).astype(jnp.float32) / quarter)
    angle_grid = positions[:, None] * inverse[None, :]
    return (jnp.cos(angle_grid)[:, None, :], jnp.sin(angle_grid)[:, None, :])

def rotate(values, cosine, sine):
    quarter = cosine.shape[-1]
    first_part = values[..., :quarter]
    second_part = values[..., quarter:2 * quarter]
    rest_part = values[..., 2 * quarter:]
    return jnp.concatenate([first_part * cosine - second_part * sine, first_part * sine + second_part * cosine, rest_part], axis=-1)

def attend(query_rows, key_rows, value_rows, allowed):
    scores = low_back(jnp.einsum('qhd,khd->hqk', query_rows, key_rows, precision=PRECISE))
    scores = jnp.where(allowed[None, None, :], scores, MASKED_SCORE)
    top_score = lax.optimization_barrier(jnp.max(scores, axis=-1, keepdims=True))
    weights = jnp.exp(scores - top_score)
    probs = weights / lax.optimization_barrier(jnp.sum(weights, axis=-1, keepdims=True))
    return jnp.einsum('hqk,khd->qhd', low(probs), value_rows, precision=PRECISE)

def forward_seq(seq_rows, seq_cond, allowed, gain_one, gain_two, gain_three, w_qkv, w_out, w_cq, w_ckv, w_co, w_gu, w_down):
    cosine, sine = rotary_tables(SEQ)
    every_key = jnp.ones((SEQ,), dtype=jnp.bool_)
    first_in = low(layer_norm(seq_rows, gain_one))
    qkv_all = low_back(matmul_high(first_in, w_qkv.reshape(D, 3 * D))).reshape(SEQ, 3, H, HD)
    query_rot = low(rotate(qkv_all[:, 0], cosine, sine) * 0.125)
    key_rot = low(rotate(qkv_all[:, 1], cosine, sine))
    value_rows = low(qkv_all[:, 2])
    mixed = low(low_back(attend(query_rot, key_rot, value_rows, every_key))).reshape(SEQ, D)
    after_self = seq_rows + low_back(matmul_high(mixed, w_out))
    second_in = low(layer_norm(after_self, gain_two))
    cross_query = low_back(matmul_high(second_in, w_cq)).reshape(SEQ, H, HD)
    cross_kv = low_back(matmul_high(seq_cond, w_ckv.reshape(DC, 2 * D))).reshape(COND, 2, H, HD)
    cross_mixed = attend(low(cross_query * 0.125), low(cross_kv[:, 0]), low(cross_kv[:, 1]), allowed)
    cross_mixed = low(low_back(cross_mixed)).reshape(SEQ, D)
    after_cross = after_self + low_back(matmul_high(cross_mixed, w_co))
    third_in = low(layer_norm(after_cross, gain_three))
    gate_up = matmul_high(third_in, w_gu.reshape(D, 2 * FF)).reshape(SEQ, 2, FF)
    gate_vals = low_back(gate_up[:, 0])
    up_vals = low_back(gate_up[:, 1])
    hidden = low(jax.nn.silu(gate_vals) * up_vals)
    return after_cross + low_back(matmul_high(hidden, w_down))

def reference(block_in, cond_tokens, cond_count, norm1_gain, norm2_gain, norm3_gain, qkv_weight, attn_out_weight, cross_q_weight, cross_kv_weight, cross_out_weight, gate_up_weight, down_weight, out_cotangent):
    params = tuple((weight.astype(jnp.float32) for weight in (norm1_gain, norm2_gain, norm3_gain, qkv_weight, attn_out_weight, cross_q_weight, cross_kv_weight, cross_out_weight, gate_up_weight, down_weight)))
    seq_inputs = block_in.reshape(NSEQ, SEQ, D)
    seq_cotangents = out_cotangent.reshape(NSEQ, SEQ, D)

    def one_sequence(totals, seq_item):
        seq_rows, seq_cond, seq_length, seq_cot = seq_item
        allowed = jnp.arange(COND) < seq_length

        def run_block(rows_given, cond_given, *weights_given):
            return forward_seq(rows_given, cond_given, allowed, *weights_given)
        output, pullback = jax.vjp(run_block, seq_rows.astype(jnp.float32), seq_cond.astype(jnp.float32), *params)
        seq_grads = pullback(seq_cot.astype(jnp.float32))
        totals = tuple((running + fresh for running, fresh in zip(totals, seq_grads[2:])))
        return (totals, (output.astype(jnp.bfloat16), seq_grads[0], seq_grads[1]))
    zero_grads = tuple((jnp.zeros(weight.shape, jnp.float32) for weight in params))
    totals, (outputs, grad_rows, grad_conds) = lax.scan(one_sequence, zero_grads, (seq_inputs, cond_tokens, cond_count, seq_cotangents))
    return (outputs.reshape(TOKENS, D), grad_rows.reshape(TOKENS, D), grad_conds, totals[0], totals[1], totals[2], totals[3], totals[4], totals[5], totals[6], totals[7], totals[8], totals[9])
```

```python
import functools

import jax
import jax.numpy as jnp
from jax import lax
from jax.experimental import pallas as pl
from jax.experimental.pallas import tpu as pltpu
from jax.sharding import Mesh
from jax.sharding import PartitionSpec as P

HD = 64


EPSILON = 1e-05
MASKED_SCORE = -1e30
BF = jnp.bfloat16
F32 = jnp.float32
NN = (((1,), (0,)), ((), ()))
NT = (((1,), (1,)), ((), ()))
VMEM_BYTES = 60 << 20


def layer_norm(values, gain):
    centre = values - jnp.mean(values, axis=-1, keepdims=True)
    spread = jnp.mean(centre * centre, axis=-1, keepdims=True)
    return centre * lax.rsqrt(spread + EPSILON) * gain


def rotate(values, cosine, sine):
    quarter = cosine.shape[-1]
    first_part = values[..., :quarter]
    second_part = values[..., quarter : 2 * quarter]
    rest_part = values[..., 2 * quarter :]
    return jnp.concatenate(
        [
            first_part * cosine - second_part * sine,
            first_part * sine + second_part * cosine,
            rest_part,
        ],
        axis=-1,
    )


def rotate_back(grads, cosine, sine):
    quarter = cosine.shape[-1]
    first_part = grads[..., :quarter]
    second_part = grads[..., quarter : 2 * quarter]
    rest_part = grads[..., 2 * quarter :]
    return jnp.concatenate(
        [
            first_part * cosine + second_part * sine,
            second_part * cosine - first_part * sine,
            rest_part,
        ],
        axis=-1,
    )


def gated(gate_vals, up_vals):
    return jax.nn.silu(gate_vals) * up_vals


def rows_by_rows(left, right):
    return lax.dot_general(
        left, right, (((0,), (0,)), ((), ())), preferred_element_type=jnp.float32
    )


def times_transposed(left, right):
    return lax.dot_general(
        left, right, (((1,), (1,)), ((), ())), preferred_element_type=jnp.float32
    )


def attend_forward(query_rows, key_rows, value_rows, allowed):
    scores = jnp.einsum("qhd,khd->hqk", query_rows, key_rows, preferred_element_type=jnp.float32)
    scores = jnp.where(allowed[None, None, :], scores, MASKED_SCORE)
    top_score = jnp.max(scores, axis=-1, keepdims=True)
    weights = jnp.exp(scores - top_score)
    totals = jnp.sum(weights, axis=-1, keepdims=True)
    probs = weights / totals
    mixed = jnp.einsum(
        "hqk,khd->qhd", probs.astype(jnp.bfloat16), value_rows, preferred_element_type=jnp.float32
    )
    return (mixed.astype(jnp.bfloat16), top_score + jnp.log(totals))


def attend_backward(query_rows, key_rows, value_rows, allowed, log_total, grad_mixed):
    scores = jnp.einsum("qhd,khd->hqk", query_rows, key_rows, preferred_element_type=jnp.float32)
    scores = jnp.where(allowed[None, None, :], scores, MASKED_SCORE)
    probs = jnp.exp(scores - log_total)
    grad_probs = jnp.einsum(
        "qhd,khd->hqk", grad_mixed, value_rows, preferred_element_type=jnp.float32
    )
    grad_values = jnp.einsum(
        "hqk,qhd->khd", probs.astype(jnp.bfloat16), grad_mixed, preferred_element_type=jnp.float32
    )
    grad_scores = probs * (grad_probs - jnp.sum(probs * grad_probs, axis=-1, keepdims=True))
    grad_scores = grad_scores.astype(jnp.bfloat16)
    grad_query = jnp.einsum(
        "hqk,khd->qhd", grad_scores, key_rows, preferred_element_type=jnp.float32
    )
    grad_keys = jnp.einsum(
        "hqk,qhd->khd", grad_scores, query_rows, preferred_element_type=jnp.float32
    )
    return (grad_query, grad_keys, grad_values)


def general_body(
    block_in,
    cond_tokens,
    cond_count,
    norm1_gain,
    norm2_gain,
    norm3_gain,
    qkv_weight,
    attn_out_weight,
    cross_q_weight,
    cross_kv_weight,
    cross_out_weight,
    gate_up_weight,
    down_weight,
    out_cotangent,
):
    local_rows = block_in.shape[0]
    model_width = block_in.shape[1]
    group_rows = local_rows * lax.axis_size("tensor")
    seq_here = cond_tokens.shape[0]
    seq_length = group_rows // seq_here
    cond_slots = cond_tokens.shape[1]
    cond_width = cond_tokens.shape[2]
    head_cols = attn_out_weight.shape[0]
    heads_here = head_cols // HD
    hidden_here = down_weight.shape[0]
    gain_one, gain_two, gain_three, w_qkv, w_out, w_cq, w_ckv, w_co, w_gu, w_down = (
        lax.all_gather(norm1_gain, "dp", axis=0, tiled=True),
        lax.all_gather(norm2_gain, "dp", axis=0, tiled=True),
        lax.all_gather(norm3_gain, "dp", axis=0, tiled=True),
        lax.all_gather(qkv_weight, "dp", axis=0, tiled=True),
        lax.all_gather(attn_out_weight, "dp", axis=1, tiled=True),
        lax.all_gather(cross_q_weight, "dp", axis=0, tiled=True),
        lax.all_gather(cross_kv_weight, "dp", axis=0, tiled=True),
        lax.all_gather(cross_out_weight, "dp", axis=1, tiled=True),
        lax.all_gather(gate_up_weight, "dp", axis=0, tiled=True),
        lax.all_gather(down_weight, "dp", axis=1, tiled=True),
    )
    quarter = HD // 4
    positions = (jnp.arange(group_rows) % seq_length).astype(jnp.float32)
    inverse = 10000.0 ** (-jnp.arange(quarter).astype(jnp.float32) / quarter)
    angle_grid = positions[:, None] * inverse[None, :]
    cosine = jnp.cos(angle_grid)[:, None, :]
    sine = jnp.sin(angle_grid)[:, None, :]
    every_key = jnp.ones((seq_length,), dtype=jnp.bool_)
    valid_slots = jnp.arange(cond_slots)[None, :] < cond_count[:, None]

    def by_sequence(array):
        return array.reshape((seq_here, seq_length) + array.shape[1:])

    def spread_rows(local_part):
        return lax.all_gather(local_part, "tensor", axis=0, tiled=True)

    def project_out(mixed_all, weight):
        return lax.psum_scatter(
            jnp.dot(mixed_all, weight, preferred_element_type=jnp.float32),
            "tensor",
            scatter_dimension=0,
            tiled=True,
        )

    def spread_grads(local_part):
        return lax.all_gather(local_part, "tensor", axis=0, tiled=True)

    def gather_back(grad_all, weight):
        return lax.psum_scatter(
            times_transposed(grad_all, weight), "tensor", scatter_dimension=0, tiled=True
        )

    def self_forward(seq_parts):
        return attend_forward(seq_parts[0], seq_parts[1], seq_parts[2], every_key)

    def cross_forward(seq_parts):
        return attend_forward(seq_parts[0], seq_parts[1][:, 0], seq_parts[1][:, 1], seq_parts[2])

    def self_backward(seq_parts):
        return attend_backward(
            seq_parts[0], seq_parts[1], seq_parts[2], every_key, seq_parts[3], seq_parts[4]
        )

    def cross_backward(seq_parts):
        return attend_backward(
            seq_parts[0],
            seq_parts[1][:, 0],
            seq_parts[1][:, 1],
            seq_parts[2],
            seq_parts[3],
            seq_parts[4],
        )

    gain_first = gain_one.astype(jnp.float32)
    gain_second = gain_two.astype(jnp.float32)
    gain_third = gain_three.astype(jnp.float32)
    input_rows = block_in.astype(jnp.float32)
    first_all = spread_rows(layer_norm(input_rows, gain_first).astype(jnp.bfloat16))
    qkv_all = jnp.dot(
        first_all, w_qkv.reshape(model_width, 3 * head_cols), preferred_element_type=jnp.float32
    )
    qkv_all = qkv_all.reshape(group_rows, 3, heads_here, HD)
    query_rot = (rotate(qkv_all[:, 0], cosine, sine) * 0.125).astype(jnp.bfloat16)
    key_rot = rotate(qkv_all[:, 1], cosine, sine).astype(jnp.bfloat16)
    value_rows = qkv_all[:, 2].astype(jnp.bfloat16)
    self_mixed, self_lse = lax.map(
        self_forward, (by_sequence(query_rot), by_sequence(key_rot), by_sequence(value_rows))
    )
    self_flat = self_mixed.reshape(group_rows, head_cols)
    after_self = input_rows + project_out(self_flat, w_out)
    second_all = spread_rows(layer_norm(after_self, gain_second).astype(jnp.bfloat16))
    cross_query = (jnp.dot(second_all, w_cq, preferred_element_type=jnp.float32) * 0.125).astype(
        jnp.bfloat16
    )
    cross_query = cross_query.reshape(group_rows, heads_here, HD)
    cond_flat = cond_tokens.reshape(seq_here * cond_slots, cond_width)
    cross_kv = jnp.dot(
        cond_flat, w_ckv.reshape(cond_width, 2 * head_cols), preferred_element_type=jnp.float32
    )
    cross_kv = cross_kv.astype(jnp.bfloat16).reshape(seq_here, cond_slots, 2, heads_here, HD)
    cross_mixed, cross_lse = lax.map(
        cross_forward, (by_sequence(cross_query), cross_kv, valid_slots)
    )
    cross_flat = cross_mixed.reshape(group_rows, head_cols)
    after_cross = after_self + project_out(cross_flat, w_co)
    third_all = spread_rows(layer_norm(after_cross, gain_third).astype(jnp.bfloat16))
    gate_up = jnp.dot(
        third_all, w_gu.reshape(model_width, 2 * hidden_here), preferred_element_type=jnp.float32
    )
    gate_up = gate_up.reshape(group_rows, 2, hidden_here)
    gate_vals = gate_up[:, 0]
    up_vals = gate_up[:, 1]
    hidden = gated(gate_vals, up_vals).astype(jnp.bfloat16)
    block_out = (after_cross + project_out(hidden, w_down)).astype(jnp.bfloat16)
    gain_one, gain_two, gain_three, w_qkv, w_out, w_cq, w_ckv, w_co, w_gu, w_down = (
        lax.all_gather(norm1_gain, "dp", axis=0, tiled=True),
        lax.all_gather(norm2_gain, "dp", axis=0, tiled=True),
        lax.all_gather(norm3_gain, "dp", axis=0, tiled=True),
        lax.all_gather(qkv_weight, "dp", axis=0, tiled=True),
        lax.all_gather(attn_out_weight, "dp", axis=1, tiled=True),
        lax.all_gather(cross_q_weight, "dp", axis=0, tiled=True),
        lax.all_gather(cross_kv_weight, "dp", axis=0, tiled=True),
        lax.all_gather(cross_out_weight, "dp", axis=1, tiled=True),
        lax.all_gather(gate_up_weight, "dp", axis=0, tiled=True),
        lax.all_gather(down_weight, "dp", axis=1, tiled=True),
    )
    gain_first = gain_one.astype(jnp.float32)
    gain_second = gain_two.astype(jnp.float32)
    gain_third = gain_three.astype(jnp.float32)
    grad_top = out_cotangent.astype(jnp.float32)
    third_grads = spread_grads(out_cotangent)
    grad_hidden = times_transposed(third_grads, w_down)
    grad_down = rows_by_rows(hidden, third_grads)
    gated_out, gated_pull = jax.vjp(gated, gate_vals, up_vals)
    grad_gate, grad_up = gated_pull(grad_hidden)
    grad_gate_up = (
        jnp.stack([grad_gate, grad_up], axis=1)
        .astype(jnp.bfloat16)
        .reshape(group_rows, 2 * hidden_here)
    )
    grad_gu_weight = rows_by_rows(third_all, grad_gate_up).reshape(model_width, 2, hidden_here)
    grad_third = gather_back(grad_gate_up, w_gu.reshape(model_width, 2 * hidden_here))
    norm_out, norm_pull = jax.vjp(layer_norm, after_cross, gain_third)
    part_rows, grad_gain_third = norm_pull(grad_third)
    grad_cross_rows = grad_top + part_rows
    second_grads = spread_grads(grad_cross_rows.astype(jnp.bfloat16))
    grad_cross_mixed = times_transposed(second_grads, w_co).astype(jnp.bfloat16)
    grad_co_weight = rows_by_rows(cross_flat, second_grads)
    cross_gq, cross_gk, cross_gv = lax.map(
        cross_backward,
        (
            by_sequence(cross_query),
            cross_kv,
            valid_slots,
            cross_lse,
            by_sequence(grad_cross_mixed.reshape(group_rows, heads_here, HD)),
        ),
    )
    grad_cross_query = (cross_gq * 0.125).astype(jnp.bfloat16).reshape(group_rows, head_cols)
    grad_cross_kv = (
        jnp.stack([cross_gk, cross_gv], axis=2)
        .astype(jnp.bfloat16)
        .reshape(seq_here * cond_slots, 2 * head_cols)
    )
    grad_cq_weight = rows_by_rows(second_all, grad_cross_query)
    grad_ckv_weight = rows_by_rows(cond_flat, grad_cross_kv).reshape(cond_width, 2, head_cols)
    cond_partial = times_transposed(
        grad_cross_kv, w_ckv.reshape(cond_width, 2 * head_cols)
    ).reshape(seq_here, cond_slots, cond_width)
    grad_cond = lax.psum_scatter(cond_partial, "tensor", scatter_dimension=2, tiled=True)
    grad_second = gather_back(grad_cross_query, w_cq)
    norm_out, norm_pull = jax.vjp(layer_norm, after_self, gain_second)
    part_rows, grad_gain_second = norm_pull(grad_second)
    grad_self_rows = grad_cross_rows + part_rows
    first_grads = spread_grads(grad_self_rows.astype(jnp.bfloat16))
    grad_self_mixed = times_transposed(first_grads, w_out).astype(jnp.bfloat16)
    grad_out_weight = rows_by_rows(self_flat, first_grads)
    self_gq, self_gk, self_gv = lax.map(
        self_backward,
        (
            by_sequence(query_rot),
            by_sequence(key_rot),
            by_sequence(value_rows),
            self_lse,
            by_sequence(grad_self_mixed.reshape(group_rows, heads_here, HD)),
        ),
    )
    grad_query = rotate_back(self_gq.reshape(group_rows, heads_here, HD) * 0.125, cosine, sine)
    grad_keys = rotate_back(self_gk.reshape(group_rows, heads_here, HD), cosine, sine)
    grad_values = self_gv.reshape(group_rows, heads_here, HD)
    grad_qkv_all = (
        jnp.stack([grad_query, grad_keys, grad_values], axis=1)
        .astype(jnp.bfloat16)
        .reshape(group_rows, 3 * head_cols)
    )
    grad_qkv_weight = rows_by_rows(first_all, grad_qkv_all).reshape(model_width, 3, head_cols)
    grad_first = gather_back(grad_qkv_all, w_qkv.reshape(model_width, 3 * head_cols))
    norm_out, norm_pull = jax.vjp(layer_norm, input_rows, gain_first)
    part_rows, grad_gain_first = norm_pull(grad_first)
    grad_input = grad_self_rows + part_rows
    owned = (
        lax.psum_scatter(grad_gain_first, "dp", scatter_dimension=0, tiled=True),
        lax.psum_scatter(grad_gain_second, "dp", scatter_dimension=0, tiled=True),
        lax.psum_scatter(grad_gain_third, "dp", scatter_dimension=0, tiled=True),
        lax.psum_scatter(grad_qkv_weight, "dp", scatter_dimension=0, tiled=True),
        lax.psum_scatter(grad_out_weight, "dp", scatter_dimension=1, tiled=True),
        lax.psum_scatter(grad_cq_weight, "dp", scatter_dimension=0, tiled=True),
        lax.psum_scatter(grad_ckv_weight, "dp", scatter_dimension=0, tiled=True),
        lax.psum_scatter(grad_co_weight, "dp", scatter_dimension=1, tiled=True),
        lax.psum_scatter(grad_gu_weight, "dp", scatter_dimension=0, tiled=True),
        lax.psum_scatter(grad_down, "dp", scatter_dimension=1, tiled=True),
    )
    gain_grads = lax.psum((owned[0], owned[1], owned[2]), "tensor")
    return (
        block_out,
        grad_input,
        grad_cond,
        gain_grads[0],
        gain_grads[1],
        gain_grads[2],
        owned[3],
        owned[4],
        owned[5],
        owned[6],
        owned[7],
        owned[8],
        owned[9],
    )


def general_solution(mesh):
    return jax.shard_map(
        general_body,
        mesh=mesh,
        in_specs=(
            P(("dp", "tensor"), None),
            P("dp", None, None),
            P("dp"),
            P("dp"),
            P("dp"),
            P("dp"),
            P("dp", None, "tensor"),
            P("tensor", "dp"),
            P("dp", "tensor"),
            P("dp", None, "tensor"),
            P("tensor", "dp"),
            P("dp", None, "tensor"),
            P("tensor", "dp"),
            P(("dp", "tensor"), None),
        ),
        out_specs=(
            P(("dp", "tensor"), None),
            P(("dp", "tensor"), None),
            P("dp", None, "tensor"),
            P("dp"),
            P("dp"),
            P("dp"),
            P("dp", None, "tensor"),
            P("tensor", "dp"),
            P("dp", "tensor"),
            P("dp", None, "tensor"),
            P("tensor", "dp"),
            P("dp", None, "tensor"),
            P("tensor", "dp"),
        ),
        check_vma=False,
    )


def dot(left, right, dims=NN):
    return lax.dot_general(left, right, dims, preferred_element_type=F32)


def rot(values, tables):
    cosine, sine_up, sine_down = tables
    return (
        values * cosine
        + pltpu.roll(values, 16, 1) * sine_up
        + pltpu.roll(values, 112, 1) * sine_down
    )


def rot_back(grads, tables):
    cosine, sine_up, sine_down = tables
    return (
        grads * cosine
        - pltpu.roll(grads, 16, 1) * sine_up
        - pltpu.roll(grads, 112, 1) * sine_down
    )


def rot_tables(positions):
    quarter = HD // 4
    inverse = 10000.0 ** (-jnp.arange(quarter).astype(F32) / quarter)
    angle_grid = positions.astype(F32)[:, None] * inverse[None, :]
    cosine, sine = jnp.cos(angle_grid), jnp.sin(angle_grid)
    rest = jnp.zeros((positions.shape[0], 2 * quarter), F32)
    none = jnp.zeros_like(sine)
    return (
        jnp.concatenate([cosine, cosine, rest + 1.0] * 2, axis=1),
        jnp.concatenate([none, sine, rest] * 2, axis=1),
        jnp.concatenate([-sine, none, rest] * 2, axis=1),
    )


def to_rows(picks, columns):
    first = columns.astype(BF)
    rest = columns - first.astype(F32)
    second = rest.astype(BF)
    third = (rest - second.astype(F32)).astype(BF)
    return dot(picks, first, NT) + dot(picks, second, NT) + dot(picks, third, NT)


def iota(shape, axis):
    return lax.broadcasted_iota(jnp.int32, shape, axis)


def self_forward_kernel(
    step, rows_ref, own_ref, other_ref, c_ref, su_ref, sd_ref,
    q_ref, k_ref, v_ref, mine_ref, theirs_ref, lse_ref,
):
    count, width = rows_ref.shape
    half = width // 2
    qkv = dot(rows_ref[:, :half], own_ref[0]) + dot(rows_ref[:, half:], other_ref[0])
    tables = (c_ref[...], su_ref[...], sd_ref[...])
    query = (rot(qkv[:, :128], tables) * 0.125).astype(BF)
    key = rot(qkv[:, 128:256], tables).astype(BF)
    value = qkv[:, 256:].astype(BF)
    q_ref[...] = query
    k_ref[...] = key
    v_ref[...] = value
    lane = iota((step, 128), 1)
    picks = jnp.where(iota((8, 128), 0) == iota((8, 128), 1), 1.0, 0.0).astype(BF)
    for at in range(0, count, step):
        part = query[at : at + step]
        mixed, logs = [], []
        for head in range(2):
            here = (lane // HD) == head
            scores = dot(jnp.where(here, part, jnp.zeros_like(part)), key, NT)
            top = jnp.max(scores, axis=1, keepdims=True)
            weights = jnp.exp(scores - top)
            total = jnp.sum(weights, axis=1, keepdims=True)
            mixed.append(dot(weights.astype(BF), value) * (1.0 / total))
            logs.append(top + jnp.log(total))
        out = jnp.where(lane < HD, mixed[0], mixed[1]).astype(BF)
        both = jnp.where(lane == 0, logs[0], jnp.where(lane == 1, logs[1], 0.0))
        lse_ref[0, :, at : at + step] = to_rows(picks, both)
        if at < count // 2:
            mine_ref[at : at + step, :] = out
        else:
            theirs_ref[at - count // 2 : at - count // 2 + step, :] = out


def whole(shape):
    return pl.BlockSpec(shape, lambda p: (0,) * len(shape))


def columns_of(rows):
    return pl.BlockSpec((rows, 128), lambda p: (0, p))


def self_forward(rows, own, other, tables):
    count, width = rows.shape
    per = own.shape[2] // 384
    pairs = own.shape[0] * per
    wide = pairs * 128
    weight = pl.BlockSpec((1, own.shape[1], 384), lambda p: (p // per, 0, p % per))
    return pl.pallas_call(
        functools.partial(self_forward_kernel, min(512, count // 2)),
        grid=(pairs,),
        in_specs=[whole((count, width)), weight, weight] + [whole((count, 128))] * 3,
        out_specs=[columns_of(count)] * 3
        + [columns_of(count // 2)] * 2
        + [pl.BlockSpec((1, 8, count), lambda p: (p, 0, 0))],
        out_shape=[jax.ShapeDtypeStruct((count, wide), BF)] * 3
        + [jax.ShapeDtypeStruct((count // 2, wide), BF)] * 2
        + [jax.ShapeDtypeStruct((pairs, 8, count), F32)],
        compiler_params=pltpu.CompilerParams(vmem_limit_bytes=VMEM_BYTES),
        cost_estimate=pl.CostEstimate(
            flops=6 * count * width * wide + 8 * count * count * wide,
            bytes_accessed=6 * width * wide + 12 * count * wide,
            transcendentals=2 * count * count * pairs,
        ),
        name="self_forward",
    )(rows, own, other, *tables)


def self_backward_kernel(
    step, q_ref, k_ref, v_ref, mine_ref, theirs_ref, dmine_ref, dtheirs_ref, lse_ref,
    c_ref, su_ref, sd_ref, out_ref,
):
    count = q_ref.shape[0]
    query = q_ref[...]
    grads = jnp.concatenate([dmine_ref[...], dtheirs_ref[...]], axis=0)
    mixed = jnp.concatenate([mine_ref[...], theirs_ref[...]], axis=0)
    picks = jnp.where((iota((8, 128), 1) // HD) == iota((8, 128), 0), 1.0, 0.0).astype(BF)
    delta = to_rows(picks, grads.astype(F32) * mixed.astype(F32))
    lane = iota((step, 128), 1)
    row = iota((128, step), 0)
    keys_across = jnp.transpose(k_ref[...].astype(F32)).astype(BF)
    query_across = jnp.zeros((128, count), F32)
    tables = (c_ref[...], su_ref[...], sd_ref[...])
    for at in range(0, count, step):
        here = slice(at, at + step)
        key, value = k_ref[here, :], v_ref[here, :]
        across = keys_across[:, here]
        dkeys, dvalues = [], []
        for head in range(2):
            inside = (lane // HD) == head
            scores = dot(jnp.where(inside, key, jnp.zeros_like(key)), query, NT)
            probs = jnp.exp(scores - lse_ref[0, head : head + 1, :])
            dprobs = dot(jnp.where(inside, value, jnp.zeros_like(value)), grads, NT)
            dscores = (probs * (dprobs - delta[head : head + 1, :])).astype(BF)
            dvalues.append(dot(probs.astype(BF), grads))
            dkeys.append(dot(dscores, query))
            picked = jnp.where((row // HD) == head, across, jnp.zeros_like(across))
            query_across = query_across + dot(picked, dscores)
        dkey = jnp.where(lane < HD, dkeys[0], dkeys[1])
        dvalue = jnp.where(lane < HD, dvalues[0], dvalues[1])
        out_ref[here, 128:256] = rot_back(dkey, [t[here] for t in tables]).astype(BF)
        out_ref[here, 256:384] = dvalue.astype(BF)
    dquery = jnp.transpose(query_across)
    out_ref[:, 0:128] = (rot_back(dquery, tables) * 0.125).astype(BF)


def self_backward(query, key, value, mine, theirs, dmine, dtheirs, lse, tables):
    count, wide = query.shape
    pairs = wide // 128
    return pl.pallas_call(
        functools.partial(self_backward_kernel, min(512, count // 2)),
        grid=(pairs,),
        in_specs=[columns_of(count)] * 3
        + [columns_of(count // 2)] * 4
        + [pl.BlockSpec((1, 8, count), lambda p: (p, 0, 0))]
        + [whole((count, 128))] * 3,
        out_specs=pl.BlockSpec((count, 384), lambda p: (0, p)),
        out_shape=jax.ShapeDtypeStruct((count, 3 * wide), BF),
        compiler_params=pltpu.CompilerParams(vmem_limit_bytes=VMEM_BYTES),
        cost_estimate=pl.CostEstimate(
            flops=20 * count * count * wide,
            bytes_accessed=20 * count * wide,
            transcendentals=2 * count * count * pairs,
        ),
        name="self_backward",
    )(query, key, value, mine, theirs, dmine, dtheirs, lse, *tables)


def ffn_kernel(
    has_start, tile, rows_ref, across_ref, dy_ref, dyx_ref, own_ref, other_ref, *rest,
):
    if has_start:
        y_in, d_in, y_out, d_out, gown_ref, gother_ref = rest
    else:
        y_out, d_out, gown_ref, gother_ref = rest
    half = rows_ref.shape[1] // 2
    both = 2 * tile

    @pl.when(pl.program_id(0) == 0)
    def _():
        if has_start:
            y_out[...] = y_in[...]
            d_out[...] = d_in[...]
        else:
            y_out[...] = jnp.zeros_like(y_out)
            d_out[...] = jnp.zeros_like(d_out)

    own, other = own_ref[0], other_ref[0]
    gate_up = dot(rows_ref[:, :half], own[:, :both]) + dot(rows_ref[:, half:], other[:, :both])
    dhidden = dot(dy_ref[:, :half], own[:, both:]) + dot(dy_ref[:, half:], other[:, both:])
    gate, up = gate_up[:, :tile], gate_up[:, tile:]
    sigma = 1.0 / (1.0 + jnp.exp(-gate))
    silu = gate * sigma
    hidden = (silu * up).astype(BF)
    dup = (dhidden * silu).astype(BF)
    dgate = (dhidden * up * (sigma * (1.0 + gate * (1.0 - sigma)))).astype(BF)
    dgate_up = jnp.concatenate([dgate, dup], axis=1)
    y_out[:, :half] += dot(hidden, own[:, both:], NT)
    y_out[:, half:] += dot(hidden, other[:, both:], NT)
    d_out[:, :half] += dot(dgate_up, own[:, :both], NT)
    d_out[:, half:] += dot(dgate_up, other[:, :both], NT)
    gown_ref[0, :, :both] = dot(across_ref[:half, :], dgate_up).astype(BF)
    gother_ref[0, :, :both] = dot(across_ref[half:, :], dgate_up).astype(BF)
    gown_ref[0, :, both:] = dot(dyx_ref[:half, :], hidden).astype(BF)
    gother_ref[0, :, both:] = dot(dyx_ref[half:, :], hidden).astype(BF)


def ffn(rows, across, dy, dyx, own, other, tile, start=None):
    count, width = rows.shape
    groups, half, wide = own.shape
    tiles = wide // (3 * tile)
    block = pl.BlockSpec((1, half, 3 * tile), lambda p: (p // tiles, 0, p % tiles))
    full = whole((count, width))
    flipped = whole((width, count))
    once = pl.BlockSpec((count, width), lambda p: (0, 0), pipeline_mode=pl.Buffered(1))
    fixed = pl.BlockSpec((width, count), lambda p: (0, 0), pipeline_mode=pl.Buffered(1))
    extra = [] if start is None else list(start)
    return pl.pallas_call(
        functools.partial(ffn_kernel, start is not None, tile),
        grid=(groups * tiles,),
        in_specs=[once, fixed, once, fixed, block, block] + [once] * len(extra),
        out_specs=[once, once, block, block],
        out_shape=[jax.ShapeDtypeStruct((count, width), F32)] * 2
        + [jax.ShapeDtypeStruct(own.shape, BF)] * 2,
        input_output_aliases={} if start is None else {6: 0, 7: 1},
        compiler_params=pltpu.CompilerParams(vmem_limit_bytes=VMEM_BYTES),
        cost_estimate=pl.CostEstimate(
            flops=6 * count * width * groups * wide,
            bytes_accessed=8 * groups * width * wide // 2 + 24 * count * width,
            transcendentals=count * groups * wide // 3,
        ),
        name="feed_forward",
    )(rows, across, dy, dyx, own, other, *extra)


def cross_scores(query, key, allowed):
    scores = jnp.einsum("qhd,khd->hqk", query, key, preferred_element_type=F32)
    return jnp.where(allowed[None, None, :], scores, MASKED_SCORE)


def normalize(values):
    centre = values - jnp.mean(values, axis=-1, keepdims=True)
    scale = lax.rsqrt(jnp.mean(centre * centre, axis=-1, keepdims=True) + EPSILON)
    return centre * scale, scale


def normalize_back(grads, gain, normal, scale):
    inner = grads * gain
    return (
        inner
        - jnp.mean(inner, axis=-1, keepdims=True)
        - normal * jnp.mean(inner * normal, axis=-1, keepdims=True)
    ) * scale


def swap(array, axis, bit=1):
    return lax.ppermute(array, axis, [(i, i ^ bit) for i in range(lax.axis_size(axis))])


def pick(flag, on, off):
    return jnp.where(flag, on, off)


def pair_body(
    block_in,
    cond_tokens,
    cond_count,
    norm1_gain,
    norm2_gain,
    norm3_gain,
    qkv_weight,
    attn_out_weight,
    cross_q_weight,
    cross_kv_weight,
    cross_out_weight,
    gate_up_weight,
    down_weight,
    out_cotangent,
    chunks,
    tile,
):
    rows, width = block_in.shape
    shard = qkv_weight.shape[0]
    head_cols = attn_out_weight.shape[0]
    hidden_cols = down_weight.shape[0]
    cond_slots, cond_width = cond_tokens.shape[1:]
    cond_shard = cross_kv_weight.shape[0]
    dp = lax.axis_index("dp")
    seq = lax.axis_index("seq")
    side = lax.axis_index("half")
    dp_size = lax.axis_size("dp")
    z_size = dp_size // 2
    core = (dp % 2) == 1
    z = dp // 2
    half = width // 2
    pairs_here = head_cols // 128
    per_chunk = hidden_cols // chunks
    z_bits = []
    bit = z_size // 2
    while bit:
        z_bits.append(bit)
        bit //= 2

    def over_z(array):
        array = array[None]
        for bit in z_bits:
            got = swap(array, "dp", 2 * bit)
            upper = (z & bit) != 0
            both = jnp.stack([pick(upper, got, array), pick(upper, array, got)], axis=1)
            array = both.reshape((-1,) + array.shape[1:])
        return array

    def gather(pack, wide):
        array = over_z(pack).reshape(half, pack.shape[1])
        array = jnp.stack([array, swap(array, "seq")])
        if wide:
            array = jnp.stack([array, swap(array, "half")])
        return array, swap(array, "dp", 1)

    def to_core_order(array, piece):
        parts = array.reshape(array.shape[0], z_size, 2, piece)
        even = parts[:, :, 0].reshape(array.shape[0], -1)
        odd = parts[:, :, 1].reshape(array.shape[0], -1)
        return jnp.concatenate([pick(core, odd, even), pick(core, even, odd)], axis=1)

    def from_core_order(array, piece):
        count = array.shape[0]
        middle = array.shape[1] // 2
        own, other = array[:, :middle], array[:, middle:]
        even = pick(core, other, own).reshape(count, z_size, piece)
        odd = pick(core, own, other).reshape(count, z_size, piece)
        return jnp.stack([even, odd], axis=2).reshape(count, -1)

    def scatter_z(array):
        array = array.reshape((z_size, -1) + array.shape[1:])
        for bit in z_bits[::-1]:
            array = array.reshape((-1, 2) + array.shape[1:])
            mine = (z & bit) // bit
            keep = lax.dynamic_index_in_dim(array, mine, 1, keepdims=False)
            send = lax.dynamic_index_in_dim(array, 1 - mine, 1, keepdims=False)
            array = keep.astype(F32) + swap(send, "dp", 2 * bit).astype(F32)
            if bit != z_bits[0]:
                array = array.astype(BF)
        return array.astype(F32)[0]

    def fold(keep, send, axis, bit=1):
        return (keep.astype(F32) + swap(send, axis, bit).astype(F32)).astype(BF)

    gu_parts = gate_up_weight.reshape(shard, 2, chunks, per_chunk // tile, 1, tile)
    down_across = down_weight.T.reshape(shard, 1, chunks, per_chunk // tile, 1, tile)
    ffn_pack = jnp.concatenate([gu_parts, down_across], axis=1)
    ffn_pack = ffn_pack.transpose(2, 0, 3, 1, 4, 5).reshape(chunks, shard, 3 * per_chunk)
    qkv_pack = (
        qkv_weight.reshape(shard, 3, pairs_here, 128)
        .transpose(0, 2, 1, 3)
        .reshape(shard, 3 * head_cols)
    )
    square_pack = jnp.concatenate(
        [
            attn_out_weight.T,
            cross_q_weight,
            cross_kv_weight.transpose(1, 0, 2).reshape(shard, head_cols),
            cross_out_weight.T,
        ],
        axis=1,
    )
    gains = jnp.stack([norm1_gain, norm2_gain, norm3_gain])

    qkv_own, qkv_other = gather(qkv_pack, False)
    gains = over_z(gains)
    gains = jnp.concatenate([gains, swap(gains, "dp", 1)])
    gains = gains.transpose(1, 0, 2).reshape(3, width).astype(F32)

    mine_in = to_core_order(block_in, shard)
    all_in = jnp.concatenate([mine_in, swap(mine_in, "half")], axis=0)
    top_grads = to_core_order(out_cotangent, shard)
    all_top = jnp.concatenate([top_grads, swap(top_grads, "half")], axis=0)
    square_own, square_other = gather(square_pack, True)
    ffn_weights = [gather(ffn_pack[i], False) for i in range(chunks)]

    def square(section):
        cut = slice(section * head_cols, (section + 1) * head_cols)
        both = jnp.stack([square_own[..., cut], square_other[..., cut]])
        return both.transpose(0, 3, 1, 2, 4).reshape(width, 4 * head_cols)

    positions = jnp.concatenate([side * rows + jnp.arange(rows), (1 - side) * rows + jnp.arange(rows)])
    tables = rot_tables(positions)
    first_normal, first_scale = normalize(all_in.astype(F32))
    first_all = (first_normal * gains[0]).astype(BF)
    query, key, value, mine, theirs, lse = self_forward(first_all, qkv_own, qkv_other, tables)
    mixed = jnp.concatenate([mine, swap(theirs, "half")], axis=1)
    w_out = square(0)
    after_self = mine_in.astype(F32) + dot(mixed, w_out, NT)
    second_normal, second_scale = normalize(after_self)
    second = (second_normal * gains[1]).astype(BF)
    heads = 4 * head_cols // HD
    w_cq = square(1)
    cross_query = (dot(second, w_cq) * 0.125).astype(BF).reshape(rows, heads, HD)
    my_cond = to_core_order(cond_tokens[seq], cond_shard)
    w_ckv = square(2).reshape(width // (2 * cond_shard), 2, cond_shard, 4 * head_cols)
    w_ckv = w_ckv.transpose(0, 2, 1, 3).reshape(cond_width, 2 * 4 * head_cols)
    cross_kv = dot(my_cond, w_ckv).astype(BF).reshape(cond_slots, 2, heads, HD)
    allowed = jnp.arange(cond_slots) < cond_count[seq]
    cross_mixed, cross_lse = attend_forward(cross_query, cross_kv[:, 0], cross_kv[:, 1], allowed)
    cross_flat = cross_mixed.reshape(rows, 4 * head_cols)
    w_co = square(3)
    after_cross = after_self + dot(cross_flat, w_co, NT)
    third_normal, third_scale = normalize(after_cross)
    third = (third_normal * gains[2]).astype(BF)
    third_all = jnp.concatenate([third, swap(third, "half")], axis=0)
    third_across = third_all.T
    top_across = all_top.T
    sums = None
    ffn_grads = []
    for own, other in ffn_weights:
        y_sum, d_sum, gown, gother = ffn(
            third_all, third_across, all_top, top_across, own, other, tile, sums
        )
        sums = (y_sum, d_sum)
        ffn_grads.append((gown, gother))
    grad_third = d_sum[:rows] + swap(d_sum[rows:].astype(BF), "half").astype(F32)
    y_mine = y_sum[:rows] + swap(y_sum[rows:].astype(BF), "half").astype(F32)
    block_out = from_core_order((after_cross + y_mine).astype(BF), shard)

    def scatter_ffn(gown, gother):
        kept = fold(gown, gother, "dp")
        kept = fold(kept[0], kept[1], "seq")
        return scatter_z(kept)

    ffn_owned = jnp.stack([scatter_ffn(*pair) for pair in ffn_grads])
    ffn_owned = ffn_owned.reshape(chunks, shard, per_chunk // tile, 3, tile)
    ffn_owned = ffn_owned.transpose(1, 3, 0, 2, 4).reshape(shard, 3, hidden_cols)
    grad_gate_up = ffn_owned[:, :2]
    grad_down = ffn_owned[:, 2].T

    gain_third = jnp.sum(grad_third * third_normal, axis=0)
    grad_cross_rows = top_grads.astype(F32) + normalize_back(
        grad_third, gains[2], third_normal, third_scale
    )
    second_grads = grad_cross_rows.astype(BF)
    grad_cross_mixed = dot(second_grads, w_co).astype(BF)
    grad_co = rows_by_rows(second_grads, cross_flat).astype(BF)
    cross_gq, cross_gk, cross_gv = attend_backward(
        cross_query,
        cross_kv[:, 0],
        cross_kv[:, 1],
        allowed,
        cross_lse,
        grad_cross_mixed.reshape(rows, heads, HD),
    )
    grad_cross_query = (cross_gq * 0.125).astype(BF).reshape(rows, 4 * head_cols)
    grad_cross_kv = (
        jnp.stack([cross_gk, cross_gv], axis=1).astype(BF).reshape(cond_slots, 8 * head_cols)
    )
    grad_cq = rows_by_rows(second, grad_cross_query).astype(BF)
    grad_ckv = rows_by_rows(my_cond, grad_cross_kv).astype(BF)
    grad_ckv = grad_ckv.reshape(width // (2 * cond_shard), cond_shard, 2, 4 * head_cols)
    grad_ckv = grad_ckv.transpose(0, 2, 1, 3).reshape(width, 4 * head_cols)

    def scatter_square(stack):
        wide = stack.shape[2]
        kept = fold(stack[:, :half], stack[:, half:], "dp")
        kept = fold(kept[..., : wide // 2], kept[..., wide // 2 :], "half")
        kept = fold(kept[..., : wide // 4], kept[..., wide // 4 :], "seq")
        return jnp.stack([scatter_z(kept[i]) for i in range(stack.shape[0])])

    owned = scatter_square(jnp.stack([grad_cq, grad_ckv, grad_co]))
    grad_cross_q = owned[0]
    grad_cross_kv_weight = owned[1].reshape(2, cond_shard, head_cols).transpose(1, 0, 2)
    grad_cross_out = owned[2].T

    cond_mine = from_core_order(times_transposed(grad_cross_kv, w_ckv), cond_shard)
    cond_mine = cond_mine.reshape(cond_slots, 2, 2, cond_width // 4)
    cond_keep = lax.dynamic_index_in_dim(cond_mine, side, 2, keepdims=False)
    cond_send = lax.dynamic_index_in_dim(cond_mine, 1 - side, 2, keepdims=False)
    cond_mine = cond_keep + swap(cond_send, "half")
    cond_keep = lax.dynamic_index_in_dim(cond_mine, seq, 1, keepdims=False)
    cond_send = lax.dynamic_index_in_dim(cond_mine, 1 - seq, 1, keepdims=False)
    cond_got = swap(cond_send, "seq")
    odd = seq == 1
    grad_cond = jnp.stack([pick(odd, cond_got, cond_keep), pick(odd, cond_keep, cond_got)])

    grad_second = times_transposed(grad_cross_query, w_cq)
    gain_second = jnp.sum(grad_second * second_normal, axis=0)
    grad_self_rows = grad_cross_rows + normalize_back(
        grad_second, gains[1], second_normal, second_scale
    )
    first_grads = grad_self_rows.astype(BF)
    grad_mixed = dot(first_grads, w_out).astype(BF)
    grad_out = rows_by_rows(first_grads, mixed).astype(BF)
    dmine = grad_mixed[:, : 2 * head_cols]
    dtheirs = swap(grad_mixed[:, 2 * head_cols :], "half")
    grad_qkv_rows = self_backward(
        query, key, value, mine, theirs, dmine, dtheirs, lse, tables
    )
    grad_attn_out = scatter_square(grad_out[None])[0].T
    cut = 3 * head_cols
    parts = [grad_qkv_rows[:, :cut], grad_qkv_rows[:, cut:]]

    def first_back(weights):
        return times_transposed(parts[0], weights[0]) + times_transposed(parts[1], weights[1])

    grad_first = jnp.concatenate([first_back(qkv_own), first_back(qkv_other)], axis=1)
    gain_first = jnp.sum(grad_first * first_normal, axis=0)
    grad_first = grad_first[:rows] + swap(grad_first[rows:].astype(BF), "half").astype(F32)
    g_other = rows_by_rows(first_all[:, half:], grad_qkv_rows).astype(BF)
    g_own = rows_by_rows(first_all[:, :half], grad_qkv_rows).astype(BF)
    kept = fold(g_own, g_other, "dp")
    kept = fold(kept[:, :cut], kept[:, cut:], "seq")
    grad_qkv = (
        scatter_z(kept).reshape(shard, pairs_here, 3, 128).transpose(0, 2, 1, 3)
    ).reshape(shard, 3, head_cols)
    grad_input = grad_self_rows + normalize_back(
        grad_first, gains[0], first_normal[:rows], first_scale[:rows]
    )
    grad_input = from_core_order(grad_input, shard)

    gain_grads = jnp.stack([gain_first, gain_second, gain_third])
    gain_grads = gain_grads[:, :half] + swap(gain_grads[:, half:], "dp", 1)
    gain_grads = gain_grads + swap(gain_grads, "seq")
    gain_grads = gain_grads + swap(gain_grads, "half")
    gain_grads = scatter_z(gain_grads.reshape(3, z_size, shard).transpose(1, 0, 2).reshape(-1, shard))
    return (
        block_out,
        grad_input,
        grad_cond,
        gain_grads[0],
        gain_grads[1],
        gain_grads[2],
        grad_qkv,
        grad_attn_out,
        grad_cross_q,
        grad_cross_kv_weight,
        grad_cross_out,
        grad_gate_up,
        grad_down,
    )


def power_of_two(number):
    return number > 0 and number & (number - 1) == 0


def pair_solution(mesh, sequences):
    dp, tensor = mesh.devices.shape
    finer = Mesh(mesh.devices.reshape(dp, sequences, tensor // sequences), ("dp", "seq", "half"))
    every = ("dp", "seq", "half")
    both = ("seq", "half")
    return jax.shard_map(
        functools.partial(pair_body, chunks=CHUNKS, tile=TILE),
        mesh=finer,
        in_specs=(
            P(every, None),
            P("dp", None, None),
            P("dp"),
            P("dp"),
            P("dp"),
            P("dp"),
            P("dp", None, both),
            P(both, "dp"),
            P("dp", both),
            P("dp", None, both),
            P(both, "dp"),
            P("dp", None, both),
            P(both, "dp"),
            P(every, None),
        ),
        out_specs=(
            P(every, None),
            P(every, None),
            P("dp", None, both),
            P("dp"),
            P("dp"),
            P("dp"),
            P("dp", None, both),
            P(both, "dp"),
            P("dp", both),
            P("dp", None, both),
            P(both, "dp"),
            P("dp", None, both),
            P(both, "dp"),
        ),
        check_vma=False,
    )


CHUNKS = 2
TILE = 256


def solution(mesh):
    dp, tensor = mesh.devices.shape

    def run(*args):
        cond_tokens, qkv, down = args[1], args[6], args[12]
        sequences = cond_tokens.shape[0] // dp
        fits = (
            sequences == 2
            and tensor == 4
            and power_of_two(dp)
            and dp >= 4
            and qkv.shape[2] % (tensor * 128) == 0
            and down.shape[0] % (tensor * CHUNKS * TILE) == 0
            and qkv.shape[0] == 2 * cond_tokens.shape[2]
        )
        if fits:
            return pair_solution(mesh, sequences)(*args)
        return general_solution(mesh)(*args)

    return run
```

```python
import functools
import math

import jax
import jax.numpy as jnp
from jax import lax
from jax.experimental import pallas as pl
from jax.experimental.pallas import tpu as pltpu
from jax.sharding import Mesh
from jax.sharding import PartitionSpec as P

HD = 64


EPSILON = 1e-05
MASKED_SCORE = -1e30
BF = jnp.bfloat16
F32 = jnp.float32
NN = (((1,), (0,)), ((), ()))
NT = (((1,), (1,)), ((), ()))
VMEM_BYTES = 60 << 20


def layer_norm(values, gain):
    centre = values - jnp.mean(values, axis=-1, keepdims=True)
    spread = jnp.mean(centre * centre, axis=-1, keepdims=True)
    return centre * lax.rsqrt(spread + EPSILON) * gain


def rotate(values, cosine, sine):
    quarter = cosine.shape[-1]
    first_part = values[..., :quarter]
    second_part = values[..., quarter : 2 * quarter]
    rest_part = values[..., 2 * quarter :]
    return jnp.concatenate(
        [
            first_part * cosine - second_part * sine,
            first_part * sine + second_part * cosine,
            rest_part,
        ],
        axis=-1,
    )


def rotate_back(grads, cosine, sine):
    quarter = cosine.shape[-1]
    first_part = grads[..., :quarter]
    second_part = grads[..., quarter : 2 * quarter]
    rest_part = grads[..., 2 * quarter :]
    return jnp.concatenate(
        [
            first_part * cosine + second_part * sine,
            second_part * cosine - first_part * sine,
            rest_part,
        ],
        axis=-1,
    )


def gated(gate_vals, up_vals):
    return jax.nn.silu(gate_vals) * up_vals


def rows_by_rows(left, right):
    return lax.dot_general(
        left, right, (((0,), (0,)), ((), ())), preferred_element_type=jnp.float32
    )


def times_transposed(left, right):
    return lax.dot_general(
        left, right, (((1,), (1,)), ((), ())), preferred_element_type=jnp.float32
    )


def attend_forward(query_rows, key_rows, value_rows, allowed):
    scores = jnp.einsum("qhd,khd->hqk", query_rows, key_rows, preferred_element_type=jnp.float32)
    scores = jnp.where(allowed[None, None, :], scores, MASKED_SCORE)
    top_score = jnp.max(scores, axis=-1, keepdims=True)
    weights = jnp.exp(scores - top_score)
    totals = jnp.sum(weights, axis=-1, keepdims=True)
    probs = weights / totals
    mixed = jnp.einsum(
        "hqk,khd->qhd", probs.astype(jnp.bfloat16), value_rows, preferred_element_type=jnp.float32
    )
    return (mixed.astype(jnp.bfloat16), top_score + jnp.log(totals))


def attend_backward(query_rows, key_rows, value_rows, allowed, log_total, grad_mixed):
    scores = jnp.einsum("qhd,khd->hqk", query_rows, key_rows, preferred_element_type=jnp.float32)
    scores = jnp.where(allowed[None, None, :], scores, MASKED_SCORE)
    probs = jnp.exp(scores - log_total)
    grad_probs = jnp.einsum(
        "qhd,khd->hqk", grad_mixed, value_rows, preferred_element_type=jnp.float32
    )
    grad_values = jnp.einsum(
        "hqk,qhd->khd", probs.astype(jnp.bfloat16), grad_mixed, preferred_element_type=jnp.float32
    )
    grad_scores = probs * (grad_probs - jnp.sum(probs * grad_probs, axis=-1, keepdims=True))
    grad_scores = grad_scores.astype(jnp.bfloat16)
    grad_query = jnp.einsum(
        "hqk,khd->qhd", grad_scores, key_rows, preferred_element_type=jnp.float32
    )
    grad_keys = jnp.einsum(
        "hqk,qhd->khd", grad_scores, query_rows, preferred_element_type=jnp.float32
    )
    return (grad_query, grad_keys, grad_values)


def general_body(
    block_in,
    cond_tokens,
    cond_count,
    norm1_gain,
    norm2_gain,
    norm3_gain,
    qkv_weight,
    attn_out_weight,
    cross_q_weight,
    cross_kv_weight,
    cross_out_weight,
    gate_up_weight,
    down_weight,
    out_cotangent,
):
    local_rows = block_in.shape[0]
    model_width = block_in.shape[1]
    group_rows = local_rows * lax.axis_size("tensor")
    seq_here = cond_tokens.shape[0]
    seq_length = group_rows // seq_here
    cond_slots = cond_tokens.shape[1]
    cond_width = cond_tokens.shape[2]
    head_cols = attn_out_weight.shape[0]
    heads_here = head_cols // HD
    hidden_here = down_weight.shape[0]
    gain_one, gain_two, gain_three, w_qkv, w_out, w_cq, w_ckv, w_co, w_gu, w_down = (
        lax.all_gather(norm1_gain, "dp", axis=0, tiled=True),
        lax.all_gather(norm2_gain, "dp", axis=0, tiled=True),
        lax.all_gather(norm3_gain, "dp", axis=0, tiled=True),
        lax.all_gather(qkv_weight, "dp", axis=0, tiled=True),
        lax.all_gather(attn_out_weight, "dp", axis=1, tiled=True),
        lax.all_gather(cross_q_weight, "dp", axis=0, tiled=True),
        lax.all_gather(cross_kv_weight, "dp", axis=0, tiled=True),
        lax.all_gather(cross_out_weight, "dp", axis=1, tiled=True),
        lax.all_gather(gate_up_weight, "dp", axis=0, tiled=True),
        lax.all_gather(down_weight, "dp", axis=1, tiled=True),
    )
    quarter = HD // 4
    positions = (jnp.arange(group_rows) % seq_length).astype(jnp.float32)
    inverse = 10000.0 ** (-jnp.arange(quarter).astype(jnp.float32) / quarter)
    angle_grid = positions[:, None] * inverse[None, :]
    cosine = jnp.cos(angle_grid)[:, None, :]
    sine = jnp.sin(angle_grid)[:, None, :]
    every_key = jnp.ones((seq_length,), dtype=jnp.bool_)
    valid_slots = jnp.arange(cond_slots)[None, :] < cond_count[:, None]

    def by_sequence(array):
        return array.reshape((seq_here, seq_length) + array.shape[1:])

    def spread_rows(local_part):
        return lax.all_gather(local_part, "tensor", axis=0, tiled=True)

    def project_out(mixed_all, weight):
        return lax.psum_scatter(
            jnp.dot(mixed_all, weight, preferred_element_type=jnp.float32),
            "tensor",
            scatter_dimension=0,
            tiled=True,
        )

    def spread_grads(local_part):
        return lax.all_gather(local_part, "tensor", axis=0, tiled=True)

    def gather_back(grad_all, weight):
        return lax.psum_scatter(
            times_transposed(grad_all, weight), "tensor", scatter_dimension=0, tiled=True
        )

    def self_forward(seq_parts):
        return attend_forward(seq_parts[0], seq_parts[1], seq_parts[2], every_key)

    def cross_forward(seq_parts):
        return attend_forward(seq_parts[0], seq_parts[1][:, 0], seq_parts[1][:, 1], seq_parts[2])

    def self_backward(seq_parts):
        return attend_backward(
            seq_parts[0], seq_parts[1], seq_parts[2], every_key, seq_parts[3], seq_parts[4]
        )

    def cross_backward(seq_parts):
        return attend_backward(
            seq_parts[0],
            seq_parts[1][:, 0],
            seq_parts[1][:, 1],
            seq_parts[2],
            seq_parts[3],
            seq_parts[4],
        )

    gain_first = gain_one.astype(jnp.float32)
    gain_second = gain_two.astype(jnp.float32)
    gain_third = gain_three.astype(jnp.float32)
    input_rows = block_in.astype(jnp.float32)
    first_all = spread_rows(layer_norm(input_rows, gain_first).astype(jnp.bfloat16))
    qkv_all = jnp.dot(
        first_all, w_qkv.reshape(model_width, 3 * head_cols), preferred_element_type=jnp.float32
    )
    qkv_all = qkv_all.reshape(group_rows, 3, heads_here, HD)
    query_rot = (rotate(qkv_all[:, 0], cosine, sine) * 0.125).astype(jnp.bfloat16)
    key_rot = rotate(qkv_all[:, 1], cosine, sine).astype(jnp.bfloat16)
    value_rows = qkv_all[:, 2].astype(jnp.bfloat16)
    self_mixed, self_lse = lax.map(
        self_forward, (by_sequence(query_rot), by_sequence(key_rot), by_sequence(value_rows))
    )
    self_flat = self_mixed.reshape(group_rows, head_cols)
    after_self = input_rows + project_out(self_flat, w_out)
    second_all = spread_rows(layer_norm(after_self, gain_second).astype(jnp.bfloat16))
    cross_query = (jnp.dot(second_all, w_cq, preferred_element_type=jnp.float32) * 0.125).astype(
        jnp.bfloat16
    )
    cross_query = cross_query.reshape(group_rows, heads_here, HD)
    cond_flat = cond_tokens.reshape(seq_here * cond_slots, cond_width)
    cross_kv = jnp.dot(
        cond_flat, w_ckv.reshape(cond_width, 2 * head_cols), preferred_element_type=jnp.float32
    )
    cross_kv = cross_kv.astype(jnp.bfloat16).reshape(seq_here, cond_slots, 2, heads_here, HD)
    cross_mixed, cross_lse = lax.map(
        cross_forward, (by_sequence(cross_query), cross_kv, valid_slots)
    )
    cross_flat = cross_mixed.reshape(group_rows, head_cols)
    after_cross = after_self + project_out(cross_flat, w_co)
    third_all = spread_rows(layer_norm(after_cross, gain_third).astype(jnp.bfloat16))
    gate_up = jnp.dot(
        third_all, w_gu.reshape(model_width, 2 * hidden_here), preferred_element_type=jnp.float32
    )
    gate_up = gate_up.reshape(group_rows, 2, hidden_here)
    gate_vals = gate_up[:, 0]
    up_vals = gate_up[:, 1]
    hidden = gated(gate_vals, up_vals).astype(jnp.bfloat16)
    block_out = (after_cross + project_out(hidden, w_down)).astype(jnp.bfloat16)
    gain_one, gain_two, gain_three, w_qkv, w_out, w_cq, w_ckv, w_co, w_gu, w_down = (
        lax.all_gather(norm1_gain, "dp", axis=0, tiled=True),
        lax.all_gather(norm2_gain, "dp", axis=0, tiled=True),
        lax.all_gather(norm3_gain, "dp", axis=0, tiled=True),
        lax.all_gather(qkv_weight, "dp", axis=0, tiled=True),
        lax.all_gather(attn_out_weight, "dp", axis=1, tiled=True),
        lax.all_gather(cross_q_weight, "dp", axis=0, tiled=True),
        lax.all_gather(cross_kv_weight, "dp", axis=0, tiled=True),
        lax.all_gather(cross_out_weight, "dp", axis=1, tiled=True),
        lax.all_gather(gate_up_weight, "dp", axis=0, tiled=True),
        lax.all_gather(down_weight, "dp", axis=1, tiled=True),
    )
    gain_first = gain_one.astype(jnp.float32)
    gain_second = gain_two.astype(jnp.float32)
    gain_third = gain_three.astype(jnp.float32)
    grad_top = out_cotangent.astype(jnp.float32)
    third_grads = spread_grads(out_cotangent)
    grad_hidden = times_transposed(third_grads, w_down)
    grad_down = rows_by_rows(hidden, third_grads)
    gated_out, gated_pull = jax.vjp(gated, gate_vals, up_vals)
    grad_gate, grad_up = gated_pull(grad_hidden)
    grad_gate_up = (
        jnp.stack([grad_gate, grad_up], axis=1)
        .astype(jnp.bfloat16)
        .reshape(group_rows, 2 * hidden_here)
    )
    grad_gu_weight = rows_by_rows(third_all, grad_gate_up).reshape(model_width, 2, hidden_here)
    grad_third = gather_back(grad_gate_up, w_gu.reshape(model_width, 2 * hidden_here))
    norm_out, norm_pull = jax.vjp(layer_norm, after_cross, gain_third)
    part_rows, grad_gain_third = norm_pull(grad_third)
    grad_cross_rows = grad_top + part_rows
    second_grads = spread_grads(grad_cross_rows.astype(jnp.bfloat16))
    grad_cross_mixed = times_transposed(second_grads, w_co).astype(jnp.bfloat16)
    grad_co_weight = rows_by_rows(cross_flat, second_grads)
    cross_gq, cross_gk, cross_gv = lax.map(
        cross_backward,
        (
            by_sequence(cross_query),
            cross_kv,
            valid_slots,
            cross_lse,
            by_sequence(grad_cross_mixed.reshape(group_rows, heads_here, HD)),
        ),
    )
    grad_cross_query = (cross_gq * 0.125).astype(jnp.bfloat16).reshape(group_rows, head_cols)
    grad_cross_kv = (
        jnp.stack([cross_gk, cross_gv], axis=2)
        .astype(jnp.bfloat16)
        .reshape(seq_here * cond_slots, 2 * head_cols)
    )
    grad_cq_weight = rows_by_rows(second_all, grad_cross_query)
    grad_ckv_weight = rows_by_rows(cond_flat, grad_cross_kv).reshape(cond_width, 2, head_cols)
    cond_partial = times_transposed(
        grad_cross_kv, w_ckv.reshape(cond_width, 2 * head_cols)
    ).reshape(seq_here, cond_slots, cond_width)
    grad_cond = lax.psum_scatter(cond_partial, "tensor", scatter_dimension=2, tiled=True)
    grad_second = gather_back(grad_cross_query, w_cq)
    norm_out, norm_pull = jax.vjp(layer_norm, after_self, gain_second)
    part_rows, grad_gain_second = norm_pull(grad_second)
    grad_self_rows = grad_cross_rows + part_rows
    first_grads = spread_grads(grad_self_rows.astype(jnp.bfloat16))
    grad_self_mixed = times_transposed(first_grads, w_out).astype(jnp.bfloat16)
    grad_out_weight = rows_by_rows(self_flat, first_grads)
    self_gq, self_gk, self_gv = lax.map(
        self_backward,
        (
            by_sequence(query_rot),
            by_sequence(key_rot),
            by_sequence(value_rows),
            self_lse,
            by_sequence(grad_self_mixed.reshape(group_rows, heads_here, HD)),
        ),
    )
    grad_query = rotate_back(self_gq.reshape(group_rows, heads_here, HD) * 0.125, cosine, sine)
    grad_keys = rotate_back(self_gk.reshape(group_rows, heads_here, HD), cosine, sine)
    grad_values = self_gv.reshape(group_rows, heads_here, HD)
    grad_qkv_all = (
        jnp.stack([grad_query, grad_keys, grad_values], axis=1)
        .astype(jnp.bfloat16)
        .reshape(group_rows, 3 * head_cols)
    )
    grad_qkv_weight = rows_by_rows(first_all, grad_qkv_all).reshape(model_width, 3, head_cols)
    grad_first = gather_back(grad_qkv_all, w_qkv.reshape(model_width, 3 * head_cols))
    norm_out, norm_pull = jax.vjp(layer_norm, input_rows, gain_first)
    part_rows, grad_gain_first = norm_pull(grad_first)
    grad_input = grad_self_rows + part_rows
    owned = (
        lax.psum_scatter(grad_gain_first, "dp", scatter_dimension=0, tiled=True),
        lax.psum_scatter(grad_gain_second, "dp", scatter_dimension=0, tiled=True),
        lax.psum_scatter(grad_gain_third, "dp", scatter_dimension=0, tiled=True),
        lax.psum_scatter(grad_qkv_weight, "dp", scatter_dimension=0, tiled=True),
        lax.psum_scatter(grad_out_weight, "dp", scatter_dimension=1, tiled=True),
        lax.psum_scatter(grad_cq_weight, "dp", scatter_dimension=0, tiled=True),
        lax.psum_scatter(grad_ckv_weight, "dp", scatter_dimension=0, tiled=True),
        lax.psum_scatter(grad_co_weight, "dp", scatter_dimension=1, tiled=True),
        lax.psum_scatter(grad_gu_weight, "dp", scatter_dimension=0, tiled=True),
        lax.psum_scatter(grad_down, "dp", scatter_dimension=1, tiled=True),
    )
    gain_grads = lax.psum((owned[0], owned[1], owned[2]), "tensor")
    return (
        block_out,
        grad_input,
        grad_cond,
        gain_grads[0],
        gain_grads[1],
        gain_grads[2],
        owned[3],
        owned[4],
        owned[5],
        owned[6],
        owned[7],
        owned[8],
        owned[9],
    )


def general_solution(mesh):
    return jax.shard_map(
        general_body,
        mesh=mesh,
        in_specs=(
            P(("dp", "tensor"), None),
            P("dp", None, None),
            P("dp"),
            P("dp"),
            P("dp"),
            P("dp"),
            P("dp", None, "tensor"),
            P("tensor", "dp"),
            P("dp", "tensor"),
            P("dp", None, "tensor"),
            P("tensor", "dp"),
            P("dp", None, "tensor"),
            P("tensor", "dp"),
            P(("dp", "tensor"), None),
        ),
        out_specs=(
            P(("dp", "tensor"), None),
            P(("dp", "tensor"), None),
            P("dp", None, "tensor"),
            P("dp"),
            P("dp"),
            P("dp"),
            P("dp", None, "tensor"),
            P("tensor", "dp"),
            P("dp", "tensor"),
            P("dp", None, "tensor"),
            P("tensor", "dp"),
            P("dp", None, "tensor"),
            P("tensor", "dp"),
        ),
        check_vma=False,
    )


def dot(left, right, dims=NN):
    return lax.dot_general(left, right, dims, preferred_element_type=F32)


def iota(shape, axis):
    return lax.broadcasted_iota(jnp.int32, shape, axis)


def whole(shape):
    return pl.BlockSpec(shape, lambda *p: (0,) * len(shape), pipeline_mode=pl.Buffered(1))


def columns_of(rows, first=0):
    return pl.BlockSpec((rows, 128), lambda p, s: (0, first + p))


SCALAR = pl.BlockSpec(memory_space=pltpu.SMEM)


def shaped(shape, dtype):
    return jax.ShapeDtypeStruct(shape, dtype)


def call(kernel, grid, ins, outs, name, micros, scratch=(), after=(), scalars=None):
    lead = 0 if scalars is None else 1

    def without_after(*refs):
        kernel(*refs[: lead + len(ins)], *refs[lead + len(ins) + len(after) :])

    in_specs = [spec for spec, _ in ins] + [pl.BlockSpec(memory_space=pl.ANY)] * len(after)
    out_specs = [spec for spec, _ in outs]
    if lead:
        how = dict(
            grid_spec=pltpu.PrefetchScalarGridSpec(
                num_scalar_prefetch=1, grid=grid, in_specs=in_specs, out_specs=out_specs,
                scratch_shapes=list(scratch),
            )
        )
    else:
        how = dict(
            grid=grid, in_specs=in_specs, out_specs=out_specs, scratch_shapes=list(scratch)
        )
    return pl.pallas_call(
        without_after,
        **how,
        out_shape=[shape for _, shape in outs],
        compiler_params=pltpu.CompilerParams(vmem_limit_bytes=VMEM_BYTES),
        cost_estimate=pl.CostEstimate(
            flops=int(micros * FLOPS), bytes_accessed=0, transcendentals=0
        ),
        name=name,
    )(*([] if scalars is None else [scalars]), *[array for _, array in ins], *after)


def unravel(shard):
    size = 4 * shard
    source, target = iota((size, size), 0), iota((size, size), 1)
    z, core, at = source // (2 * shard), (source // shard) % 2, source % shard
    return jnp.where(core * 2 * shard + z * shard + at == target, 1.0, 0.0).astype(BF)


def put_in_order(values, turn, odd):
    size = turn.shape[0]
    own, other = [], []
    for at in range(0, values.shape[1], size):
        both = dot(values[:, at : at + size], turn)
        even, odds = both[:, : size // 2], both[:, size // 2 :]
        own.append(jnp.where(odd, odds, even))
        other.append(jnp.where(odd, even, odds))
    return jnp.concatenate(own + other, axis=1)


def put_back(values, turn, odd, parts):
    size = turn.shape[0]
    middle = values.shape[1] // 2
    result = []
    for at in range(0, middle, size // 2):
        own = values[:, at : at + size // 2]
        other = values[:, middle + at : middle + at + size // 2]
        both = jnp.concatenate(
            [jnp.where(odd, other, own), jnp.where(odd, own, other)], axis=1
        )
        total = None
        for _ in range(parts):
            term = both.astype(BF)
            moved = dot(term, turn, NT)
            total = moved if total is None else total + moved
            both = both - term.astype(F32)
        result.append(total)
    return jnp.concatenate(result, axis=1)


def hold(array, after):
    anywhere = pl.BlockSpec(memory_space=pl.ANY)
    return pl.pallas_call(
        lambda *refs: None,
        in_specs=[anywhere] * (1 + len(after)),
        out_specs=anywhere,
        out_shape=shaped(array.shape, array.dtype),
        input_output_aliases={0: 0},
        cost_estimate=pl.CostEstimate(flops=0, bytes_accessed=0, transcendentals=0),
        name="hold",
    )(array, *after)


def normalize(values):
    centre = values - jnp.mean(values, axis=-1, keepdims=True)
    scale = lax.rsqrt(jnp.mean(centre * centre, axis=-1, keepdims=True) + EPSILON)
    return centre * scale, scale


def normalize_back(grads, gain, normal, scale):
    inner = grads * gain
    return (
        inner
        - jnp.mean(inner, axis=-1, keepdims=True)
        - normal * jnp.mean(inner * normal, axis=-1, keepdims=True)
    ) * scale


def first_norm(mine_ref, theirs_ref, gains_ref, out_ref, across_ref):
    rows = mine_ref.shape[0]
    step = 256
    for ref, base in ((mine_ref, 0), (theirs_ref, rows)):
        for at in range(0, rows, step):
            normal, _ = normalize(ref[at : at + step, :].astype(F32))
            out = (normal * gains_ref[0:1, :]).astype(BF)
            out_ref[base + at : base + at + step, :] = out
            across_ref[:, base + at : base + at + step] = jnp.transpose(out)


QKV_CHAINS = (("z2", "z1", "y", "c"), ("z2", "y", "z1", "c"))
SQUARE_CHAINS = (
    ("z2", "z1", "y", "x", "c"),
    ("z2", "z1", "x", "y", "c"),
    ("z2", "x", "y", "z1", "c"),
    ("z2", "z1", "y", "x", "c"),
)
AXES = ("z2", "z1", "c", "y", "x")
STEPS = (
    "Q0.0", "Q1.0", "S0.0", "Q1.1", "S1.0", "in", "S2.0", "S3.0", "Q0.1", "S0.1", "top",
    "Q0.2", "Q1.2", "S2.1", "S1.1", "S0.2", "S3.1", "Q0.3", "Q1.3", "S1.2", "S2.2", "S3.2",
    "S0.3", "S2.3", "S1.3", "S0.4", "S2.4", "S3.3", "S1.4", "S3.4",
)


def gather_kernel(
    qkv_ref, square_ref, gains_ref, rows_ref, tops_ref, gu_ref, down_ref,
    wq_ref, w0_ref, w1_ref, w2_ref, w3_ref,
    mine_ref, theirs_ref, tops_out, their_tops_ref, gains_out, first_ref, across_ref, turn_ref,
    *rest,
):
    *pack_refs, sum_ref, slot_ref, sends, receives, local_sems = rest
    dp, seq, side = (lax.axis_index(name) for name in ("dp", "seq", "half"))
    here = {"z2": dp // 4, "z1": (dp // 2) % 2, "c": dp % 2, "y": seq, "x": side}
    partners = {
        "z2": (dp + 4 - 8 * (dp // 4), seq, side),
        "z1": (dp + 2 - 4 * ((dp // 2) % 2), seq, side),
        "c": (dp + 1 - 2 * (dp % 2), seq, side),
        "y": (dp, 1 - seq, side),
        "x": (dp, seq, 1 - side),
    }
    barrier = pltpu.get_barrier_semaphore()
    for axis in AXES:
        pl.semaphore_signal(
            barrier, inc=1, device_id=partners[axis], device_id_type=pl.DeviceIdType.MESH
        )
    pl.semaphore_wait(barrier, len(AXES))
    count = [0]

    def send(source, target, axis):
        copy = pltpu.make_async_remote_copy(
            source, target, sends.at[count[0]], receives.at[count[0]],
            device_id=partners[axis], device_id_type=pl.DeviceIdType.MESH,
        )
        count[0] += 1
        copy.start()
        return copy

    chains = {}
    columns = qkv_ref.shape[1]
    cut = columns // 2 // 128 * 128 + 128
    for at, (order, low, high) in enumerate(
        ((QKV_CHAINS[0], 0, cut), (QKV_CHAINS[1], cut, columns))
    ):
        chains["Q%d" % at] = (wq_ref, qkv_ref, low, high, order, AXES[:4])
    wide = square_ref.shape[1] // 4
    for at, (order, ref) in enumerate(zip(SQUARE_CHAINS, (w0_ref, w1_ref, w2_ref, w3_ref))):
        chains["S%d" % at] = (ref, square_ref, at * wide, (at + 1) * wide, order, AXES)

    own_copies = {}

    def region(name, step):
        ref, _, low, high, order, axes = chains[name]
        grown = order[:step]
        index = tuple(slice(None) if axis in grown else here[axis] for axis in axes)
        if name[0] == "Q":
            index += (slice(None), slice(low, high))
        return ref.at[index]

    def begin(name, step):
        _, source, low, high, order, _ = chains[name]
        if step == 0:
            part = source.at[:, slice(low, high)]
            copy = pltpu.make_async_copy(part, region(name, 0), local_sems.at[len(own_copies)])
            copy.start()
            own_copies[name] = copy
            return send(part, region(name, 0), order[0])
        if step == 1:
            own_copies[name].wait()
        return send(region(name, step), region(name, step), order[step])

    flying = {}
    for name in chains:
        flying[name] = begin(name, 0)
    odd = here["c"] == 1
    turn_ref[...] = unravel(qkv_ref.shape[0])
    turn = turn_ref[...]
    mine_ref[...] = put_in_order(rows_ref[...], turn, odd).astype(BF)
    swaps = {"in": send(mine_ref, theirs_ref, "x")}
    tops_out[...] = put_in_order(tops_ref[...], turn, odd).astype(BF)
    sum_ref[...] = gains_ref[...]
    for at, axis in enumerate(("c", "z1", "z2")):
        copy = send(sum_ref, slot_ref.at[at], axis)
        copy.wait()
        sum_ref[...] += slot_ref[at]
    gains_out[...] = put_in_order(sum_ref[...].astype(BF), turn, odd)
    hidden = down_ref.shape[0]
    tiles = hidden // len(pack_refs) // TILE
    for i, pack_ref in enumerate(pack_refs):
        for j in range(tiles):
            at, low = 3 * j * TILE, (i * tiles + j) * TILE
            pack_ref[:, at : at + TILE] = gu_ref[:, low : low + TILE]
            pack_ref[:, at + TILE : at + 2 * TILE] = gu_ref[:, hidden + low : hidden + low + TILE]
            pack_ref[:, at + 2 * TILE : at + 3 * TILE] = jnp.transpose(
                down_ref[low : low + TILE, :]
            )

    for event in STEPS:
        if event in ("in", "top"):
            swaps[event].wait()
            if event == "in":
                swaps["top"] = send(tops_out, their_tops_ref, "x")
                first_norm(mine_ref, theirs_ref, gains_out, first_ref, across_ref)
            continue
        name, step = event.split(".")
        flying[name].wait()
        if int(step) + 1 < len(chains[name][4]):
            flying[name] = begin(name, int(step) + 1)


def gather_first(qkv, square, gains, rows, tops, gate_up, down):
    anywhere, vmem = pl.BlockSpec(memory_space=pl.ANY), pl.BlockSpec(memory_space=pltpu.VMEM)
    shard = qkv.shape[0]
    wide = square.shape[1] // 4
    count, width = rows.shape
    copies = 4 * 2 + 5 * 4 + 2 + 3
    return pl.pallas_call(
        gather_kernel,
        in_specs=[anywhere, anywhere] + [vmem] * 5,
        out_specs=[anywhere] * 5 + [vmem] * (8 + CHUNKS),
        out_shape=[shaped((2, 2, 2, 2) + qkv.shape, BF)]
        + [shaped((2, 2, 2, 2, 2, shard, wide), BF)] * 4
        + [shaped(rows.shape, BF)] * 4
        + [shaped(gains.shape, F32), shaped((2 * count, width), BF), shaped((width, 2 * count), BF)]
        + [shaped((4 * shard, 4 * shard), BF)]
        + [shaped((shard, 3 * down.shape[0] // CHUNKS), BF)] * CHUNKS,
        scratch_shapes=[
            pltpu.VMEM(gains.shape, F32),
            pltpu.VMEM((3,) + gains.shape, F32),
            pltpu.SemaphoreType.DMA((copies,)),
            pltpu.SemaphoreType.DMA((copies,)),
            pltpu.SemaphoreType.DMA((6,)),
        ],
        compiler_params=pltpu.CompilerParams(
            vmem_limit_bytes=VMEM_BYTES, collective_id=0, has_side_effects=True
        ),
        name="gather_first",
    )(qkv, square, gains, rows, tops, gate_up, down)


def across_kernel(*refs):
    count = len(refs) // 2
    for source, target in zip(refs[:count], refs[count:]):
        step = 256
        for at in range(0, source.shape[0], step):
            target[:, at : at + step] = jnp.transpose(source[at : at + step, :])


def across(*arrays):
    shape = arrays[0].shape
    flipped = (shape[1], shape[0])
    return call(
        across_kernel, (1,),
        [(whole(shape), array) for array in arrays],
        [(whole(flipped), shaped(flipped, BF))] * len(arrays),
        "across", 3 * len(arrays),
    )


def rot(values, tables):
    cosine, sine_up, sine_down = tables
    return (
        values * cosine
        + pltpu.roll(values, 16, 1) * sine_up
        + pltpu.roll(values, 112, 1) * sine_down
    )


def rot_back(grads, tables):
    cosine, sine_up, sine_down = tables
    return (
        grads * cosine
        - pltpu.roll(grads, 16, 1) * sine_up
        - pltpu.roll(grads, 112, 1) * sine_down
    )


def rot_tables(positions):
    quarter = HD // 4
    inverse = 10000.0 ** (-jnp.arange(quarter).astype(F32) / quarter)
    angle_grid = positions.astype(F32)[:, None] * inverse[None, :]
    cosine, sine = jnp.cos(angle_grid), jnp.sin(angle_grid)
    rest = jnp.zeros((positions.shape[0], 2 * quarter), F32)
    none = jnp.zeros_like(sine)
    return (
        jnp.concatenate([cosine, cosine, rest + 1.0] * 2, axis=1),
        jnp.concatenate([none, sine, rest] * 2, axis=1),
        jnp.concatenate([-sine, none, rest] * 2, axis=1),
    )


def to_rows(picks, columns):
    first = columns.astype(BF)
    rest = columns - first.astype(F32)
    second = rest.astype(BF)
    third = (rest - second.astype(F32)).astype(BF)
    return dot(picks, first, NT) + dot(picks, second, NT) + dot(picks, third, NT)


def self_forward_kernel(
    step, place_ref, rows_ref, own_ref, other_ref, c_ref, su_ref, sd_ref,
    q_ref, k_ref, v_ref, mine_ref, theirs_ref, lse_ref,
):
    count, width = rows_ref.shape
    half = width // 2
    own, other = own_ref[...].reshape(half, 384), other_ref[...].reshape(half, 384)
    qkv = dot(rows_ref[:, :half], own) + dot(rows_ref[:, half:], other)
    tables = (c_ref[...], su_ref[...], sd_ref[...])
    query = (rot(qkv[:, :128], tables) * 0.125).astype(BF)
    key = rot(qkv[:, 128:256], tables).astype(BF)
    value = qkv[:, 256:].astype(BF)
    q_ref[...] = query
    k_ref[...] = key
    v_ref[...] = value
    lane = iota((step, 128), 1)
    picks = jnp.where(iota((8, 128), 0) == iota((8, 128), 1), 1.0, 0.0).astype(BF)
    for at in range(0, count, step):
        part = query[at : at + step]
        mixed, logs = [], []
        for head in range(2):
            here = (lane // HD) == head
            scores = dot(jnp.where(here, part, jnp.zeros_like(part)), key, NT)
            top = jnp.max(scores, axis=1, keepdims=True)
            weights = jnp.exp(scores - top)
            total = jnp.sum(weights, axis=1, keepdims=True)
            mixed.append(dot(weights.astype(BF), value) * (1.0 / total))
            logs.append(top + jnp.log(total))
        out = jnp.where(lane < HD, mixed[0], mixed[1]).astype(BF)
        both = jnp.where(lane == 0, logs[0], jnp.where(lane == 1, logs[1], 0.0))
        lse_ref[0, :, at : at + step] = to_rows(picks, both)
        if at < count // 2:
            mine_ref[at : at + step, :] = out
        else:
            theirs_ref[at - count // 2 : at - count // 2 + step, :] = out


def self_weights(weights, first=0):
    shape = (weights.shape[0], 1, 1, weights.shape[3], 384)
    return [
        (pl.BlockSpec(shape, lambda p, s: (0, s[0], p % 2, 0, first // 2 + p // 2)), weights),
        (pl.BlockSpec(shape, lambda p, s: (0, 1 - s[0], p % 2, 0, first // 2 + p // 2)), weights),
    ]


def self_forward(place, rows, weights, tables, after=()):
    count, width = rows.shape
    wide = weights.shape[2] * weights.shape[4] // 3
    pairs = wide // 128
    return call(
        functools.partial(self_forward_kernel, 512),
        (pairs,),
        [(whole(rows.shape), rows)] + self_weights(weights)
        + [(whole((count, 128)), table) for table in tables],
        [(columns_of(count), shaped((count, wide), BF))] * 3
        + [(columns_of(count // 2), shaped((count // 2, wide), BF))] * 2
        + [(pl.BlockSpec((1, 8, count), lambda p, s: (p, 0, 0)), shaped((pairs, 8, count), F32))],
        "self_forward", 7 * pairs,
        after=after,
        scalars=place,
    )


def self_backward_kernel(
    step, begins, ends, place_ref, q_ref, k_ref, v_ref, mine_ref, theirs_ref, dmine_ref, dtheirs_ref, lse_ref,
    c_ref, su_ref, sd_ref, across_ref, own_ref, other_ref, *rest,
):
    if begins:
        gown_ref, gother_ref, *outs, qkv_ref, sum_ref = rest
    else:
        start_ref, gown_ref, gother_ref, *outs, qkv_ref, sum_ref = rest
    count = q_ref.shape[0]
    query = q_ref[...]
    grads = jnp.concatenate([dmine_ref[...], dtheirs_ref[...]], axis=0)
    mixed = jnp.concatenate([mine_ref[...], theirs_ref[...]], axis=0)
    picks = jnp.where((iota((8, 128), 1) // HD) == iota((8, 128), 0), 1.0, 0.0).astype(BF)
    delta = to_rows(picks, grads.astype(F32) * mixed.astype(F32))
    lane = iota((step, 128), 1)
    row = iota((128, step), 0)
    keys_across = jnp.transpose(k_ref[...].astype(F32)).astype(BF)
    query_across = jnp.zeros((128, count), F32)
    tables = (c_ref[...], su_ref[...], sd_ref[...])
    for at in range(0, count, step):
        here = slice(at, at + step)
        key, value = k_ref[here, :], v_ref[here, :]
        flipped = keys_across[:, here]
        dkeys, dvalues = [], []
        for head in range(2):
            inside = (lane // HD) == head
            scores = dot(jnp.where(inside, key, jnp.zeros_like(key)), query, NT)
            probs = jnp.exp(scores - lse_ref[0, head : head + 1, :])
            dprobs = dot(jnp.where(inside, value, jnp.zeros_like(value)), grads, NT)
            dscores = (probs * (dprobs - delta[head : head + 1, :])).astype(BF)
            dvalues.append(dot(probs.astype(BF), grads))
            dkeys.append(dot(dscores, query))
            picked = jnp.where((row // HD) == head, flipped, jnp.zeros_like(flipped))
            query_across = query_across + dot(picked, dscores)
        dkey = jnp.where(lane < HD, dkeys[0], dkeys[1])
        dvalue = jnp.where(lane < HD, dvalues[0], dvalues[1])
        qkv_ref[here, 128:256] = rot_back(dkey, [t[here] for t in tables]).astype(BF)
        qkv_ref[here, 256:384] = dvalue.astype(BF)
    dquery = jnp.transpose(query_across)
    qkv_ref[:, 0:128] = (rot_back(dquery, tables) * 0.125).astype(BF)

    first = pl.program_id(0) == 0
    last = pl.program_id(0) == pl.num_programs(0) - 1
    half = across_ref.shape[0] // 2
    own, other = own_ref[...].reshape(half, 384), other_ref[...].reshape(half, 384)
    both = qkv_ref[...]
    gown_ref[0] = dot(across_ref[:half, :], both).astype(BF)
    gother_ref[0] = dot(across_ref[half:, :], both).astype(BF)
    back = jnp.concatenate([dot(both, own, NT), dot(both, other, NT)], axis=1)

    @pl.when(first)
    def _():
        sum_ref[...] = back if begins else start_ref[...] + back

    @pl.when(jnp.logical_not(first))
    def _():
        sum_ref[...] += back

    @pl.when(last)
    def _():
        if ends:
            outs[0][...] = sum_ref[: count // 2, :].astype(BF)
            outs[1][...] = sum_ref[count // 2 :, :].astype(BF)
        else:
            outs[0][...] = sum_ref[...]


def self_backward(
    place, query, key, value, mine, theirs, dmine, dtheirs, lse, tables, flipped, weights, first, pairs,
    start, ends, after=(),
):
    count = query.shape[0]
    wide = 128 * pairs
    width = flipped.shape[0]
    out = pl.BlockSpec((1, width // 2, 384), lambda p, s: (p % 2, 0, p // 2))
    out_shape = (2, width // 2, 192 * pairs)
    rows, half = columns_of(count, first), columns_of(count // 2, first)
    half_rows = (count // 2, width)
    all_rows = (count, width)
    if ends:
        sums = [(whole(half_rows), shaped(half_rows, BF))] * 2
    else:
        sums = [(whole(all_rows), shaped(all_rows, F32))]
    starts = [] if start is None else [(whole(all_rows), start)]
    return call(
        functools.partial(self_backward_kernel, 512, start is None, ends),
        (pairs,),
        [(rows, array) for array in (query, key, value)]
        + [(half, array) for array in (mine, theirs, dmine, dtheirs)]
        + [(pl.BlockSpec((1, 8, count), lambda p, s: (first + p, 0, 0)), lse)]
        + [(whole((count, 128)), table) for table in tables]
        + [(whole(flipped.shape), flipped)] + self_weights(weights, first) + starts,
        [(out, shaped(out_shape, BF))] * 2 + sums,
        "self_backward", 13 * pairs,
        scratch=[pltpu.VMEM((count, 384), BF), pltpu.VMEM((count, width), F32)],
        after=after,
        scalars=place,
    )


def ffn_kernel(
    tile, carried, place_ref, mine_ref, theirs_ref, fmine_ref, ftheirs_ref,
    tmine_ref, ttheirs_ref, gmine_ref, gtheirs_ref, own_ref, other_ref, *rest,
):
    starts, rest = rest[: 4 * carried], rest[4 * carried :]
    ymine_ref, ytheirs_ref, dmine_ref, dtheirs_ref, gown_ref, gother_ref, y_ref, d_ref = rest
    rows, width = mine_ref.shape
    half = width // 2
    both = 2 * tile
    first = pl.program_id(0) == 0
    last = pl.program_id(0) == pl.num_programs(0) - 1

    @pl.when(first)
    def _():
        if carried:
            for part in range(2):
                y_ref[part] = starts[part][...].astype(F32)
                d_ref[part] = starts[2 + part][...].astype(F32)
        else:
            y_ref[...] = jnp.zeros_like(y_ref)
            d_ref[...] = jnp.zeros_like(d_ref)

    own = own_ref[...].reshape(half, 3 * tile)
    other = other_ref[...].reshape(half, 3 * tile)
    hidden_parts, dgate_up_parts = [], []
    for part, (ref, top_ref) in enumerate(((mine_ref, tmine_ref), (theirs_ref, ttheirs_ref))):
        gate_up = dot(ref[:, :half], own[:, :both]) + dot(ref[:, half:], other[:, :both])
        dhidden = dot(top_ref[:, :half], own[:, both:]) + dot(top_ref[:, half:], other[:, both:])
        gate, up = gate_up[:, :tile], gate_up[:, tile:]
        sigma = 1.0 / (1.0 + jnp.exp(-gate))
        silu = gate * sigma
        hidden = (silu * up).astype(BF)
        dup = (dhidden * silu).astype(BF)
        dgate = (dhidden * up * (sigma * (1.0 + gate * (1.0 - sigma)))).astype(BF)
        dgate_up = jnp.concatenate([dgate, dup], axis=1)
        y_ref[part, :, :half] += dot(hidden, own[:, both:], NT)
        y_ref[part, :, half:] += dot(hidden, other[:, both:], NT)
        d_ref[part, :, :half] += dot(dgate_up, own[:, :both], NT)
        d_ref[part, :, half:] += dot(dgate_up, other[:, :both], NT)
        hidden_parts.append(hidden)
        dgate_up_parts.append(dgate_up)
    for out, cut in ((gown_ref, slice(0, half)), (gother_ref, slice(half, width))):
        out[0, :, :both] = (
            dot(fmine_ref[cut, :], dgate_up_parts[0]) + dot(ftheirs_ref[cut, :], dgate_up_parts[1])
        ).astype(BF)
        out[0, :, both:] = (
            dot(gmine_ref[cut, :], hidden_parts[0]) + dot(gtheirs_ref[cut, :], hidden_parts[1])
        ).astype(BF)

    @pl.when(last)
    def _():
        ymine_ref[...] = y_ref[0].astype(BF)
        ytheirs_ref[...] = y_ref[1].astype(BF)
        dmine_ref[...] = d_ref[0].astype(BF)
        dtheirs_ref[...] = d_ref[1].astype(BF)


def ffn(place, rows, flipped, tops, tops_flipped, weights, tile, starts=(), after=()):
    count, width = rows[0].shape
    zs, _, groups, shard, wide = weights.shape
    half = zs * shard
    tiles = wide // (3 * tile)
    own_block = pl.BlockSpec(
        (zs, 1, 1, shard, 3 * tile), lambda p, s: (0, s[0], p // tiles, 0, p % tiles)
    )
    other_block = pl.BlockSpec(
        (zs, 1, 1, shard, 3 * tile), lambda p, s: (0, 1 - s[0], p // tiles, 0, p % tiles)
    )
    block = pl.BlockSpec((1, half, 3 * tile), lambda p, s: (p // tiles, 0, p % tiles))
    out = shaped((groups, half, wide), BF)
    once, fixed = whole((count, width)), whole((width, count))
    return call(
        functools.partial(ffn_kernel, tile, len(starts) // 4),
        (groups * tiles,),
        [(once, a) for a in rows] + [(fixed, a) for a in flipped]
        + [(once, a) for a in tops] + [(fixed, a) for a in tops_flipped]
        + [(own_block, weights), (other_block, weights)] + [(once, a) for a in starts],
        [(once, shaped((count, width), BF))] * 4 + [(block, out)] * 2,
        "feed_forward", 9 * groups * tiles,
        scratch=[pltpu.VMEM((2, count, width), F32)] * 2,
        after=after,
        scalars=place,
    )


def section(square, other):
    zs, _, ys, xs, shard, wide = square.shape
    return (
        pl.BlockSpec(
            (zs, 1, ys, xs, shard, wide),
            lambda *a: (0, 1 - a[-1][0] if other else a[-1][0], 0, 0, 0, 0),
            pipeline_mode=pl.Buffered(1),
        ),
        square,
    )


def sections(squares):
    return [section(squares[n], other) for n in (0, 1, 3) for other in (False, True)]


def weight_of(ref, x, y):
    zs, _, _, _, shard, wide = ref.shape
    return ref[:, 0, y, x].reshape(zs * shard, wide)


def cond_kernel(place_ref, cond_ref, own_ref, other_ref, key_ref, value_ref):
    shard = cond_ref.shape[1] // 8
    half = 4 * shard
    wide = own_ref.shape[-1]
    for x in range(2):
        for y in range(2):
            at = (2 * x + y) * wide
            for kind, out in ((0, key_ref), (1, value_ref)):
                total = None
                for part, ref in ((0, own_ref), (1, other_ref)):
                    weight = ref[:, 0, y, x, kind * shard : (kind + 1) * shard, :]
                    weight = weight.reshape(half, wide)
                    term = dot(cond_ref[:, part * half : (part + 1) * half], weight)
                    total = term if total is None else total + term
                out[:, at : at + wide] = total.astype(BF)


def cond_forward(place, cond, square):
    slots, width = cond.shape
    wide = 4 * square.shape[-1]
    return call(
        cond_kernel, (1,),
        [(whole(cond.shape), cond), section(square, False), section(square, True)],
        [(whole((slots, wide)), shaped((slots, wide), BF))] * 2,
        "cond_forward", 6,
        scalars=place,
    )


def beside(ref, y):
    return jnp.concatenate(
        [ref[:, at : at + 128] for at in range(y * 128, ref.shape[1], 256)], axis=1
    )


def middle_forward_kernel(
    place_ref, rows_ref, mine_ref, theirs_ref, gains_ref, key_ref, value_ref,
    out_own, out_other, cq_own, cq_other, co_own, co_other,
    x1_ref, second_ref, query_ref, mixed_ref, x2_ref, third_ref,
):
    rows, width = rows_ref.shape
    half = width // 2
    wide = out_own.shape[-1]
    slots = key_ref.shape[0]
    valid = iota((rows, slots), 1) < place_ref[3]
    lane = iota((rows, 128), 1)
    for out, cut in ((out_own, 0), (out_other, half)):
        total = rows_ref[:, cut : cut + half].astype(F32)
        for x in range(2):
            for y in range(2):
                mixed = jnp.where(
                    place_ref[2] == x, beside(mine_ref, y), beside(theirs_ref, y)
                )
                total += dot(mixed, weight_of(out, x, y), NT)
        x1_ref[:, cut : cut + half] = total
    normal, _ = normalize(x1_ref[...])
    second = (normal * gains_ref[1:2, :]).astype(BF)
    second_ref[...] = second
    for x in range(2):
        for y in range(2):
            at = (2 * x + y) * wide
            query = dot(second[:, :half], weight_of(cq_own, x, y)) + dot(
                second[:, half:], weight_of(cq_other, x, y)
            )
            query_ref[:, at : at + wide] = (query * 0.125).astype(BF)
    for at in range(0, 4 * wide, 128):
        query, key, value = (
            ref[:, at : at + 128] for ref in (query_ref, key_ref, value_ref)
        )
        mixed = []
        for head in range(2):
            part = jnp.where((lane // HD) == head, query, jnp.zeros_like(query))
            scores = jnp.where(valid, dot(part, key, NT), MASKED_SCORE)
            top = jnp.max(scores, axis=1, keepdims=True)
            weights = jnp.exp(scores - top)
            total = jnp.sum(weights, axis=1, keepdims=True)
            mixed.append(dot(weights.astype(BF), value) * (1.0 / total))
        mixed_ref[:, at : at + 128] = jnp.where(lane < HD, mixed[0], mixed[1]).astype(BF)
    for out, cut in ((co_own, 0), (co_other, half)):
        total = x1_ref[:, cut : cut + half]
        for x in range(2):
            for y in range(2):
                at = (2 * x + y) * wide
                total += dot(mixed_ref[:, at : at + wide], weight_of(out, x, y), NT)
        x2_ref[:, cut : cut + half] = total
    normal, _ = normalize(x2_ref[...])
    third_ref[...] = (normal * gains_ref[2:3, :]).astype(BF)


def middle_forward(place, rows, mine, theirs, gains, key, value, squares, after=()):
    full = whole(rows.shape)
    part = whole(mine.shape)
    cond = whole(key.shape)
    return call(
        middle_forward_kernel, (1,),
        [(full, rows), (part, mine), (part, theirs)]
        + [(whole(gains.shape), gains), (cond, key), (cond, value)] + sections(squares),
        [(full, shaped(rows.shape, dtype)) for dtype in (F32, BF, BF, BF, F32, BF)],
        "middle_forward", 26,
        after=after, scalars=place,
    )


def middle_backward_kernel(
    place_ref, d_ref, r_ref, top_ref, x2_ref, x1_ref, gains_ref,
    query_ref, key_ref, value_ref,
    out_own, out_other, cq_own, cq_other, co_own, co_other,
    dx1_ref, e2_ref, dquery_ref, dkey_ref, dvalue_ref, e1_ref, *refs,
):
    dmine_ref, dtheirs_ref, dmixed_ref = refs
    rows, width = x1_ref.shape
    half = width // 2
    wide = out_own.shape[-1]
    slots = key_ref.shape[0]
    grad_third = d_ref[...].astype(F32) + r_ref[...].astype(F32)
    normal, scale = normalize(x2_ref[...])
    dx2 = top_ref[...].astype(F32) + normalize_back(grad_third, gains_ref[2:3, :], normal, scale)
    dx1_ref[...] = dx2
    e2 = dx2.astype(BF)
    e2_ref[...] = e2
    for x in range(2):
        for y in range(2):
            at = (2 * x + y) * wide
            dmixed_ref[:, at : at + wide] = (
                dot(e2[:, :half], weight_of(co_own, x, y))
                + dot(e2[:, half:], weight_of(co_other, x, y))
            ).astype(BF)
    valid = iota((slots, rows), 0) < place_ref[3]
    lane = iota((slots, 128), 1)
    row = iota((128, slots), 0)
    for at in range(0, 4 * wide, 128):
        here = slice(at, at + 128)
        query, key, value, grads = (
            ref[:, here] for ref in (query_ref, key_ref, value_ref, dmixed_ref)
        )
        flipped = jnp.transpose(key.astype(F32)).astype(BF)
        dkeys, dvalues = [], []
        query_across = None
        for head in range(2):
            inside = (lane // HD) == head
            scores = dot(jnp.where(inside, key, jnp.zeros_like(key)), query, NT)
            scores = jnp.where(valid, scores, MASKED_SCORE)
            weights = jnp.exp(scores - jnp.max(scores, axis=0, keepdims=True))
            probs = weights * (1.0 / jnp.sum(weights, axis=0, keepdims=True))
            dprobs = dot(jnp.where(inside, value, jnp.zeros_like(value)), grads, NT)
            shared = jnp.sum(probs * dprobs, axis=0, keepdims=True)
            dscores = (probs * (dprobs - shared)).astype(BF)
            dvalues.append(dot(probs.astype(BF), grads))
            dkeys.append(dot(dscores, query))
            term = dot(jnp.where((row // HD) == head, flipped, jnp.zeros_like(flipped)), dscores)
            query_across = term if query_across is None else query_across + term
        dkey_ref[:, here] = jnp.where(lane < HD, dkeys[0], dkeys[1]).astype(BF)
        dvalue_ref[:, here] = jnp.where(lane < HD, dvalues[0], dvalues[1]).astype(BF)
        dquery_ref[:, here] = (jnp.transpose(query_across) * 0.125).astype(BF)
    parts = []
    for weight in (cq_own, cq_other):
        total = None
        for x in range(2):
            for y in range(2):
                at = (2 * x + y) * wide
                term = dot(dquery_ref[:, at : at + wide], weight_of(weight, x, y), NT)
                total = term if total is None else total + term
        parts.append(total)
    grad_second = jnp.concatenate(parts, axis=1)
    normal, scale = normalize(x1_ref[...])
    dx1 = dx1_ref[...] + normalize_back(grad_second, gains_ref[1:2, :], normal, scale)
    dx1_ref[...] = dx1
    e1 = dx1.astype(BF)
    e1_ref[...] = e1
    for y in range(2):
        first, second = (
            dot(e1[:, :half], weight_of(out_own, x, y))
            + dot(e1[:, half:], weight_of(out_other, x, y))
            for x in range(2)
        )
        low = place_ref[2] == 0
        for out, grads in (
            (dtheirs_ref, jnp.where(low, second, first).astype(BF)),
            (dmine_ref, jnp.where(low, first, second).astype(BF)),
        ):
            for j in range(wide // 128):
                at = (2 * j + y) * 128
                out[:, at : at + 128] = grads[:, j * 128 : (j + 1) * 128]


def middle_backward(
    place, d, r, top, x2, x1, gains, query, key, value, squares, after=()
):
    full = whole(x1.shape)
    rows, width = x1.shape
    part = (rows, width // 2)
    cond = whole(key.shape)
    return call(
        middle_backward_kernel, (1,),
        [(full, array) for array in (d, r, top, x2, x1)]
        + [(whole(gains.shape), gains), (full, query), (cond, key), (cond, value)]
        + sections(squares),
        [(full, shaped(x1.shape, F32)), (full, shaped(x1.shape, BF)), (full, shaped(x1.shape, BF))]
        + [(cond, shaped(key.shape, BF))] * 2
        + [(full, shaped(x1.shape, BF))]
        + [(whole(part), shaped(part, BF))] * 2,
        "middle_backward", 40,
        scratch=[pltpu.VMEM((rows, width), BF)],
        after=after,
        scalars=place,
    )


def middle_weights_kernel(
    pieces, place_ref, e1_ref, second_ref, dquery_ref, cond_ref, dkey_ref, dvalue_ref,
    e2_ref, mixed_ref, kv_own, kv_other, *rest,
):
    mine_refs, theirs_refs = rest[:pieces], rest[pieces : 2 * pieces]
    aown_ref, aother_ref, bown_ref, bother_ref, dcond_ref = rest[2 * pieces : 2 * pieces + 5]
    f1_ref, fsecond_ref, f2_ref, fcond_ref = rest[2 * pieces + 5 :]
    width = e1_ref.shape[1]
    half = width // 2
    wide = kv_own.shape[-1]
    shard = cond_ref.shape[1] // 8
    first = pl.program_id(0) == 0

    @pl.when(first)
    def _():
        for source, target in (
            (e1_ref, f1_ref), (second_ref, fsecond_ref), (e2_ref, f2_ref), (cond_ref, fcond_ref)
        ):
            target[...] = jnp.transpose(source[...])
        dcond_ref[...] = jnp.zeros_like(dcond_ref)

    from_theirs = pl.program_id(0) // 2 != place_ref[2]
    mixed = jnp.concatenate(
        [jnp.where(from_theirs, b[...], a[...]) for a, b in zip(mine_refs, theirs_refs)], axis=1
    )
    for part, (first_out, out, kv) in enumerate(
        ((aown_ref, bown_ref, kv_own), (aother_ref, bother_ref, kv_other))
    ):
        cut = slice(part * half, (part + 1) * half)
        first_out[0, 0, :, 0:wide] = dot(f1_ref[cut, :], mixed).astype(BF)
        first_out[0, 0, :, wide : 2 * wide] = dot(fsecond_ref[cut, :], dquery_ref[...]).astype(BF)
        out[0, 0, :, wide : 2 * wide] = dot(f2_ref[cut, :], mixed_ref[...]).astype(BF)
        weights = []
        for kind, grads in ((0, dkey_ref), (1, dvalue_ref)):
            at = part * 4 * shard
            both = dot(fcond_ref[at : at + 4 * shard, :], grads[...]).astype(BF)
            for z in range(4):
                low = (2 * z + kind) * shard
                out[0, 0, low : low + shard, 0:wide] = both[z * shard : (z + 1) * shard]
            weight = kv[:, 0, 0, 0, kind * shard : (kind + 1) * shard, :]
            weights.append(weight.reshape(4 * shard, wide))
        dcond_ref[:, part * 4 * shard : (part + 1) * 4 * shard] += dot(
            dkey_ref[...], weights[0], NT
        ) + dot(dvalue_ref[...], weights[1], NT)


def middle_weights(
    place, e1, mine, theirs, second, dquery, cond, dkey, dvalue, e2, mixed, square, after=()
):
    zs, _, _, _, square_shard, wide = square.shape
    rows, width = e1.shape
    slots = cond.shape[0]
    full = whole(e1.shape)
    block = pl.BlockSpec((rows, wide), lambda p, s: (0, p))
    pairs = [
        pl.BlockSpec((rows, 128), lambda p, s, j=j: (0, 2 * j + p % 2))
        for j in range(mine.shape[1] // 256)
    ]
    cond_block = pl.BlockSpec((slots, wide), lambda p, s: (0, p))
    shape = (zs, 1, 1, 1, square_shard, wide)
    own = pl.BlockSpec(shape, lambda p, s: (0, s[0], p % 2, p // 2, 0, 0))
    other = pl.BlockSpec(shape, lambda p, s: (0, 1 - s[0], p % 2, p // 2, 0, 0))
    out = pl.BlockSpec((1, 1, width // 2, 2 * wide), lambda p, s: (p // 2, p % 2, 0, 0))
    out_shape = (2, 2, width // 2, 2 * wide)
    return call(
        functools.partial(middle_weights_kernel, len(pairs)), (4,),
        [(full, e1), (full, second), (block, dquery)]
        + [(whole(cond.shape), cond), (cond_block, dkey), (cond_block, dvalue)]
        + [(full, e2), (block, mixed), (own, square), (other, square)]
        + [(pair, a) for a in (mine, theirs) for pair in pairs],
        [(out, shaped(out_shape, BF))] * 4 + [(whole(cond.shape), shaped(cond.shape, F32))],
        "middle_weights", 22,
        scratch=[pltpu.VMEM((width, rows), BF)] * 3 + [pltpu.VMEM((cond.shape[1], slots), BF)],
        after=after,
        scalars=place,
    )


def fold_kernel(place_ref, keep_ref, got_keep_ref, send_ref, got_send_ref, keep_out, send_out):
    send_out[...] = (send_ref[...].astype(F32) + got_send_ref[...].astype(F32)).astype(BF)
    keep_out[...] = (keep_ref[...].astype(F32) + got_keep_ref[...].astype(F32)).astype(BF)


def fold(place, bit, here, got, at):
    shape = here.shape
    before, after = math.prod(shape[:at]), math.prod(shape[at + 1 : -2])
    view = (before, 2, after) + shape[-2:]
    block = (1, 1, 1) + shape[-2:]
    keep = pl.BlockSpec(block, lambda a, b, s: (a, s[bit], b, 0, 0))
    send = pl.BlockSpec(block, lambda a, b, s: (a, 1 - s[bit], b, 0, 0))
    out = pl.BlockSpec(block, lambda a, b, s: (a, 0, b, 0, 0))
    out_shape = shaped((before, 1, after) + shape[-2:], BF)
    here, got = here.reshape(view), got.reshape(view)
    results = call(
        fold_kernel, (before, after),
        [(keep, here), (keep, got), (send, here), (send, got)],
        [(out, out_shape)] * 2,
        "fold", here.size * 1.3e-6, scalars=place,
    )
    left = shape[:at] + (1,) + shape[at + 1 :]
    return [array.reshape(left) for array in results]


def finish_ffn_kernel(weight_ref, gain_ref, *refs):
    *sources, gu_ref, down_ref, norm_ref = refs
    chunks = len(sources) // 2
    tiles = sources[0].shape[1] // (3 * TILE)
    hidden = chunks * tiles * TILE
    total = jnp.zeros((gain_ref.shape[0], 1), F32)
    for i in range(chunks):
        keep, got = sources[2 * i], sources[2 * i + 1]
        for j in range(tiles):
            at = 3 * j * TILE
            target = (i * tiles + j) * TILE
            grads = keep[:, at : at + 3 * TILE].astype(F32) + got[:, at : at + 3 * TILE].astype(F32)
            for kind in range(2):
                cut = slice(kind * hidden + target, kind * hidden + target + TILE)
                part = grads[:, kind * TILE : (kind + 1) * TILE]
                gu_ref[:, cut] = part
                total += jnp.sum(part * weight_ref[:, cut].astype(F32), axis=1, keepdims=True)
            down_ref[target : target + TILE, :] = jnp.transpose(grads[:, 2 * TILE :])
    norm_ref[...] = total / gain_ref[...]


def finish_ffn(weight, gain, sources):
    shard, wide = weight.shape
    return call(
        finish_ffn_kernel, (1,),
        [(whole(weight.shape), weight), (whole(gain.shape), gain)]
        + [(whole(a.shape), a) for a in sources],
        [
            (whole(weight.shape), shaped(weight.shape, F32)),
            (whole((wide // 2, shard)), shaped((wide // 2, shard), F32)),
            (whole(gain.shape), shaped(gain.shape, F32)),
        ],
        "finish_ffn", 5,
    )


def scatter_kernel(
    queries, dx_ref, their_dx_ref, gain_ref, qkv_weight, query_weight, third_ref,
    x2_ref, y_ref, y_got_ref, turn_ref, rows_ref, gains_ref, dx1_ref, *refs,
):
    inputs, refs = refs[: 4 + 2 * queries], refs[4 + 2 * queries :]
    outs, refs = refs[:8], refs[8:]
    block_ref, dinput_ref, out_ref, cq_ref, ckv_ref, co_ref, qkv_ref, norm_ref = outs
    dx_slot, norm_slot, refs = refs[0], refs[1], refs[2:]
    works, slots, refs = refs[: 2 + queries], refs[2 + queries : 5 * (2 + queries)], refs[5 * (2 + queries) :]
    sends, receives, local_sems = refs
    dp, seq, side = (lax.axis_index(name) for name in ("dp", "seq", "half"))
    here = {"z2": dp // 4, "z1": (dp // 2) % 2, "c": dp % 2, "y": seq, "x": side}
    partners = {
        "z2": (dp + 4 - 8 * (dp // 4), seq, side),
        "z1": (dp + 2 - 4 * ((dp // 2) % 2), seq, side),
        "c": (dp + 1 - 2 * (dp % 2), seq, side),
        "y": (dp, 1 - seq, side),
        "x": (dp, seq, 1 - side),
    }
    barrier = pltpu.get_barrier_semaphore()
    for axis in AXES:
        pl.semaphore_signal(
            barrier, inc=1, device_id=partners[axis], device_id_type=pl.DeviceIdType.MESH
        )
    pl.semaphore_wait(barrier, len(AXES))
    count = [0, 0]

    def send(source, target, axis):
        copy = pltpu.make_async_remote_copy(
            source, target, sends.at[count[0]], receives.at[count[0]],
            device_id=partners[axis], device_id_type=pl.DeviceIdType.MESH,
        )
        count[0] += 1
        copy.start()
        return copy

    def load(source, target):
        copy = pltpu.make_async_copy(source, target, local_sems.at[count[1]])
        count[1] += 1
        copy.start()
        return copy

    def add(target, source):
        target[...] = (target[...].astype(F32) + source[...].astype(F32)).astype(BF)

    dx_copy = send(their_dx_ref, dx_slot, "x")
    names = ["A", "B"] + ["Q%d" % i for i in range(queries)]
    work = dict(zip(names, works))
    slot = {name: slots[4 * i : 4 * i + 4] for i, name in enumerate(names)}
    first = dict.fromkeys(names, "y")
    first["B"] = "x"
    flying = {}
    for i in range(queries):
        own, other = inputs[4 + 2 * i], inputs[5 + 2 * i]
        name = "Q%d" % i
        flying[name] = [load(own, work[name]), send(other, slot[name][0], "c")]
    for i, name in enumerate("AB"):
        flying[name] = [load(inputs[2 * i], work[name]), load(inputs[2 * i + 1], slot[name][0])]

    def part(name, step):
        ref, mine = work[name], here[first[name]]
        if step == 0:
            return ref.at[mine], ref.at[1 - mine]
        if step == 1:
            return ref.at[mine, :, here["z1"]], ref.at[mine, :, 1 - here["z1"]]
        return ref.at[mine, here["z2"], here["z1"]], ref.at[mine, 1 - here["z2"], here["z1"]]

    def advance(name, step):
        for copy in flying[name]:
            copy.wait()
        keep = work[name] if step == 0 else part(name, step - 1)[0]
        add(keep, slot[name][step])
        axis = (first[name], "z1", "z2")[step]
        flying[name] = [send(part(name, step)[1], slot[name][step + 1], axis)]

    def end(name):
        for copy in flying[name]:
            copy.wait()
        return part(name, 2)[0][...].astype(F32) + slot[name][3][...].astype(F32)

    odd = here["c"] == 1
    for name in ("A", "B") + tuple(names[2:]):
        advance(name, 0)
    total = x2_ref[...] + (y_ref[...].astype(F32) + y_got_ref[...].astype(F32))
    block_ref[...] = put_back(total.astype(BF).astype(F32), turn_ref[...], odd, 1).astype(BF)
    advance("A", 1)
    dx_copy.wait()
    normal, scale = normalize(rows_ref[...].astype(F32))
    grads = dx_ref[...].astype(F32) + dx_slot[...].astype(F32)
    total = dx1_ref[...] + normalize_back(grads, gains_ref[0:1, :], normal, scale)
    dinput_ref[...] = put_back(total, turn_ref[...], odd, 2)
    advance("A", 2)
    advance(names[2], 1)
    advance("B", 1)
    for name in names[3:]:
        advance(name, 1)
    advance(names[2], 2)
    advance("B", 2)
    for name in names[3:]:
        advance(name, 2)

    wide = cq_ref.shape[1]
    grads = end("A")
    out_ref[...] = jnp.transpose(grads[:, :wide])
    cq_ref[...] = grads[:, wide:]
    second = jnp.sum(grads[:, wide:] * query_weight[...].astype(F32), axis=1, keepdims=True)
    grads = end("B")
    ckv_ref[...] = grads[:, :wide]
    co_ref[...] = jnp.transpose(grads[:, wide:])
    total = jnp.zeros(second.shape, F32)
    j = 0
    for name in names[2:]:
        grads = end(name)
        for at in range(0, grads.shape[1], 384):
            for kind in range(3):
                cut = slice(kind * wide + j * 128, kind * wide + (j + 1) * 128)
                piece = grads[:, at + kind * 128 : at + (kind + 1) * 128]
                qkv_ref[:, cut] = piece
                total += jnp.sum(piece * qkv_weight[:, cut].astype(F32), axis=1, keepdims=True)
            j += 1
    lane = iota(norm_ref.shape, 1)
    norm_ref[...] = jnp.where(
        lane == 0,
        total / gain_ref[:, 0:1],
        jnp.where(lane == 1, second / gain_ref[:, 1:2], jnp.where(lane == 2, third_ref[...], 0.0)),
    )
    for at, axis in enumerate(("y", "x")):
        send(norm_ref, norm_slot.at[at], axis).wait()
        norm_ref[...] += norm_slot[at]


def scatter_last(
    dx, their_dx, gain_columns, qkv_weight, query_weight, third, x2, y, y_got, turn, rows, gains,
    dx1, squares, queries,
):
    anywhere, vmem = pl.BlockSpec(memory_space=pl.ANY), pl.BlockSpec(memory_space=pltpu.VMEM)
    shard, wide = query_weight.shape
    shapes = [a.shape for a, _ in squares] + [a.shape for a, _ in queries]
    assert all(shape[:3] == (2, 2, 2) for shape in shapes)
    few = [dx, their_dx, gain_columns, qkv_weight, query_weight, third, x2, y, y_got, turn, rows]
    few += [gains, dx1]
    many = [a for pair in (*squares, *queries) for a in pair]
    outs = [(x2.shape, BF), (x2.shape, F32), ((wide, shard), F32), ((shard, wide), F32)]
    outs += [((shard, wide), F32), ((wide, shard), F32), ((shard, 3 * wide), F32)]
    outs += [((shard, 128), F32)]
    slots = [pltpu.VMEM(shape[at:], BF) for shape in shapes for at in range(4)]
    copies = 1 + 2 + len(queries) * 4 + len(squares) * 3
    return pl.pallas_call(
        functools.partial(scatter_kernel, len(queries)),
        in_specs=[vmem] * len(few) + [anywhere] * len(many),
        out_specs=[vmem] * len(outs),
        out_shape=[shaped(*out) for out in outs],
        scratch_shapes=[pltpu.VMEM(rows.shape, BF), pltpu.VMEM((2, shard, 128), F32)]
        + [pltpu.VMEM(shape, BF) for shape in shapes]
        + slots
        + [
            pltpu.SemaphoreType.DMA((copies,)),
            pltpu.SemaphoreType.DMA((copies,)),
            pltpu.SemaphoreType.DMA((4 + len(queries),)),
        ],
        compiler_params=pltpu.CompilerParams(
            vmem_limit_bytes=VMEM_BYTES, collective_id=1, has_side_effects=True
        ),
        name="scatter_last",
    )(*few, *many)


def swap(array, axis, bit=1):
    return lax.ppermute(array, axis, [(i, i ^ bit) for i in range(lax.axis_size(axis))])


def pair_body(
    block_in,
    cond_tokens,
    cond_count,
    norm1_gain,
    norm2_gain,
    norm3_gain,
    qkv_weight,
    attn_out_weight,
    cross_q_weight,
    cross_kv_weight,
    cross_out_weight,
    gate_up_weight,
    down_weight,
    out_cotangent,
):
    rows, width = block_in.shape
    shard = qkv_weight.shape[0]
    head_cols = attn_out_weight.shape[0]
    hidden_cols = down_weight.shape[0]
    cond_slots, cond_width = cond_tokens.shape[1:]
    cond_shard = cross_kv_weight.shape[0]
    dp = lax.axis_index("dp")
    seq = lax.axis_index("seq")
    side = lax.axis_index("half")
    z_size = lax.axis_size("dp") // 2
    core, z = dp % 2, dp // 2
    odd = core.astype(jnp.int32).reshape(1)
    half = width // 2
    pairs_here = head_cols // 128
    per_chunk = hidden_cols // CHUNKS
    z_bits = []
    bit = z_size // 2
    while bit:
        z_bits.append(bit)
        bit //= 2

    places = {"half": 0, "seq": 1}
    steps = {"half": ("half", 1, 2), "seq": ("seq", 1, 1)}
    for at, bit in enumerate(z_bits):
        name = "z%d" % bit
        places[name] = 2 + at
        steps[name] = ("dp", 2 * bit, 4 + at)
    far, near = "z%d" % z_bits[0], "z%d" % z_bits[-1]

    class Way:
        def __init__(self, own, other, wide, order):
            full = (2 if wide else 1, 2) + (2,) * len(z_bits) + (shard, own.shape[-1])
            self.order = list(order)
            self.here = own.reshape(full)
            self.got = swap(other, "dp", 1).reshape(full)

        def step(self, after=(), late=()):
            step = self.order.pop(0)
            if late:
                self.here = hold(self.here, late)
            axis, bit, which = steps[step]
            self.here, send = fold(place, which, self.here, self.got, places[step])
            if after:
                send = hold(send, after)
            self.got = swap(send, axis, bit)
            return self.here

        def end(self):
            while self.order:
                self.step()
            shape = self.here.shape[-2:]
            return [self.here.reshape(shape), self.got.reshape(shape)]

    qkv_pack = jnp.concatenate(
        [
            qkv_weight[:, :, j * 128 : (j + 1) * 128].reshape(shard, 384)
            for j in range(pairs_here)
        ],
        axis=1,
    )
    square_pack = jnp.concatenate(
        [
            attn_out_weight.T,
            cross_q_weight,
            cross_kv_weight.transpose(1, 0, 2).reshape(shard, head_cols),
            cross_out_weight.T,
        ],
        axis=1,
    )
    gains = jnp.stack([norm1_gain, norm2_gain, norm3_gain]).astype(F32)
    gains = lax.dynamic_update_slice(jnp.zeros((8, width), F32), gains, (0, dp * shard))
    gate_up_flat = gate_up_weight.reshape(shard, 2 * hidden_cols)
    (
        wq, w0, w1, w2, w3, mine_in, theirs_in, top_grads, their_top, gains, first_all,
        first_across, turn, *ffn_pack,
    ) = gather_first(
        qkv_pack, square_pack, gains, block_in, out_cotangent, gate_up_flat, down_weight
    )
    wq = wq.reshape((z_size, 2, 2) + qkv_pack.shape)
    squares = [w.reshape((z_size, 2, 2, 2, shard, head_cols)) for w in (w0, w1, w2, w3)]
    place = jnp.stack([core, seq, side, cond_count[seq], z // 2, z % 2]).astype(jnp.int32)
    ffn_weights = []
    for i in range(CHUNKS):
        gathered = lax.all_gather(ffn_pack[i], ("dp", "seq"))
        ffn_weights.append(gathered.reshape((z_size, 2, 2) + ffn_pack[i].shape))

    along = jnp.arange(rows)
    tables = rot_tables(jnp.concatenate([side * rows + along, (1 - side) * rows + along]))
    query, key, value, mine, theirs, lse = self_forward(place, first_all, wq, tables)
    mixed = swap(theirs, "half")

    my_cond = cond_tokens[seq].reshape(cond_slots, z_size, 2, cond_shard)
    swapped = jnp.where(core == 1, my_cond[:, :, ::-1], my_cond)
    my_cond = swapped.transpose(0, 2, 1, 3).reshape(cond_slots, cond_width)
    my_cond = jnp.pad(my_cond, ((0, SLOTS - cond_slots), (0, 0)))
    (top_across,) = across(top_grads)
    (their_top_across,) = across(their_top)
    cross_key, cross_value = cond_forward(place, my_cond, squares[2])
    x1, second, cross_query, cross_mixed, x2, third = middle_forward(
        place, mine_in, mine, mixed, gains, cross_key, cross_value, squares,
        (top_across, their_top_across),
    )
    their_third = swap(third, "half")
    (third_across,) = across(third)
    (their_third_across,) = across(their_third)
    ffn_weights[0] = hold(ffn_weights[0], (their_third_across, third_across))
    sums, ways, after = (), [], ()
    for i in range(CHUNKS):
        *sums, gown, gother = ffn(
            place,
            (third, their_third),
            (third_across, their_third_across),
            (top_grads, their_top),
            (top_across, their_top_across),
            ffn_weights[i],
            TILE,
            sums,
            after,
        )
        arrived = [way.got for way in ways]
        if arrived:
            gother = hold(gother, arrived)
        ways.append(Way(gown, gother, False, ("seq", near, far)))
        if i < CHUNKS - 1:
            after = tuple(way.step() for way in ways)
    ymine, ytheirs, dmine, dtheirs = sums
    d_received = swap(hold(dtheirs, arrived), "half")

    after = [way.step() for way in ways]
    dx1, e2, dquery, dkey, dvalue, e1, dmine, dtheirs = middle_backward(
        place, dmine, d_received, top_grads, x2, x1, gains,
        cross_query, cross_key, cross_value, squares, after,
    )
    dtheirs = swap(dtheirs, "half")
    y_received = swap(hold(ytheirs, (dx1,)), "half")
    aown, aother, bown, bother, dcond = middle_weights(
        place, e1, mine, mixed, second, dquery, my_cond, dkey, dvalue, e2, cross_mixed, squares[2]
    )
    arrived = [way.got for way in ways] + [dtheirs]
    aother, bother = hold(aother, arrived), hold(bother, arrived)
    dcond = hold(dcond, arrived)
    first_way = Way(aown, aother, True, ("half", "seq", near, far))
    second_way = Way(bown, bother, True, ("seq", "half", near, far))
    qkv_grads = []
    pairs = 2 * pairs_here
    after = [dcond, y_received] + [way.step() for way in ways if way.order]
    running = None
    for first, several in ((0, 2), (2, pairs - 2)):
        gown, gother, *sums = self_backward(
            place, query, key, value, mine, theirs, dmine, dtheirs, lse, tables, first_across,
            wq, first, several, running, first > 0, after,
        )
        full = (2, 2, 2, shard, gown.shape[-1])
        qkv_grads.append((gown.reshape(full), gother.reshape(full)))
        running = sums[0]
        if first == 0:
            arrived = [way.got for way in ways] + [first_way.got, second_way.got]
            running = hold(running, arrived)
            after = [way.step(late=(running,)) for way in ways if way.order]
            after += [first_way.step(late=(running,)), second_way.step(late=(running,))]
    rmine, rtheirs = sums
    rtheirs = hold(rtheirs, (first_way.got, second_way.got, ways[-1].got))
    gain_columns = [g.astype(F32).reshape(shard, 1) for g in (norm1_gain, norm2_gain, norm3_gain)]
    grad_gate_up, grad_down, gain_third = finish_ffn(
        gate_up_flat, gain_columns[2], [array for way in ways for array in way.end()]
    )
    grad_gate_up = grad_gate_up.reshape(shard, 2, hidden_cols)
    (
        block_out, grad_input, grad_out, grad_cq, grad_ckv, grad_co, grad_qkv, gain_grads,
    ) = scatter_last(
        rmine, rtheirs, jnp.concatenate(gain_columns[:2], axis=1),
        qkv_weight.reshape(shard, 3 * head_cols), cross_q_weight, gain_third,
        x2, ymine, y_received, turn, mine_in, gains, dx1,
        [
            tuple(a.reshape((2, 2, 2) + a.shape[-2:]) for a in (way.here, way.got))
            for way in (first_way, second_way)
        ],
        qkv_grads,
    )
    grad_ckv = grad_ckv.reshape(2, cond_shard, head_cols).transpose(1, 0, 2)
    grad_qkv = grad_qkv.reshape(shard, 3, head_cols)

    dcond = dcond[:cond_slots].reshape(cond_slots, 2, z_size, cond_shard)
    dcond = jnp.where(core == 1, dcond[:, ::-1], dcond).transpose(0, 2, 1, 3)
    dcond = dcond.reshape(cond_slots, 2, 2, cond_width // 4)
    cond_keep = lax.dynamic_index_in_dim(dcond, side, 2, keepdims=False)
    cond_send = lax.dynamic_index_in_dim(dcond, 1 - side, 2, keepdims=False)
    dcond = cond_keep + swap(cond_send, "half")
    cond_keep = lax.dynamic_index_in_dim(dcond, seq, 1, keepdims=False)
    cond_send = lax.dynamic_index_in_dim(dcond, 1 - seq, 1, keepdims=False)
    cond_got = swap(cond_send, "seq")
    grad_cond = jnp.stack(
        [jnp.where(seq == 1, cond_got, cond_keep), jnp.where(seq == 1, cond_keep, cond_got)]
    )

    gain_grads = gain_grads[:, :3].T
    return (
        block_out,
        grad_input,
        grad_cond,
        gain_grads[0],
        gain_grads[1],
        gain_grads[2],
        grad_qkv,
        grad_out,
        grad_cq,
        grad_ckv,
        grad_co,
        grad_gate_up,
        grad_down,
    )


def pair_solution(mesh, sequences):
    dp, tensor = mesh.devices.shape
    finer = Mesh(mesh.devices.reshape(dp, sequences, tensor // sequences), ("dp", "seq", "half"))
    every = ("dp", "seq", "half")
    both = ("seq", "half")
    return jax.shard_map(
        pair_body,
        mesh=finer,
        in_specs=(
            P(every, None),
            P("dp", None, None),
            P("dp"),
            P("dp"),
            P("dp"),
            P("dp"),
            P("dp", None, both),
            P(both, "dp"),
            P("dp", both),
            P("dp", None, both),
            P(both, "dp"),
            P("dp", None, both),
            P(both, "dp"),
            P(every, None),
        ),
        out_specs=(
            P(every, None),
            P(every, None),
            P("dp", None, both),
            P("dp"),
            P("dp"),
            P("dp"),
            P("dp", None, both),
            P(both, "dp"),
            P("dp", both),
            P("dp", None, both),
            P(both, "dp"),
            P("dp", None, both),
            P(both, "dp"),
        ),
        check_vma=False,
    )


CHUNKS = 3
FLOPS = 1.15e9
TILE = 256
SLOTS = 256


def solution(mesh):
    dp, tensor = mesh.devices.shape

    def run(*args):
        block_in, cond_tokens, qkv, down = args[0], args[1], args[6], args[12]
        sequences = cond_tokens.shape[0] // dp
        fits = (
            sequences == 2
            and tensor == 4
            and dp == 8
            and qkv.shape[2] % (tensor * 128) == 0
            and (qkv.shape[0] // dp) % 64 == 0
            and down.shape[0] % (tensor * CHUNKS * TILE) == 0
            and qkv.shape[0] == 2 * cond_tokens.shape[2]
            and qkv.shape[2] == qkv.shape[0]
            and cond_tokens.shape[1] <= SLOTS
            and block_in.shape[0] == 1024 * cond_tokens.shape[0]
        )
        if fits:
            return pair_solution(mesh, sequences)(*args)
        return general_solution(mesh)(*args)

    return run
```

```python
import functools
import math

import jax
import jax.numpy as jnp
from jax import lax
from jax.experimental import pallas as pl
from jax.experimental.pallas import tpu as pltpu
from jax.sharding import Mesh
from jax.sharding import PartitionSpec as P

HD = 64


EPSILON = 1e-05
MASKED_SCORE = -1e30
BF = jnp.bfloat16
F32 = jnp.float32
NN = (((1,), (0,)), ((), ()))
NT = (((1,), (1,)), ((), ()))
VMEM_BYTES = 60 << 20
DP, TENSOR = "dp", "tensor"


def layer_norm(values, gain):
    centre = values - jnp.mean(values, axis=-1, keepdims=True)
    spread = jnp.mean(centre * centre, axis=-1, keepdims=True)
    return centre * lax.rsqrt(spread + EPSILON) * gain


def rotate(values, cosine, sine):
    quarter = cosine.shape[-1]
    first_part = values[..., :quarter]
    second_part = values[..., quarter : 2 * quarter]
    rest_part = values[..., 2 * quarter :]
    return jnp.concatenate(
        [
            first_part * cosine - second_part * sine,
            first_part * sine + second_part * cosine,
            rest_part,
        ],
        axis=-1,
    )


def rotate_back(grads, cosine, sine):
    quarter = cosine.shape[-1]
    first_part = grads[..., :quarter]
    second_part = grads[..., quarter : 2 * quarter]
    rest_part = grads[..., 2 * quarter :]
    return jnp.concatenate(
        [
            first_part * cosine + second_part * sine,
            second_part * cosine - first_part * sine,
            rest_part,
        ],
        axis=-1,
    )


def gated(gate_vals, up_vals):
    return jax.nn.silu(gate_vals) * up_vals


def rows_by_rows(left, right):
    return lax.dot_general(
        left, right, (((0,), (0,)), ((), ())), preferred_element_type=jnp.float32
    )


def times_transposed(left, right):
    return lax.dot_general(
        left, right, (((1,), (1,)), ((), ())), preferred_element_type=jnp.float32
    )


def attend_forward(query_rows, key_rows, value_rows, allowed):
    scores = jnp.einsum("qhd,khd->hqk", query_rows, key_rows, preferred_element_type=jnp.float32)
    scores = jnp.where(allowed[None, None, :], scores, MASKED_SCORE)
    top_score = jnp.max(scores, axis=-1, keepdims=True)
    weights = jnp.exp(scores - top_score)
    totals = jnp.sum(weights, axis=-1, keepdims=True)
    probs = weights / totals
    mixed = jnp.einsum(
        "hqk,khd->qhd", probs.astype(jnp.bfloat16), value_rows, preferred_element_type=jnp.float32
    )
    return (mixed.astype(jnp.bfloat16), top_score + jnp.log(totals))


def attend_backward(query_rows, key_rows, value_rows, allowed, log_total, grad_mixed):
    scores = jnp.einsum("qhd,khd->hqk", query_rows, key_rows, preferred_element_type=jnp.float32)
    scores = jnp.where(allowed[None, None, :], scores, MASKED_SCORE)
    probs = jnp.exp(scores - log_total)
    grad_probs = jnp.einsum(
        "qhd,khd->hqk", grad_mixed, value_rows, preferred_element_type=jnp.float32
    )
    grad_values = jnp.einsum(
        "hqk,qhd->khd", probs.astype(jnp.bfloat16), grad_mixed, preferred_element_type=jnp.float32
    )
    grad_scores = probs * (grad_probs - jnp.sum(probs * grad_probs, axis=-1, keepdims=True))
    grad_scores = grad_scores.astype(jnp.bfloat16)
    grad_query = jnp.einsum(
        "hqk,khd->qhd", grad_scores, key_rows, preferred_element_type=jnp.float32
    )
    grad_keys = jnp.einsum(
        "hqk,qhd->khd", grad_scores, query_rows, preferred_element_type=jnp.float32
    )
    return (grad_query, grad_keys, grad_values)


def general_body(
    block_in,
    cond_tokens,
    cond_count,
    norm1_gain,
    norm2_gain,
    norm3_gain,
    qkv_weight,
    attn_out_weight,
    cross_q_weight,
    cross_kv_weight,
    cross_out_weight,
    gate_up_weight,
    down_weight,
    out_cotangent,
):
    local_rows = block_in.shape[0]
    model_width = block_in.shape[1]
    group_rows = local_rows * lax.axis_size(TENSOR)
    seq_here = cond_tokens.shape[0]
    seq_length = group_rows // seq_here
    cond_slots = cond_tokens.shape[1]
    cond_width = cond_tokens.shape[2]
    head_cols = attn_out_weight.shape[0]
    heads_here = head_cols // HD
    hidden_here = down_weight.shape[0]
    gain_one, gain_two, gain_three, w_qkv, w_out, w_cq, w_ckv, w_co, w_gu, w_down = (
        lax.all_gather(norm1_gain, DP, axis=0, tiled=True),
        lax.all_gather(norm2_gain, DP, axis=0, tiled=True),
        lax.all_gather(norm3_gain, DP, axis=0, tiled=True),
        lax.all_gather(qkv_weight, DP, axis=0, tiled=True),
        lax.all_gather(attn_out_weight, DP, axis=1, tiled=True),
        lax.all_gather(cross_q_weight, DP, axis=0, tiled=True),
        lax.all_gather(cross_kv_weight, DP, axis=0, tiled=True),
        lax.all_gather(cross_out_weight, DP, axis=1, tiled=True),
        lax.all_gather(gate_up_weight, DP, axis=0, tiled=True),
        lax.all_gather(down_weight, DP, axis=1, tiled=True),
    )
    quarter = HD // 4
    positions = (jnp.arange(group_rows) % seq_length).astype(jnp.float32)
    inverse = 10000.0 ** (-jnp.arange(quarter).astype(jnp.float32) / quarter)
    angle_grid = positions[:, None] * inverse[None, :]
    cosine = jnp.cos(angle_grid)[:, None, :]
    sine = jnp.sin(angle_grid)[:, None, :]
    every_key = jnp.ones((seq_length,), dtype=jnp.bool_)
    valid_slots = jnp.arange(cond_slots)[None, :] < cond_count[:, None]

    def by_sequence(array):
        return array.reshape((seq_here, seq_length) + array.shape[1:])

    def spread_rows(local_part):
        return lax.all_gather(local_part, TENSOR, axis=0, tiled=True)

    def project_out(mixed_all, weight):
        return lax.psum_scatter(
            jnp.dot(mixed_all, weight, preferred_element_type=jnp.float32),
            TENSOR,
            scatter_dimension=0,
            tiled=True,
        )

    def spread_grads(local_part):
        return lax.all_gather(local_part, TENSOR, axis=0, tiled=True)

    def gather_back(grad_all, weight):
        return lax.psum_scatter(
            times_transposed(grad_all, weight), TENSOR, scatter_dimension=0, tiled=True
        )

    def self_forward(seq_parts):
        return attend_forward(seq_parts[0], seq_parts[1], seq_parts[2], every_key)

    def cross_forward(seq_parts):
        return attend_forward(seq_parts[0], seq_parts[1][:, 0], seq_parts[1][:, 1], seq_parts[2])

    def self_backward(seq_parts):
        return attend_backward(
            seq_parts[0], seq_parts[1], seq_parts[2], every_key, seq_parts[3], seq_parts[4]
        )

    def cross_backward(seq_parts):
        return attend_backward(
            seq_parts[0],
            seq_parts[1][:, 0],
            seq_parts[1][:, 1],
            seq_parts[2],
            seq_parts[3],
            seq_parts[4],
        )

    gain_first = gain_one.astype(jnp.float32)
    gain_second = gain_two.astype(jnp.float32)
    gain_third = gain_three.astype(jnp.float32)
    input_rows = block_in.astype(jnp.float32)
    first_all = spread_rows(layer_norm(input_rows, gain_first).astype(jnp.bfloat16))
    qkv_all = jnp.dot(
        first_all, w_qkv.reshape(model_width, 3 * head_cols), preferred_element_type=jnp.float32
    )
    qkv_all = qkv_all.reshape(group_rows, 3, heads_here, HD)
    query_rot = (rotate(qkv_all[:, 0], cosine, sine) * 0.125).astype(jnp.bfloat16)
    key_rot = rotate(qkv_all[:, 1], cosine, sine).astype(jnp.bfloat16)
    value_rows = qkv_all[:, 2].astype(jnp.bfloat16)
    self_mixed, self_lse = lax.map(
        self_forward, (by_sequence(query_rot), by_sequence(key_rot), by_sequence(value_rows))
    )
    self_flat = self_mixed.reshape(group_rows, head_cols)
    after_self = input_rows + project_out(self_flat, w_out)
    second_all = spread_rows(layer_norm(after_self, gain_second).astype(jnp.bfloat16))
    cross_query = (jnp.dot(second_all, w_cq, preferred_element_type=jnp.float32) * 0.125).astype(
        jnp.bfloat16
    )
    cross_query = cross_query.reshape(group_rows, heads_here, HD)
    cond_flat = cond_tokens.reshape(seq_here * cond_slots, cond_width)
    cross_kv = jnp.dot(
        cond_flat, w_ckv.reshape(cond_width, 2 * head_cols), preferred_element_type=jnp.float32
    )
    cross_kv = cross_kv.astype(jnp.bfloat16).reshape(seq_here, cond_slots, 2, heads_here, HD)
    cross_mixed, cross_lse = lax.map(
        cross_forward, (by_sequence(cross_query), cross_kv, valid_slots)
    )
    cross_flat = cross_mixed.reshape(group_rows, head_cols)
    after_cross = after_self + project_out(cross_flat, w_co)
    third_all = spread_rows(layer_norm(after_cross, gain_third).astype(jnp.bfloat16))
    gate_up = jnp.dot(
        third_all, w_gu.reshape(model_width, 2 * hidden_here), preferred_element_type=jnp.float32
    )
    gate_up = gate_up.reshape(group_rows, 2, hidden_here)
    gate_vals = gate_up[:, 0]
    up_vals = gate_up[:, 1]
    hidden = gated(gate_vals, up_vals).astype(jnp.bfloat16)
    block_out = (after_cross + project_out(hidden, w_down)).astype(jnp.bfloat16)
    gain_one, gain_two, gain_three, w_qkv, w_out, w_cq, w_ckv, w_co, w_gu, w_down = (
        lax.all_gather(norm1_gain, DP, axis=0, tiled=True),
        lax.all_gather(norm2_gain, DP, axis=0, tiled=True),
        lax.all_gather(norm3_gain, DP, axis=0, tiled=True),
        lax.all_gather(qkv_weight, DP, axis=0, tiled=True),
        lax.all_gather(attn_out_weight, DP, axis=1, tiled=True),
        lax.all_gather(cross_q_weight, DP, axis=0, tiled=True),
        lax.all_gather(cross_kv_weight, DP, axis=0, tiled=True),
        lax.all_gather(cross_out_weight, DP, axis=1, tiled=True),
        lax.all_gather(gate_up_weight, DP, axis=0, tiled=True),
        lax.all_gather(down_weight, DP, axis=1, tiled=True),
    )
    gain_first = gain_one.astype(jnp.float32)
    gain_second = gain_two.astype(jnp.float32)
    gain_third = gain_three.astype(jnp.float32)
    grad_top = out_cotangent.astype(jnp.float32)
    third_grads = spread_grads(out_cotangent)
    grad_hidden = times_transposed(third_grads, w_down)
    grad_down = rows_by_rows(hidden, third_grads)
    gated_out, gated_pull = jax.vjp(gated, gate_vals, up_vals)
    grad_gate, grad_up = gated_pull(grad_hidden)
    grad_gate_up = (
        jnp.stack([grad_gate, grad_up], axis=1)
        .astype(jnp.bfloat16)
        .reshape(group_rows, 2 * hidden_here)
    )
    grad_gu_weight = rows_by_rows(third_all, grad_gate_up).reshape(model_width, 2, hidden_here)
    grad_third = gather_back(grad_gate_up, w_gu.reshape(model_width, 2 * hidden_here))
    norm_out, norm_pull = jax.vjp(layer_norm, after_cross, gain_third)
    part_rows, grad_gain_third = norm_pull(grad_third)
    grad_cross_rows = grad_top + part_rows
    second_grads = spread_grads(grad_cross_rows.astype(jnp.bfloat16))
    grad_cross_mixed = times_transposed(second_grads, w_co).astype(jnp.bfloat16)
    grad_co_weight = rows_by_rows(cross_flat, second_grads)
    cross_gq, cross_gk, cross_gv = lax.map(
        cross_backward,
        (
            by_sequence(cross_query),
            cross_kv,
            valid_slots,
            cross_lse,
            by_sequence(grad_cross_mixed.reshape(group_rows, heads_here, HD)),
        ),
    )
    grad_cross_query = (cross_gq * 0.125).astype(jnp.bfloat16).reshape(group_rows, head_cols)
    grad_cross_kv = (
        jnp.stack([cross_gk, cross_gv], axis=2)
        .astype(jnp.bfloat16)
        .reshape(seq_here * cond_slots, 2 * head_cols)
    )
    grad_cq_weight = rows_by_rows(second_all, grad_cross_query)
    grad_ckv_weight = rows_by_rows(cond_flat, grad_cross_kv).reshape(cond_width, 2, head_cols)
    cond_partial = times_transposed(
        grad_cross_kv, w_ckv.reshape(cond_width, 2 * head_cols)
    ).reshape(seq_here, cond_slots, cond_width)
    grad_cond = lax.psum_scatter(cond_partial, TENSOR, scatter_dimension=2, tiled=True)
    grad_second = gather_back(grad_cross_query, w_cq)
    norm_out, norm_pull = jax.vjp(layer_norm, after_self, gain_second)
    part_rows, grad_gain_second = norm_pull(grad_second)
    grad_self_rows = grad_cross_rows + part_rows
    first_grads = spread_grads(grad_self_rows.astype(jnp.bfloat16))
    grad_self_mixed = times_transposed(first_grads, w_out).astype(jnp.bfloat16)
    grad_out_weight = rows_by_rows(self_flat, first_grads)
    self_gq, self_gk, self_gv = lax.map(
        self_backward,
        (
            by_sequence(query_rot),
            by_sequence(key_rot),
            by_sequence(value_rows),
            self_lse,
            by_sequence(grad_self_mixed.reshape(group_rows, heads_here, HD)),
        ),
    )
    grad_query = rotate_back(self_gq.reshape(group_rows, heads_here, HD) * 0.125, cosine, sine)
    grad_keys = rotate_back(self_gk.reshape(group_rows, heads_here, HD), cosine, sine)
    grad_values = self_gv.reshape(group_rows, heads_here, HD)
    grad_qkv_all = (
        jnp.stack([grad_query, grad_keys, grad_values], axis=1)
        .astype(jnp.bfloat16)
        .reshape(group_rows, 3 * head_cols)
    )
    grad_qkv_weight = rows_by_rows(first_all, grad_qkv_all).reshape(model_width, 3, head_cols)
    grad_first = gather_back(grad_qkv_all, w_qkv.reshape(model_width, 3 * head_cols))
    norm_out, norm_pull = jax.vjp(layer_norm, input_rows, gain_first)
    part_rows, grad_gain_first = norm_pull(grad_first)
    grad_input = grad_self_rows + part_rows
    owned = (
        lax.psum_scatter(grad_gain_first, DP, scatter_dimension=0, tiled=True),
        lax.psum_scatter(grad_gain_second, DP, scatter_dimension=0, tiled=True),
        lax.psum_scatter(grad_gain_third, DP, scatter_dimension=0, tiled=True),
        lax.psum_scatter(grad_qkv_weight, DP, scatter_dimension=0, tiled=True),
        lax.psum_scatter(grad_out_weight, DP, scatter_dimension=1, tiled=True),
        lax.psum_scatter(grad_cq_weight, DP, scatter_dimension=0, tiled=True),
        lax.psum_scatter(grad_ckv_weight, DP, scatter_dimension=0, tiled=True),
        lax.psum_scatter(grad_co_weight, DP, scatter_dimension=1, tiled=True),
        lax.psum_scatter(grad_gu_weight, DP, scatter_dimension=0, tiled=True),
        lax.psum_scatter(grad_down, DP, scatter_dimension=1, tiled=True),
    )
    gain_grads = lax.psum((owned[0], owned[1], owned[2]), TENSOR)
    return (
        block_out,
        grad_input,
        grad_cond,
        gain_grads[0],
        gain_grads[1],
        gain_grads[2],
        owned[3],
        owned[4],
        owned[5],
        owned[6],
        owned[7],
        owned[8],
        owned[9],
    )


def general_solution(mesh):
    return jax.shard_map(
        general_body,
        mesh=mesh,
        in_specs=(
            P((DP, TENSOR), None),
            P(DP, None, None),
            P(DP),
            P(DP),
            P(DP),
            P(DP),
            P(DP, None, TENSOR),
            P(TENSOR, DP),
            P(DP, TENSOR),
            P(DP, None, TENSOR),
            P(TENSOR, DP),
            P(DP, None, TENSOR),
            P(TENSOR, DP),
            P((DP, TENSOR), None),
        ),
        out_specs=(
            P((DP, TENSOR), None),
            P((DP, TENSOR), None),
            P(DP, None, TENSOR),
            P(DP),
            P(DP),
            P(DP),
            P(DP, None, TENSOR),
            P(TENSOR, DP),
            P(DP, TENSOR),
            P(DP, None, TENSOR),
            P(TENSOR, DP),
            P(DP, None, TENSOR),
            P(TENSOR, DP),
        ),
        check_vma=False,
    )


def dot(left, right, dims=NN):
    return lax.dot_general(left, right, dims, preferred_element_type=F32)


def iota(shape, axis):
    return lax.broadcasted_iota(jnp.int32, shape, axis)


def whole(shape):
    return pl.BlockSpec(shape, lambda *p: (0,) * len(shape), pipeline_mode=pl.Buffered(1))


def columns_of(rows, first=0):
    return pl.BlockSpec((rows, 128), lambda p, s: (0, first + p))


SCALAR = pl.BlockSpec(memory_space=pltpu.SMEM)


def shaped(shape, dtype):
    return jax.ShapeDtypeStruct(shape, dtype)


def call(kernel, grid, ins, outs, name, micros, scratch=(), after=(), scalars=None):
    lead = 0 if scalars is None else 1

    def without_after(*refs):
        kernel(*refs[: lead + len(ins)], *refs[lead + len(ins) + len(after) :])

    in_specs = [spec for spec, _ in ins] + [pl.BlockSpec(memory_space=pl.ANY)] * len(after)
    out_specs = [spec for spec, _ in outs]
    if lead:
        how = dict(
            grid_spec=pltpu.PrefetchScalarGridSpec(
                num_scalar_prefetch=1, grid=grid, in_specs=in_specs, out_specs=out_specs,
                scratch_shapes=list(scratch),
            )
        )
    else:
        how = dict(
            grid=grid, in_specs=in_specs, out_specs=out_specs, scratch_shapes=list(scratch)
        )
    return pl.pallas_call(
        without_after,
        **how,
        out_shape=[shape for _, shape in outs],
        compiler_params=pltpu.CompilerParams(vmem_limit_bytes=VMEM_BYTES),
        cost_estimate=pl.CostEstimate(
            flops=int(micros * FLOPS), bytes_accessed=0, transcendentals=0
        ),
        name=name,
    )(*([] if scalars is None else [scalars]), *[array for _, array in ins], *after)


def unravel(shard):
    size = 4 * shard
    source, target = iota((size, size), 0), iota((size, size), 1)
    z, core, at = source // (2 * shard), (source // shard) % 2, source % shard
    return jnp.where(core * 2 * shard + z * shard + at == target, 1.0, 0.0).astype(BF)


def put_in_order(values, turn, odd):
    size = turn.shape[0]
    own, other = [], []
    for at in range(0, values.shape[1], size):
        both = dot(values[:, at : at + size], turn)
        even, odds = both[:, : size // 2], both[:, size // 2 :]
        own.append(jnp.where(odd, odds, even))
        other.append(jnp.where(odd, even, odds))
    return jnp.concatenate(own + other, axis=1)


def put_back(values, turn, odd, parts):
    size = turn.shape[0]
    middle = values.shape[1] // 2
    result = []
    for at in range(0, middle, size // 2):
        own = values[:, at : at + size // 2]
        other = values[:, middle + at : middle + at + size // 2]
        both = jnp.concatenate(
            [jnp.where(odd, other, own), jnp.where(odd, own, other)], axis=1
        )
        total = None
        for _ in range(parts):
            term = both.astype(BF)
            moved = dot(term, turn, NT)
            total = moved if total is None else total + moved
            both = both - term.astype(F32)
        result.append(total)
    return jnp.concatenate(result, axis=1)


def hold(array, after):
    anywhere = pl.BlockSpec(memory_space=pl.ANY)
    return pl.pallas_call(
        lambda *refs: None,
        in_specs=[anywhere] * (1 + len(after)),
        out_specs=anywhere,
        out_shape=shaped(array.shape, array.dtype),
        input_output_aliases={0: 0},
        cost_estimate=pl.CostEstimate(flops=0, bytes_accessed=0, transcendentals=0),
        name="hold",
    )(array, *after)


def normalize(values):
    centre = values - jnp.mean(values, axis=-1, keepdims=True)
    scale = lax.rsqrt(jnp.mean(centre * centre, axis=-1, keepdims=True) + EPSILON)
    return centre * scale, scale


def normalize_back(grads, gain, normal, scale):
    inner = grads * gain
    return (
        inner
        - jnp.mean(inner, axis=-1, keepdims=True)
        - normal * jnp.mean(inner * normal, axis=-1, keepdims=True)
    ) * scale


def first_norm(ref, base, gains_ref, out_ref, across_ref):
    step = 256
    for at in range(0, ref.shape[0], step):
        normal, _ = normalize(ref[at : at + step, :].astype(F32))
        out = (normal * gains_ref[0:1, :]).astype(BF)
        out_ref[base + at : base + at + step, :] = out
        across_ref[:, base + at : base + at + step] = jnp.transpose(out)


QKV_CHAINS = (("z2", "y", "z1", "c"), ("z1", "z2", "y", "c"))
SQUARE_CHAINS = (
    ("x", "z1", "y", "z2", "c"),
    ("z2", "y", "x", "z1", "c"),
    ("z2", "z1", "x", "y", "c"),
    ("y", "z2", "z1", "x", "c"),
)
AXES = ("z2", "z1", "c", "y", "x")
STEPS = (
    "S0.0", "S3.0", "g0", "S2.0", "S1.0", "Q1.0", "g1", "tops", "S1.1", "Q0.0", "g2", "norm",
    "S0.1", "S3.1", "Q0.1", "in", "S2.1", "norms", "S1.2", "S0.2", "Q1.1", "pack", "S2.2",
    "S3.2", "Q1.2", "Q1.3", "Q0.2", "Q0.3", "S3.3", "S2.3", "S3.4", "S0.3", "S2.4", "S1.3",
    "S0.4", "S1.4",
)


def gather_kernel(
    qkv_ref, square_ref, gains_ref, rows_ref, tops_ref, gu_ref, down_ref,
    wq_ref, w0_ref, w1_ref, w2_ref, w3_ref,
    mine_ref, theirs_ref, tops_out, gains_out, first_ref, across_ref, turn_ref,
    *rest,
):
    *pack_refs, sum_ref, slot_ref, sends, receives, local_sems = rest
    dp, seq, side = (lax.axis_index(name) for name in ("dp", "seq", "half"))
    here = {"z2": dp // 4, "z1": (dp // 2) % 2, "c": dp % 2, "y": seq, "x": side}
    partners = {
        "z2": (dp + 4 - 8 * (dp // 4), seq, side),
        "z1": (dp + 2 - 4 * ((dp // 2) % 2), seq, side),
        "c": (dp + 1 - 2 * (dp % 2), seq, side),
        "y": (dp, 1 - seq, side),
        "x": (dp, seq, 1 - side),
    }
    barrier = pltpu.get_barrier_semaphore()
    for axis in AXES:
        pl.semaphore_signal(
            barrier, inc=1, device_id=partners[axis], device_id_type=pl.DeviceIdType.MESH
        )
    pl.semaphore_wait(barrier, len(AXES))
    count = [0]

    def send(source, target, axis):
        copy = pltpu.make_async_remote_copy(
            source, target, sends.at[count[0]], receives.at[count[0]],
            device_id=partners[axis], device_id_type=pl.DeviceIdType.MESH,
        )
        count[0] += 1
        copy.start()
        return copy

    chains = {}
    columns = qkv_ref.shape[1]
    cut = columns // 2 // 128 * 128 + 128
    for at, (order, low, high) in enumerate(
        ((QKV_CHAINS[0], 0, cut), (QKV_CHAINS[1], cut, columns))
    ):
        chains["Q%d" % at] = (wq_ref, qkv_ref, low, high, order, AXES[:4])
    wide = square_ref.shape[1] // 4
    for at, (order, ref) in enumerate(zip(SQUARE_CHAINS, (w0_ref, w1_ref, w2_ref, w3_ref))):
        chains["S%d" % at] = (ref, square_ref, at * wide, (at + 1) * wide, order, AXES)

    own_copies = {}

    def region(name, step):
        ref, _, low, high, order, axes = chains[name]
        grown = order[:step]
        index = tuple(slice(None) if axis in grown else here[axis] for axis in axes)
        if name[0] == "Q":
            index += (slice(None), slice(low, high))
        return ref.at[index]

    def begin(name, step):
        _, source, low, high, order, _ = chains[name]
        if step == 0:
            part = source.at[:, slice(low, high)]
            copy = pltpu.make_async_copy(part, region(name, 0), local_sems.at[len(own_copies)])
            copy.start()
            own_copies[name] = copy
            return send(part, region(name, 0), order[0])
        if step == 1:
            own_copies[name].wait()
        return send(region(name, step), region(name, step), order[step])

    flying = {}
    for event in STEPS:
        if event.endswith(".0"):
            flying[event[:2]] = begin(event[:2], 0)
    odd = here["c"] == 1
    turn_ref[...] = unravel(qkv_ref.shape[0])
    turn = turn_ref[...]
    mine_ref[...] = put_in_order(rows_ref[...], turn, odd).astype(BF)
    their_rows = send(mine_ref, theirs_ref, "x")
    sum_ref[...] = gains_ref[...]
    gain_axes = ("c", "z1", "z2")
    gain_copy = send(sum_ref, slot_ref.at[0], gain_axes[0])

    for event in STEPS:
        if event[0] == "g":
            at = int(event[1])
            gain_copy.wait()
            sum_ref[...] += slot_ref[at]
            if at < 2:
                gain_copy = send(sum_ref, slot_ref.at[at + 1], gain_axes[at + 1])
            else:
                gains_out[...] = put_in_order(sum_ref[...].astype(BF), turn, odd)
            continue
        if event == "tops":
            tops_out[...] = put_in_order(tops_ref[...], turn, odd).astype(BF)
            continue
        if event == "pack":
            pack_parts(gu_ref, down_ref, pack_refs)
            continue
        if event == "norm":
            first_norm(mine_ref, 0, gains_out, first_ref, across_ref)
            continue
        if event == "norms":
            first_norm(theirs_ref, theirs_ref.shape[0], gains_out, first_ref, across_ref)
            continue
        if event == "in":
            their_rows.wait()
            continue
        name, step = event.split(".")
        flying[name].wait()
        if int(step) + 1 < len(chains[name][4]):
            flying[name] = begin(name, int(step) + 1)


def pack_parts(gu_ref, down_ref, pack_refs):
    hidden = down_ref.shape[1]
    tiles = hidden // len(pack_refs) // TILE
    for i, pack_ref in enumerate(pack_refs):
        for j in range(tiles):
            at, low = 3 * j * TILE, (i * tiles + j) * TILE
            pack_ref[:, at : at + TILE] = gu_ref[:, low : low + TILE]
            pack_ref[:, at + TILE : at + 2 * TILE] = gu_ref[:, hidden + low : hidden + low + TILE]
            pack_ref[:, at + 2 * TILE : at + 3 * TILE] = down_ref[:, low : low + TILE]


def gather_first(qkv, square, gains, rows, tops, gate_up, down):
    anywhere, vmem = pl.BlockSpec(memory_space=pl.ANY), pl.BlockSpec(memory_space=pltpu.VMEM)
    shard = qkv.shape[0]
    wide = square.shape[1] // 4
    count, width = rows.shape
    copies = 4 * 2 + 5 * 4 + 1 + 3
    return pl.pallas_call(
        gather_kernel,
        in_specs=[anywhere, anywhere] + [vmem] * 5,
        out_specs=[anywhere] * 5 + [vmem] * (7 + CHUNKS),
        out_shape=[shaped((2, 2, 2, 2) + qkv.shape, BF)]
        + [shaped((2, 2, 2, 2, 2, shard, wide), BF)] * 4
        + [shaped(rows.shape, BF)] * 3
        + [shaped(gains.shape, F32), shaped((2 * count, width), BF), shaped((width, 2 * count), BF)]
        + [shaped((4 * shard, 4 * shard), BF)]
        + [shaped((shard, 3 * down.shape[1] // CHUNKS), BF)] * CHUNKS,
        scratch_shapes=[
            pltpu.VMEM(gains.shape, F32),
            pltpu.VMEM((3,) + gains.shape, F32),
            pltpu.SemaphoreType.DMA((copies,)),
            pltpu.SemaphoreType.DMA((copies,)),
            pltpu.SemaphoreType.DMA((6,)),
        ],
        compiler_params=pltpu.CompilerParams(
            vmem_limit_bytes=VMEM_BYTES, collective_id=0, has_side_effects=True
        ),
        name="gather_first",
    )(qkv, square, gains, rows, tops, gate_up, down)


def across_kernel(*refs):
    count = len(refs) // 2
    for source, target in zip(refs[:count], refs[count:]):
        step = 256
        for at in range(0, source.shape[0], step):
            target[:, at : at + step] = jnp.transpose(source[at : at + step, :])


def across(*arrays):
    shape = arrays[0].shape
    flipped = (shape[1], shape[0])
    return call(
        across_kernel, (1,),
        [(whole(shape), array) for array in arrays],
        [(whole(flipped), shaped(flipped, BF))] * len(arrays),
        "across", 3 * len(arrays),
    )


def rot(values, tables):
    cosine, sine_up, sine_down = tables
    return (
        values * cosine
        + pltpu.roll(values, 16, 1) * sine_up
        + pltpu.roll(values, 112, 1) * sine_down
    )


def rot_back(grads, tables):
    cosine, sine_up, sine_down = tables
    return (
        grads * cosine
        - pltpu.roll(grads, 16, 1) * sine_up
        - pltpu.roll(grads, 112, 1) * sine_down
    )


def rot_tables(positions):
    quarter = HD // 4
    feature = jnp.arange(2 * HD) % HD
    inverse = 10000.0 ** (-(feature % quarter).astype(F32) / quarter)
    angle_grid = positions.astype(F32)[:, None] * inverse[None, :]
    cosine, sine = jnp.cos(angle_grid), jnp.sin(angle_grid)
    first, second = (feature < quarter)[None], ((feature // quarter) == 1)[None]
    return (
        jnp.where(first | second, cosine, 1.0),
        jnp.where(second, sine, 0.0),
        jnp.where(first, -sine, 0.0),
    )


def to_rows(picks, columns):
    first = columns.astype(BF)
    rest = columns - first.astype(F32)
    second = rest.astype(BF)
    third = (rest - second.astype(F32)).astype(BF)
    return dot(picks, first, NT) + dot(picks, second, NT) + dot(picks, third, NT)


def self_forward_kernel(
    step, place_ref, rows_ref, own_ref, other_ref, c_ref, su_ref, sd_ref,
    q_ref, k_ref, v_ref, mine_ref, theirs_ref, lse_ref,
):
    count, width = rows_ref.shape
    half = width // 2
    own, other = own_ref[...].reshape(half, 384), other_ref[...].reshape(half, 384)
    qkv = dot(rows_ref[:, :half], own) + dot(rows_ref[:, half:], other)
    tables = (c_ref[...], su_ref[...], sd_ref[...])
    query = (rot(qkv[:, :128], tables) * 0.125).astype(BF)
    key = rot(qkv[:, 128:256], tables).astype(BF)
    value = qkv[:, 256:].astype(BF)
    q_ref[...] = query
    k_ref[...] = key
    v_ref[...] = value
    lane = iota((step, 128), 1)
    picks = jnp.where(iota((8, 128), 0) == iota((8, 128), 1), 1.0, 0.0).astype(BF)
    for at in range(0, count, step):
        part = query[at : at + step]
        mixed, logs = [], []
        for head in range(2):
            here = (lane // HD) == head
            scores = dot(jnp.where(here, part, jnp.zeros_like(part)), key, NT)
            top = jnp.max(scores, axis=1, keepdims=True)
            weights = jnp.exp(scores - top)
            total = jnp.sum(weights, axis=1, keepdims=True)
            mixed.append(dot(weights.astype(BF), value) * (1.0 / total))
            logs.append(top + jnp.log(total))
        out = jnp.where(lane < HD, mixed[0], mixed[1]).astype(BF)
        both = jnp.where(lane == 0, logs[0], jnp.where(lane == 1, logs[1], 0.0))
        lse_ref[0, :, at : at + step] = to_rows(picks, both)
        if at < count // 2:
            mine_ref[at : at + step, :] = out
        else:
            theirs_ref[at - count // 2 : at - count // 2 + step, :] = out


def self_weights(weights, first=0):
    shape = (weights.shape[0], 1, 1, weights.shape[3], 384)
    return [
        (pl.BlockSpec(shape, lambda p, s: (0, s[0], p % 2, 0, first // 2 + p // 2)), weights),
        (pl.BlockSpec(shape, lambda p, s: (0, 1 - s[0], p % 2, 0, first // 2 + p // 2)), weights),
    ]


def self_forward(place, rows, weights, tables, after=()):
    count, width = rows.shape
    wide = weights.shape[2] * weights.shape[4] // 3
    pairs = wide // 128
    return call(
        functools.partial(self_forward_kernel, 512),
        (pairs,),
        [(whole(rows.shape), rows)] + self_weights(weights)
        + [(whole((count, 128)), table) for table in tables],
        [(columns_of(count), shaped((count, wide), BF))] * 3
        + [(columns_of(count // 2), shaped((count // 2, wide), BF))] * 2
        + [(pl.BlockSpec((1, 8, count), lambda p, s: (p, 0, 0)), shaped((pairs, 8, count), F32))],
        "self_forward", 7 * pairs,
        after=after,
        scalars=place,
    )


def self_backward_kernel(
    step, begins, ends, place_ref, q_ref, k_ref, v_ref, mine_ref, theirs_ref, dmine_ref, dtheirs_ref, lse_ref,
    c_ref, su_ref, sd_ref, across_ref, own_ref, other_ref, *rest,
):
    if begins:
        gown_ref, gother_ref, *outs, qkv_ref, sum_ref = rest
    else:
        start_ref, gown_ref, gother_ref, *outs, qkv_ref, sum_ref = rest
    count = q_ref.shape[0]
    query = q_ref[...]
    grads = jnp.concatenate([dmine_ref[...], dtheirs_ref[...]], axis=0)
    mixed = jnp.concatenate([mine_ref[...], theirs_ref[...]], axis=0)
    picks = jnp.where((iota((8, 128), 1) // HD) == iota((8, 128), 0), 1.0, 0.0).astype(BF)
    delta = to_rows(picks, grads.astype(F32) * mixed.astype(F32))
    lane = iota((step, 128), 1)
    row = iota((128, step), 0)
    keys_across = jnp.transpose(k_ref[...].astype(F32)).astype(BF)
    query_across = jnp.zeros((128, count), F32)
    tables = (c_ref[...], su_ref[...], sd_ref[...])
    for at in range(0, count, step):
        here = slice(at, at + step)
        key, value = k_ref[here, :], v_ref[here, :]
        flipped = keys_across[:, here]
        dkeys, dvalues = [], []
        for head in range(2):
            inside = (lane // HD) == head
            scores = dot(jnp.where(inside, key, jnp.zeros_like(key)), query, NT)
            probs = jnp.exp(scores - lse_ref[0, head : head + 1, :])
            dprobs = dot(jnp.where(inside, value, jnp.zeros_like(value)), grads, NT)
            dscores = (probs * (dprobs - delta[head : head + 1, :])).astype(BF)
            dvalues.append(dot(probs.astype(BF), grads))
            dkeys.append(dot(dscores, query))
            picked = jnp.where((row // HD) == head, flipped, jnp.zeros_like(flipped))
            query_across = query_across + dot(picked, dscores)
        dkey = jnp.where(lane < HD, dkeys[0], dkeys[1])
        dvalue = jnp.where(lane < HD, dvalues[0], dvalues[1])
        qkv_ref[here, 128:256] = rot_back(dkey, [t[here] for t in tables]).astype(BF)
        qkv_ref[here, 256:384] = dvalue.astype(BF)
    dquery = jnp.transpose(query_across)
    qkv_ref[:, 0:128] = (rot_back(dquery, tables) * 0.125).astype(BF)

    first = pl.program_id(0) == 0
    last = pl.program_id(0) == pl.num_programs(0) - 1
    half = across_ref.shape[0] // 2
    own, other = own_ref[...].reshape(half, 384), other_ref[...].reshape(half, 384)
    both = qkv_ref[...]
    gown_ref[0] = dot(across_ref[:half, :], both).astype(BF)
    gother_ref[0] = dot(across_ref[half:, :], both).astype(BF)
    back = jnp.concatenate([dot(both, own, NT), dot(both, other, NT)], axis=1)

    @pl.when(first)
    def _():
        sum_ref[...] = back if begins else start_ref[...] + back

    @pl.when(jnp.logical_not(first))
    def _():
        sum_ref[...] += back

    @pl.when(last)
    def _():
        if ends:
            outs[0][...] = sum_ref[: count // 2, :].astype(BF)
            outs[1][...] = sum_ref[count // 2 :, :].astype(BF)
        else:
            outs[0][...] = sum_ref[...]


def self_backward(
    place, query, key, value, mine, theirs, dmine, dtheirs, lse, tables, flipped, weights, first, pairs,
    start, ends, after=(),
):
    count = query.shape[0]
    wide = 128 * pairs
    width = flipped.shape[0]
    out = pl.BlockSpec((1, width // 2, 384), lambda p, s: (p % 2, 0, p // 2))
    out_shape = (2, width // 2, 192 * pairs)
    rows, half = columns_of(count, first), columns_of(count // 2, first)
    half_rows = (count // 2, width)
    all_rows = (count, width)
    if ends:
        sums = [(whole(half_rows), shaped(half_rows, BF))] * 2
    else:
        sums = [(whole(all_rows), shaped(all_rows, F32))]
    starts = [] if start is None else [(whole(all_rows), start)]
    return call(
        functools.partial(self_backward_kernel, 512, start is None, ends),
        (pairs,),
        [(rows, array) for array in (query, key, value)]
        + [(half, array) for array in (mine, theirs, dmine, dtheirs)]
        + [(pl.BlockSpec((1, 8, count), lambda p, s: (first + p, 0, 0)), lse)]
        + [(whole((count, 128)), table) for table in tables]
        + [(whole(flipped.shape), flipped)] + self_weights(weights, first) + starts,
        [(out, shaped(out_shape, BF))] * 2 + sums,
        "self_backward", 13 * pairs,
        scratch=[pltpu.VMEM((count, 384), BF), pltpu.VMEM((count, width), F32)],
        after=after,
        scalars=place,
    )


def ffn_kernel(
    tile, carried, place_ref, mine_ref, theirs_ref, fmine_ref, ftheirs_ref,
    tmine_ref, ttheirs_ref, gmine_ref, gtheirs_ref, *rest,
):
    weight_refs, rest = rest[: len(rest) - 4 * carried - 8], rest[len(rest) - 4 * carried - 8 :]
    starts, rest = rest[: 4 * carried], rest[4 * carried :]
    ymine_ref, ytheirs_ref, dmine_ref, dtheirs_ref, gown_ref, gother_ref, y_ref, d_ref = rest
    rows, width = mine_ref.shape
    half = width // 2
    both = 2 * tile
    first = pl.program_id(0) == 0
    last = pl.program_id(0) == pl.num_programs(0) - 1

    @pl.when(first)
    def _():
        if carried:
            for part in range(2):
                y_ref[part] = starts[part][...].astype(F32)
                d_ref[part] = starts[2 + part][...].astype(F32)
        else:
            y_ref[...] = jnp.zeros_like(y_ref)
            d_ref[...] = jnp.zeros_like(d_ref)

    if len(weight_refs) == 2:
        own, other = (ref[...] for ref in weight_refs)
    else:
        nearer = pl.program_id(0) < pl.num_programs(0) // 2
        own = jnp.where(nearer, weight_refs[0][...], weight_refs[1][...])
        other = jnp.where(nearer, weight_refs[2][...], weight_refs[3][...])
    own, other = own.reshape(half, 3 * tile), other.reshape(half, 3 * tile)
    hidden_parts, dgate_up_parts = [], []
    for part, (ref, top_ref) in enumerate(((mine_ref, tmine_ref), (theirs_ref, ttheirs_ref))):
        gate_up = dot(ref[:, :half], own[:, :both]) + dot(ref[:, half:], other[:, :both])
        dhidden = dot(top_ref[:, :half], own[:, both:]) + dot(top_ref[:, half:], other[:, both:])
        gate, up = gate_up[:, :tile], gate_up[:, tile:]
        sigma = 1.0 / (1.0 + jnp.exp(-gate))
        silu = gate * sigma
        hidden = (silu * up).astype(BF)
        dup = (dhidden * silu).astype(BF)
        dgate = (dhidden * up * (sigma * (1.0 + gate * (1.0 - sigma)))).astype(BF)
        dgate_up = jnp.concatenate([dgate, dup], axis=1)
        y_ref[part, :, :half] += dot(hidden, own[:, both:], NT)
        y_ref[part, :, half:] += dot(hidden, other[:, both:], NT)
        d_ref[part, :, :half] += dot(dgate_up, own[:, :both], NT)
        d_ref[part, :, half:] += dot(dgate_up, other[:, :both], NT)
        hidden_parts.append(hidden)
        dgate_up_parts.append(dgate_up)
    for out, cut in ((gown_ref, slice(0, half)), (gother_ref, slice(half, width))):
        out[0, :, :both] = (
            dot(fmine_ref[cut, :], dgate_up_parts[0]) + dot(ftheirs_ref[cut, :], dgate_up_parts[1])
        ).astype(BF)
        out[0, :, both:] = (
            dot(gmine_ref[cut, :], hidden_parts[0]) + dot(gtheirs_ref[cut, :], hidden_parts[1])
        ).astype(BF)

    @pl.when(last)
    def _():
        ymine_ref[...] = y_ref[0].astype(BF)
        ytheirs_ref[...] = y_ref[1].astype(BF)
        dmine_ref[...] = d_ref[0].astype(BF)
        dtheirs_ref[...] = d_ref[1].astype(BF)


def ffn(place, rows, flipped, tops, tops_flipped, weights, tile, starts=(), after=()):
    count, width = rows[0].shape
    several = isinstance(weights, list)
    zs, shard, wide = weights[0].shape if several else (weights.shape[:1] + weights.shape[3:])
    half = zs * shard
    tiles = wide // (3 * tile)
    groups = 2
    if several:
        near = pl.BlockSpec((zs, shard, 3 * tile), lambda p, s: (0, 0, jnp.minimum(p, tiles - 1)))
        far = pl.BlockSpec((zs, shard, 3 * tile), lambda p, s: (0, 0, jnp.maximum(p - tiles, 0)))
        matrices = list(zip((near, far, near, far), weights))
    else:
        shape = (zs, 1, 1, shard, 3 * tile)
        own = pl.BlockSpec(shape, lambda p, s: (0, s[0], p // tiles, 0, p % tiles))
        other = pl.BlockSpec(shape, lambda p, s: (0, 1 - s[0], p // tiles, 0, p % tiles))
        matrices = [(own, weights), (other, weights)]
    block = pl.BlockSpec((1, half, 3 * tile), lambda p, s: (p // tiles, 0, p % tiles))
    out = shaped((groups, half, wide), BF)
    once, fixed = whole((count, width)), whole((width, count))
    return call(
        functools.partial(ffn_kernel, tile, len(starts) // 4),
        (groups * tiles,),
        [(once, a) for a in rows] + [(fixed, a) for a in flipped]
        + [(once, a) for a in tops] + [(fixed, a) for a in tops_flipped]
        + matrices + [(once, a) for a in starts],
        [(once, shaped((count, width), BF))] * 4 + [(block, out)] * 2,
        "feed_forward", 9 * groups * tiles,
        scratch=[pltpu.VMEM((2, count, width), F32)] * 2,
        after=after,
        scalars=place,
    )


def section(square, other):
    zs, _, ys, xs, shard, wide = square.shape
    return (
        pl.BlockSpec(
            (zs, 1, ys, xs, shard, wide),
            lambda *a: (0, 1 - a[-1][0] if other else a[-1][0], 0, 0, 0, 0),
            pipeline_mode=pl.Buffered(1),
        ),
        square,
    )


def sections(squares):
    return [section(squares[n], other) for n in (0, 1, 3) for other in (False, True)]


def weight_of(ref, x, y):
    zs, _, _, _, shard, wide = ref.shape
    return ref[:, 0, y, x].reshape(zs * shard, wide)


def cond_kernel(place_ref, cond_ref, own_ref, other_ref, key_ref, value_ref):
    shard = cond_ref.shape[1] // 8
    half = 4 * shard
    wide = own_ref.shape[-1]
    for x in range(2):
        for y in range(2):
            at = (2 * x + y) * wide
            for kind, out in ((0, key_ref), (1, value_ref)):
                total = None
                for part, ref in ((0, own_ref), (1, other_ref)):
                    weight = ref[:, 0, y, x, kind * shard : (kind + 1) * shard, :]
                    weight = weight.reshape(half, wide)
                    term = dot(cond_ref[:, part * half : (part + 1) * half], weight)
                    total = term if total is None else total + term
                out[:, at : at + wide] = total.astype(BF)


def cond_forward(place, cond, square):
    slots, width = cond.shape
    wide = 4 * square.shape[-1]
    return call(
        cond_kernel, (1,),
        [(whole(cond.shape), cond), section(square, False), section(square, True)],
        [(whole((slots, wide)), shaped((slots, wide), BF))] * 2,
        "cond_forward", 6,
        scalars=place,
    )


def beside(ref, y):
    return jnp.concatenate(
        [ref[:, at : at + 128] for at in range(y * 128, ref.shape[1], 256)], axis=1
    )


def middle_forward_kernel(
    place_ref, rows_ref, mine_ref, theirs_ref, gains_ref, key_ref, value_ref,
    out_own, out_other, cq_own, cq_other, co_own, co_other,
    x1_ref, second_ref, query_ref, mixed_ref, x2_ref, third_ref,
):
    rows, width = rows_ref.shape
    half = width // 2
    wide = out_own.shape[-1]
    slots = key_ref.shape[0]
    valid = iota((rows, slots), 1) < place_ref[3]
    lane = iota((rows, 128), 1)
    for out, cut in ((out_own, 0), (out_other, half)):
        total = rows_ref[:, cut : cut + half].astype(F32)
        for x in range(2):
            for y in range(2):
                mixed = jnp.where(
                    place_ref[2] == x, beside(mine_ref, y), beside(theirs_ref, y)
                )
                total += dot(mixed, weight_of(out, x, y), NT)
        x1_ref[:, cut : cut + half] = total
    normal, _ = normalize(x1_ref[...])
    second = (normal * gains_ref[1:2, :]).astype(BF)
    second_ref[...] = second
    for x in range(2):
        for y in range(2):
            at = (2 * x + y) * wide
            query = dot(second[:, :half], weight_of(cq_own, x, y)) + dot(
                second[:, half:], weight_of(cq_other, x, y)
            )
            query_ref[:, at : at + wide] = (query * 0.125).astype(BF)
    for at in range(0, 4 * wide, 128):
        query, key, value = (
            ref[:, at : at + 128] for ref in (query_ref, key_ref, value_ref)
        )
        mixed = []
        for head in range(2):
            part = jnp.where((lane // HD) == head, query, jnp.zeros_like(query))
            scores = jnp.where(valid, dot(part, key, NT), MASKED_SCORE)
            top = jnp.max(scores, axis=1, keepdims=True)
            weights = jnp.exp(scores - top)
            total = jnp.sum(weights, axis=1, keepdims=True)
            mixed.append(dot(weights.astype(BF), value) * (1.0 / total))
        mixed_ref[:, at : at + 128] = jnp.where(lane < HD, mixed[0], mixed[1]).astype(BF)
    for out, cut in ((co_own, 0), (co_other, half)):
        total = x1_ref[:, cut : cut + half]
        for x in range(2):
            for y in range(2):
                at = (2 * x + y) * wide
                total += dot(mixed_ref[:, at : at + wide], weight_of(out, x, y), NT)
        x2_ref[:, cut : cut + half] = total
    normal, _ = normalize(x2_ref[...])
    third_ref[...] = (normal * gains_ref[2:3, :]).astype(BF)


def middle_forward(place, rows, mine, theirs, gains, key, value, squares, after=()):
    full = whole(rows.shape)
    part = whole(mine.shape)
    cond = whole(key.shape)
    return call(
        middle_forward_kernel, (1,),
        [(full, rows), (part, mine), (part, theirs)]
        + [(whole(gains.shape), gains), (cond, key), (cond, value)] + sections(squares),
        [(full, shaped(rows.shape, dtype)) for dtype in (F32, BF, BF, BF, F32, BF)],
        "middle_forward", 26,
        after=after, scalars=place,
    )


def middle_backward_kernel(
    place_ref, d_ref, r_ref, top_ref, x2_ref, x1_ref, gains_ref,
    query_ref, key_ref, value_ref,
    out_own, out_other, cq_own, cq_other, co_own, co_other,
    dx1_ref, e2_ref, dquery_ref, dkey_ref, dvalue_ref, e1_ref, *refs,
):
    dmine_ref, dtheirs_ref, dmixed_ref = refs
    rows, width = x1_ref.shape
    half = width // 2
    wide = out_own.shape[-1]
    slots = key_ref.shape[0]
    grad_third = d_ref[...].astype(F32) + r_ref[...].astype(F32)
    normal, scale = normalize(x2_ref[...])
    dx2 = top_ref[...].astype(F32) + normalize_back(grad_third, gains_ref[2:3, :], normal, scale)
    dx1_ref[...] = dx2
    e2 = dx2.astype(BF)
    e2_ref[...] = e2
    for x in range(2):
        for y in range(2):
            at = (2 * x + y) * wide
            dmixed_ref[:, at : at + wide] = (
                dot(e2[:, :half], weight_of(co_own, x, y))
                + dot(e2[:, half:], weight_of(co_other, x, y))
            ).astype(BF)
    valid = iota((slots, rows), 0) < place_ref[3]
    lane = iota((slots, 128), 1)
    row = iota((128, slots), 0)
    for at in range(0, 4 * wide, 128):
        here = slice(at, at + 128)
        query, key, value, grads = (
            ref[:, here] for ref in (query_ref, key_ref, value_ref, dmixed_ref)
        )
        flipped = jnp.transpose(key.astype(F32)).astype(BF)
        dkeys, dvalues = [], []
        query_across = None
        for head in range(2):
            inside = (lane // HD) == head
            scores = dot(jnp.where(inside, key, jnp.zeros_like(key)), query, NT)
            scores = jnp.where(valid, scores, MASKED_SCORE)
            weights = jnp.exp(scores - jnp.max(scores, axis=0, keepdims=True))
            probs = weights * (1.0 / jnp.sum(weights, axis=0, keepdims=True))
            dprobs = dot(jnp.where(inside, value, jnp.zeros_like(value)), grads, NT)
            shared = jnp.sum(probs * dprobs, axis=0, keepdims=True)
            dscores = (probs * (dprobs - shared)).astype(BF)
            dvalues.append(dot(probs.astype(BF), grads))
            dkeys.append(dot(dscores, query))
            term = dot(jnp.where((row // HD) == head, flipped, jnp.zeros_like(flipped)), dscores)
            query_across = term if query_across is None else query_across + term
        dkey_ref[:, here] = jnp.where(lane < HD, dkeys[0], dkeys[1]).astype(BF)
        dvalue_ref[:, here] = jnp.where(lane < HD, dvalues[0], dvalues[1]).astype(BF)
        dquery_ref[:, here] = (jnp.transpose(query_across) * 0.125).astype(BF)
    parts = []
    for weight in (cq_own, cq_other):
        total = None
        for x in range(2):
            for y in range(2):
                at = (2 * x + y) * wide
                term = dot(dquery_ref[:, at : at + wide], weight_of(weight, x, y), NT)
                total = term if total is None else total + term
        parts.append(total)
    grad_second = jnp.concatenate(parts, axis=1)
    normal, scale = normalize(x1_ref[...])
    dx1 = dx1_ref[...] + normalize_back(grad_second, gains_ref[1:2, :], normal, scale)
    dx1_ref[...] = dx1
    e1 = dx1.astype(BF)
    e1_ref[...] = e1
    for y in range(2):
        first, second = (
            dot(e1[:, :half], weight_of(out_own, x, y))
            + dot(e1[:, half:], weight_of(out_other, x, y))
            for x in range(2)
        )
        low = place_ref[2] == 0
        for out, grads in (
            (dtheirs_ref, jnp.where(low, second, first).astype(BF)),
            (dmine_ref, jnp.where(low, first, second).astype(BF)),
        ):
            for j in range(wide // 128):
                at = (2 * j + y) * 128
                out[:, at : at + 128] = grads[:, j * 128 : (j + 1) * 128]


def middle_backward(
    place, d, r, top, x2, x1, gains, query, key, value, squares, after=()
):
    full = whole(x1.shape)
    rows, width = x1.shape
    part = (rows, width // 2)
    cond = whole(key.shape)
    return call(
        middle_backward_kernel, (1,),
        [(full, array) for array in (d, r, top, x2, x1)]
        + [(whole(gains.shape), gains), (full, query), (cond, key), (cond, value)]
        + sections(squares),
        [(full, shaped(x1.shape, F32)), (full, shaped(x1.shape, BF)), (full, shaped(x1.shape, BF))]
        + [(cond, shaped(key.shape, BF))] * 2
        + [(full, shaped(x1.shape, BF))]
        + [(whole(part), shaped(part, BF))] * 2,
        "middle_backward", 40,
        scratch=[pltpu.VMEM((rows, width), BF)],
        after=after,
        scalars=place,
    )


def middle_weights_kernel(
    pieces, place_ref, e1_ref, second_ref, dquery_ref, cond_ref, dkey_ref, dvalue_ref,
    e2_ref, mixed_ref, kv_own, kv_other, *rest,
):
    mine_refs, theirs_refs = rest[:pieces], rest[pieces : 2 * pieces]
    aown_ref, aother_ref, bown_ref, bother_ref, dcond_ref = rest[2 * pieces : 2 * pieces + 5]
    f1_ref, fsecond_ref, f2_ref, fcond_ref = rest[2 * pieces + 5 :]
    width = e1_ref.shape[1]
    half = width // 2
    wide = kv_own.shape[-1]
    shard = cond_ref.shape[1] // 8
    first = pl.program_id(0) == 0

    @pl.when(first)
    def _():
        for source, target in (
            (e1_ref, f1_ref), (second_ref, fsecond_ref), (e2_ref, f2_ref), (cond_ref, fcond_ref)
        ):
            target[...] = jnp.transpose(source[...])
        dcond_ref[...] = jnp.zeros_like(dcond_ref)

    from_theirs = pl.program_id(0) // 2 != place_ref[2]
    mixed = jnp.concatenate(
        [jnp.where(from_theirs, b[...], a[...]) for a, b in zip(mine_refs, theirs_refs)], axis=1
    )
    for part, (first_out, out, kv) in enumerate(
        ((aown_ref, bown_ref, kv_own), (aother_ref, bother_ref, kv_other))
    ):
        cut = slice(part * half, (part + 1) * half)
        first_out[0, 0, :, 0:wide] = dot(f1_ref[cut, :], mixed).astype(BF)
        first_out[0, 0, :, wide : 2 * wide] = dot(fsecond_ref[cut, :], dquery_ref[...]).astype(BF)
        out[0, 0, :, wide : 2 * wide] = dot(f2_ref[cut, :], mixed_ref[...]).astype(BF)
        weights = []
        for kind, grads in ((0, dkey_ref), (1, dvalue_ref)):
            at = part * 4 * shard
            both = dot(fcond_ref[at : at + 4 * shard, :], grads[...]).astype(BF)
            for z in range(4):
                low = (2 * z + kind) * shard
                out[0, 0, low : low + shard, 0:wide] = both[z * shard : (z + 1) * shard]
            weight = kv[:, 0, 0, 0, kind * shard : (kind + 1) * shard, :]
            weights.append(weight.reshape(4 * shard, wide))
        dcond_ref[:, part * 4 * shard : (part + 1) * 4 * shard] += dot(
            dkey_ref[...], weights[0], NT
        ) + dot(dvalue_ref[...], weights[1], NT)


def middle_weights(
    place, e1, mine, theirs, second, dquery, cond, dkey, dvalue, e2, mixed, square, after=()
):
    zs, _, _, _, square_shard, wide = square.shape
    rows, width = e1.shape
    slots = cond.shape[0]
    full = whole(e1.shape)
    block = pl.BlockSpec((rows, wide), lambda p, s: (0, p))
    pairs = [
        pl.BlockSpec((rows, 128), lambda p, s, j=j: (0, 2 * j + p % 2))
        for j in range(mine.shape[1] // 256)
    ]
    cond_block = pl.BlockSpec((slots, wide), lambda p, s: (0, p))
    shape = (zs, 1, 1, 1, square_shard, wide)
    own = pl.BlockSpec(shape, lambda p, s: (0, s[0], p % 2, p // 2, 0, 0))
    other = pl.BlockSpec(shape, lambda p, s: (0, 1 - s[0], p % 2, p // 2, 0, 0))
    out = pl.BlockSpec((1, 1, width // 2, 2 * wide), lambda p, s: (p // 2, p % 2, 0, 0))
    out_shape = (2, 2, width // 2, 2 * wide)
    return call(
        functools.partial(middle_weights_kernel, len(pairs)), (4,),
        [(full, e1), (full, second), (block, dquery)]
        + [(whole(cond.shape), cond), (cond_block, dkey), (cond_block, dvalue)]
        + [(full, e2), (block, mixed), (own, square), (other, square)]
        + [(pair, a) for a in (mine, theirs) for pair in pairs],
        [(out, shaped(out_shape, BF))] * 4 + [(whole(cond.shape), shaped(cond.shape, F32))],
        "middle_weights", 5,
        scratch=[pltpu.VMEM((width, rows), BF)] * 3 + [pltpu.VMEM((cond.shape[1], slots), BF)],
        after=after,
        scalars=place,
    )


def fold_kernel(place_ref, keep_ref, got_keep_ref, send_ref, got_send_ref, keep_out, send_out):
    send_out[...] = (send_ref[...].astype(F32) + got_send_ref[...].astype(F32)).astype(BF)
    keep_out[...] = (keep_ref[...].astype(F32) + got_keep_ref[...].astype(F32)).astype(BF)


def fold(place, bit, here, got, at):
    shape = here.shape
    before, after = math.prod(shape[:at]), math.prod(shape[at + 1 : -2])
    view = (before, 2, after) + shape[-2:]
    block = (1, 1, 1) + shape[-2:]
    keep = pl.BlockSpec(block, lambda a, b, s: (a, s[bit], b, 0, 0))
    send = pl.BlockSpec(block, lambda a, b, s: (a, 1 - s[bit], b, 0, 0))
    out = pl.BlockSpec(block, lambda a, b, s: (a, 0, b, 0, 0))
    out_shape = shaped((before, 1, after) + shape[-2:], BF)
    here, got = here.reshape(view), got.reshape(view)
    results = call(
        fold_kernel, (before, after),
        [(keep, here), (keep, got), (send, here), (send, got)],
        [(out, out_shape)] * 2,
        "fold", here.size * 1.3e-6, scalars=place,
    )
    left = shape[:at] + (1,) + shape[at + 1 :]
    return [array.reshape(left) for array in results]


def finish_ffn(weight_ref, sources, gu_ref, down_ref):
    chunks = len(sources) // 2
    tiles = sources[0].shape[1] // (3 * TILE)
    hidden = chunks * tiles * TILE
    total = jnp.zeros((weight_ref.shape[0], 1), F32)
    for i in range(chunks):
        keep, got = sources[2 * i], sources[2 * i + 1]
        for j in range(tiles):
            at = 3 * j * TILE
            target = (i * tiles + j) * TILE
            grads = keep[:, at : at + 3 * TILE].astype(F32) + got[:, at : at + 3 * TILE].astype(F32)
            for kind in range(2):
                cut = slice(kind * hidden + target, kind * hidden + target + TILE)
                part = grads[:, kind * TILE : (kind + 1) * TILE]
                gu_ref[:, cut] = part
                total += jnp.sum(part * weight_ref[:, cut].astype(F32), axis=1, keepdims=True)
            down_ref[:, target : target + TILE] = grads[:, 2 * TILE :]
    return total


SUM_CHAINS = {
    "A": ("z1", "y", "z2"),
    "B": ("x", "z2", "z1"),
    "Q0": ("z2", "y", "z1"),
    "Q1": ("y", "z1", "z2"),
}
SUM_STEPS = (
    "Q0.0", "Q1.0", "out", "A.1", "B.1", "Q0.1", "Q1.1", "A.2", "Q0.2", "B.2", "in", "Q1.2",
)


def scatter_kernel(
    queries, their_dx_ref, *refs,
):
    few = 12 + 2 * CHUNKS
    sources, refs, fetched = refs[:few], refs[few : len(refs) - few], refs[len(refs) - few :]
    dx_ref, gain_ref, qkv_weight, query_weight, ffn_weight, x2_ref, y_ref = fetched[:7]
    y_got_ref, turn_ref, rows_ref, gains_ref, dx1_ref, *ffn_refs = fetched[7:]
    inputs, refs = refs[: 4 + 2 * queries], refs[4 + 2 * queries :]
    outs, refs = refs[:10], refs[10:]
    block_ref, dinput_ref, out_ref, cq_ref, ckv_ref, co_ref, qkv_ref, norm_ref = outs[:8]
    dx_slot, norm_slot, refs = refs[0], refs[1], refs[2:]
    works, slots, refs = refs[: 2 + queries], refs[2 + queries : 5 * (2 + queries)], refs[5 * (2 + queries) :]
    sends, receives, local_sems = refs
    dp, seq, side = (lax.axis_index(name) for name in ("dp", "seq", "half"))
    here = {"z2": dp // 4, "z1": (dp // 2) % 2, "c": dp % 2, "y": seq, "x": side}
    partners = {
        "z2": (dp + 4 - 8 * (dp // 4), seq, side),
        "z1": (dp + 2 - 4 * ((dp // 2) % 2), seq, side),
        "c": (dp + 1 - 2 * (dp % 2), seq, side),
        "y": (dp, 1 - seq, side),
        "x": (dp, seq, 1 - side),
    }
    barrier = pltpu.get_barrier_semaphore()
    for axis in AXES:
        pl.semaphore_signal(
            barrier, inc=1, device_id=partners[axis], device_id_type=pl.DeviceIdType.MESH
        )
    pl.semaphore_wait(barrier, len(AXES))
    count = [0, 0]

    def send(source, target, axis):
        copy = pltpu.make_async_remote_copy(
            source, target, sends.at[count[0]], receives.at[count[0]],
            device_id=partners[axis], device_id_type=pl.DeviceIdType.MESH,
        )
        count[0] += 1
        copy.start()
        return copy

    def load(source, target):
        copy = pltpu.make_async_copy(source, target, local_sems.at[count[1]])
        count[1] += 1
        copy.start()
        return copy

    def add(target, source):
        target[...] = (target[...].astype(F32) + source[...].astype(F32)).astype(BF)

    names = ["A", "B"] + ["Q%d" % i for i in range(queries)]
    work = dict(zip(names, works))
    slot = {name: slots[4 * i : 4 * i + 4] for i, name in enumerate(names)}
    first = dict.fromkeys(names, "y")
    first["B"] = "x"
    flying = {}
    for i in range(queries):
        own, other = inputs[4 + 2 * i], inputs[5 + 2 * i]
        name = "Q%d" % i
        flying[name] = [load(own, work[name]), send(other, slot[name][0], "c")]
    for i, name in enumerate("AB"):
        flying[name] = [load(inputs[2 * i], work[name]), load(inputs[2 * i + 1], slot[name][0])]

    def part(name, step, goes):
        index = [slice(None)] * 3
        for at, axis in enumerate(SUM_CHAINS[name][: step + 1]):
            place = {"z2": 1, "z1": 2}.get(axis, 0)
            index[place] = 1 - here[axis] if goes and at == step else here[axis]
        return work[name].at[tuple(index)]

    def advance(name, step):
        for copy in flying[name]:
            copy.wait()
        add(work[name] if step == 0 else part(name, step - 1, False), slot[name][step])
        target = slot[name][step + 1]
        flying[name] = [send(part(name, step, True), target, SUM_CHAINS[name][step])]

    def end(name):
        for copy in flying[name]:
            copy.wait()
        return part(name, 2, False)[...].astype(F32) + slot[name][3][...].astype(F32)

    odd = here["c"] == 1
    fetches = [load(source, target) for source, target in zip(sources, fetched)]
    advance("A", 0)
    advance("B", 0)
    dx_copy = send(their_dx_ref, dx_slot, "x")
    for event in SUM_STEPS:
        if event == "out":
            for copy in fetches:
                copy.wait()
            total = x2_ref[...] + (y_ref[...].astype(F32) + y_got_ref[...].astype(F32))
            total = total.astype(BF).astype(F32)
            block_ref[...] = put_back(total, turn_ref[...], odd, 1).astype(BF)
            third = finish_ffn(ffn_weight, ffn_refs, *outs[8:])
        elif event == "in":
            dx_copy.wait()
            normal, scale = normalize(rows_ref[...].astype(F32))
            grads = dx_ref[...].astype(F32) + dx_slot[...].astype(F32)
            total = dx1_ref[...] + normalize_back(grads, gains_ref[0:1, :], normal, scale)
            dinput_ref[...] = put_back(total, turn_ref[...], odd, 2)
        else:
            name, step = event.split(".")
            advance(name, int(step))

    wide = cq_ref.shape[1]
    grads = end("A")
    out_ref[...] = grads[:, :wide]
    cq_ref[...] = grads[:, wide:]
    second = jnp.sum(grads[:, wide:] * query_weight[...].astype(F32), axis=1, keepdims=True)
    grads = end("B")
    ckv_ref[...] = grads[:, :wide]
    co_ref[...] = grads[:, wide:]
    total = jnp.zeros(second.shape, F32)
    j = 0
    for name in names[2:]:
        grads = end(name)
        for at in range(0, grads.shape[1], 384):
            for kind in range(3):
                cut = slice(kind * wide + j * 128, kind * wide + (j + 1) * 128)
                piece = grads[:, at + kind * 128 : at + (kind + 1) * 128]
                qkv_ref[kind, :, j * 128 : (j + 1) * 128] = piece
                total += jnp.sum(piece * qkv_weight[:, cut].astype(F32), axis=1, keepdims=True)
            j += 1
    lane = iota(norm_ref.shape, 1)
    norm_ref[...] = jnp.where(
        lane == 0,
        total / gain_ref[:, 0:1],
        jnp.where(lane == 1, second / gain_ref[:, 1:2], jnp.where(lane == 2, third / gain_ref[:, 2:3], 0.0)),
    )
    for at, axis in enumerate(("y", "x")):
        send(norm_ref, norm_slot.at[at], axis).wait()
        norm_ref[...] += norm_slot[at]


def scatter_last(
    dx, their_dx, gain_columns, qkv_weight, query_weight, ffn_weight, ffn_sums, x2, y, y_got, turn, rows, gains,
    dx1, squares, queries,
):
    anywhere, vmem = pl.BlockSpec(memory_space=pl.ANY), pl.BlockSpec(memory_space=pltpu.VMEM)
    shard, wide = query_weight.shape
    shapes = [a.shape for a, _ in squares] + [a.shape for a, _ in queries]
    assert all(shape[:3] == (2, 2, 2) for shape in shapes)
    few = [dx, gain_columns, qkv_weight, query_weight, ffn_weight, x2, y, y_got, turn, rows]
    few += [gains, dx1, *ffn_sums]
    many = [a for pair in (*squares, *queries) for a in pair]
    outs = [(x2.shape, BF), (x2.shape, F32), ((shard, wide), F32), ((shard, wide), F32)]
    outs += [((shard, wide), F32), ((shard, wide), F32), ((3, shard, wide), F32)]
    outs += [((shard, 128), F32), (ffn_weight.shape, F32), ((shard, ffn_weight.shape[1] // 2), F32)]
    slots = [pltpu.VMEM(shape[at:], BF) for shape in shapes for at in range(4)]
    copies = 1 + 2 + len(queries) * 4 + len(squares) * 3
    return pl.pallas_call(
        functools.partial(scatter_kernel, len(queries)),
        in_specs=[anywhere] * (1 + len(few) + len(many)),
        out_specs=[vmem] * len(outs),
        out_shape=[shaped(*out) for out in outs],
        scratch_shapes=[pltpu.VMEM(rows.shape, BF), pltpu.VMEM((2, shard, 128), F32)]
        + [pltpu.VMEM(shape, BF) for shape in shapes]
        + slots
        + [
            pltpu.SemaphoreType.DMA((copies,)),
            pltpu.SemaphoreType.DMA((copies,)),
            pltpu.SemaphoreType.DMA((4 + len(queries) + len(few),)),
        ]
        + [pltpu.VMEM(a.shape, a.dtype) for a in few],
        compiler_params=pltpu.CompilerParams(
            vmem_limit_bytes=63 << 20, collective_id=1, has_side_effects=True
        ),
        name="scatter_last",
    )(their_dx, *few, *many)


def swap(array, axis, bit=1):
    return lax.ppermute(array, axis, [(i, i ^ bit) for i in range(lax.axis_size(axis))])


def pair_body(
    block_in,
    cond_tokens,
    cond_count,
    norm1_gain,
    norm2_gain,
    norm3_gain,
    qkv_weight,
    attn_out_weight,
    cross_q_weight,
    cross_kv_weight,
    cross_out_weight,
    gate_up_weight,
    down_weight,
    out_cotangent,
):
    rows, width = block_in.shape
    shard = qkv_weight.shape[0]
    head_cols = attn_out_weight.shape[0]
    hidden_cols = down_weight.shape[0]
    cond_slots, cond_width = cond_tokens.shape[1:]
    cond_shard = cross_kv_weight.shape[0]
    dp = lax.axis_index("dp")
    seq = lax.axis_index("seq")
    side = lax.axis_index("half")
    z_size = lax.axis_size("dp") // 2
    core, z = dp % 2, dp // 2
    odd = core.astype(jnp.int32).reshape(1)
    half = width // 2
    pairs_here = head_cols // 128
    per_chunk = hidden_cols // CHUNKS
    z_bits = []
    bit = z_size // 2
    while bit:
        z_bits.append(bit)
        bit //= 2

    qkv_pack = jnp.concatenate(
        [
            qkv_weight[:, :, j * 128 : (j + 1) * 128].reshape(shard, 384)
            for j in range(pairs_here)
        ],
        axis=1,
    )
    square_pack = jnp.concatenate(
        [
            attn_out_weight.T,
            cross_q_weight,
            cross_kv_weight.transpose(1, 0, 2).reshape(shard, head_cols),
            cross_out_weight.T,
        ],
        axis=1,
    )
    gains = jnp.stack([norm1_gain, norm2_gain, norm3_gain]).astype(F32)
    gains = lax.dynamic_update_slice(jnp.zeros((8, width), F32), gains, (0, dp * shard))
    places = {"half": 0, "seq": 1, "own": 1}
    steps = {"half": ("half", 1, 2), "seq": ("seq", 1, 1), "own": ("seq", 1, 6)}
    for at, bit in enumerate(z_bits):
        name = "z%d" % bit
        places[name] = 2 + at
        steps[name] = ("dp", 2 * bit, 4 + at)
    far, near = "z%d" % z_bits[0], "z%d" % z_bits[-1]

    gate_up_flat = gate_up_weight.reshape(shard, 2 * hidden_cols)
    (
        wq, w0, w1, w2, w3, mine_in, theirs_in, top_grads, gains, first_all, first_across, turn,
        *packs,
    ) = gather_first(
        qkv_pack, square_pack, gains, block_in, out_cotangent, gate_up_flat, down_weight.T
    )
    wq = wq.reshape((z_size, 2, 2) + qkv_pack.shape)
    squares = [w.reshape((z_size, 2, 2, 2, shard, head_cols)) for w in (w0, w1, w2, w3)]
    place = jnp.stack([core, seq, side, cond_count[seq], z // 2, z % 2, 0 * z]).astype(jnp.int32)
    their_top = swap(top_grads, "half")
    ffn_weights = []
    for pack in packs[:-1]:
        gathered = lax.all_gather(pack, ("dp", "seq"))
        ffn_weights.append(gathered.reshape((z_size, 2, 2) + pack.shape))

    def over(array, name, after):
        axis, bit, which = steps[name]
        array = hold(array, after)
        got, upper = swap(array, axis, bit), place[which] == 1
        return jnp.stack([jnp.where(upper, got, array), jnp.where(upper, array, got)], axis=-3)

    slab = over(packs[-1], far, (gains,))

    class Way:
        def __init__(self, own, other, wide, order):
            full = (2 if wide else 1, 2) + (2,) * len(z_bits) + (shard, own.shape[-1])
            self.order = list(order)
            self.here = own.reshape(full)
            self.got = swap(other, "dp", 1).reshape(full)

        def step(self, after=(), late=()):
            step = self.order.pop(0)
            if late:
                self.here = hold(self.here, late)
            axis, bit, which = steps[step]
            self.here, send = fold(place, which, self.here, self.got, places[step])
            if after:
                send = hold(send, after)
            self.got = swap(send, axis, bit)
            return self.here

        def end(self):
            while self.order:
                self.step()
            shape = self.here.shape[-2:]
            return [self.here.reshape(shape), self.got.reshape(shape)]

    along = jnp.arange(rows)
    tables = rot_tables(jnp.concatenate([side * rows + along, (1 - side) * rows + along]))
    query, key, value, mine, theirs, lse = self_forward(place, first_all, wq, tables)
    theirs = hold(theirs, (their_top,))
    slab = over(slab, near, (lse,))
    mixed = swap(theirs, "half")

    my_cond = hold(cond_tokens[seq], (theirs,)).reshape(cond_slots, z_size, 2, cond_shard)
    swapped = jnp.where(core == 1, my_cond[:, :, ::-1], my_cond)
    my_cond = swapped.transpose(0, 2, 1, 3).reshape(cond_slots, cond_width)
    my_cond = jnp.pad(my_cond, ((0, SLOTS - cond_slots), (0, 0)))
    top_across, their_top_across = across(hold(top_grads, (theirs,)), their_top)
    cross_key, cross_value = cond_forward(place, my_cond, squares[2])
    x1, second, cross_query, cross_mixed, x2, third = middle_forward(
        place, mine_in, mine, mixed, gains, cross_key, cross_value, squares,
        (top_across, their_top_across),
    )
    slab = slab.reshape((z_size,) + slab.shape[2:])
    their_third = swap(third, "half")
    (third_across,) = across(third)
    (their_third_across,) = across(their_third)
    ffn_weights[0] = hold(ffn_weights[0], (their_third_across, third_across))
    sums, ways, after = (), [], (slab,)
    for i in range(CHUNKS):
        *sums, gown, gother = ffn(
            place,
            (third, their_third),
            (third_across, their_third_across),
            (top_grads, their_top),
            (top_across, their_top_across),
            ffn_weights[i],
            TILE,
            sums,
            after,
        )
        if i == 0:
            slab = hold(slab, (sums[2],))
            far_slab = swap(slab, "seq")
            slabs = [slab, far_slab]
            ffn_weights.append(slabs + [swap(s, "dp", 1) for s in slabs])
        else:
            arrived = [far_slab if i == 1 else ways[0].got]
            gother = hold(gother, arrived)
        ways.append(Way(gown, gother, False, ("own" if i == CHUNKS - 1 else "seq", near, far)))
        if i < CHUNKS - 1:
            after = (ways[i].step(((far_slab, ways[0].got)[i],)),)
    ymine, ytheirs, dmine, dtheirs = sums
    d_received = swap(hold(dtheirs, arrived), "half")

    after = [ways[0].step(), ways[2].step()]
    dx1, e2, dquery, dkey, dvalue, e1, dmine, dtheirs = middle_backward(
        place, dmine, d_received, top_grads, x2, x1, gains,
        cross_query, cross_key, cross_value, squares, after,
    )
    dtheirs = swap(dtheirs, "half")
    y_received = swap(hold(ytheirs, (dx1,)), "half")
    aown, aother, bown, bother, dcond = middle_weights(
        place, e1, mine, mixed, second, dquery, my_cond, dkey, dvalue, e2, cross_mixed, squares[2]
    )
    arrived = [way.got for way in ways] + [dtheirs]
    aother, bother = hold(aother, arrived), hold(bother, arrived)
    first_way = Way(aown, aother, True, ("half", "seq", near, far))
    second_way = Way(bown, bother, True, ("seq", "half", near, far))
    qkv_grads = []
    pairs = 2 * pairs_here
    after = [aother] + [way.step() for way in ways if way.order]
    running = None
    for first, several in ((0, 2), (2, pairs - 2)):
        gown, gother, *sums = self_backward(
            place, query, key, value, mine, theirs, dmine, dtheirs, lse, tables, first_across,
            wq, first, several, running, first > 0, after,
        )
        full = (2, 2, 2, shard, gown.shape[-1])
        qkv_grads.append((gown.reshape(full), gother.reshape(full)))
        running = sums[0]
        if first == 0:
            arrived = [way.got for way in ways] + [first_way.got, second_way.got, y_received]
            running = hold(running, arrived)
            dcond = hold(dcond, (running,))
            after = [way.step(late=(running,)) for way in ways if way.order]
            after += [first_way.step(late=(running,)), second_way.step(late=(running,))]
    rmine, rtheirs = sums
    rtheirs = hold(rtheirs, (first_way.got, second_way.got, ways[-1].got))
    gain_columns = [g.astype(F32).reshape(shard, 1) for g in (norm1_gain, norm2_gain, norm3_gain)]
    (
        block_out, grad_input, grad_out, grad_cq, grad_ckv, grad_co, grad_qkv, gain_grads,
        grad_gate_up, grad_down,
    ) = scatter_last(
        rmine, rtheirs, jnp.concatenate(gain_columns, axis=1),
        qkv_weight.reshape(shard, 3 * head_cols), cross_q_weight,
        gate_up_flat, [array for way in ways for array in way.end()],
        x2, ymine, y_received, turn, mine_in, gains, dx1,
        [
            tuple(a.reshape((2, 2, 2) + a.shape[-2:]) for a in (way.here, way.got))
            for way in (first_way, second_way)
        ],
        qkv_grads,
    )
    grad_ckv = grad_ckv.reshape(2, cond_shard, head_cols).transpose(1, 0, 2)
    grad_qkv = grad_qkv.transpose(1, 0, 2)
    grad_gate_up = grad_gate_up.reshape(shard, 2, hidden_cols)

    dcond = dcond[:cond_slots].reshape(cond_slots, 2, z_size, cond_shard)
    dcond = jnp.where(core == 1, dcond[:, ::-1], dcond).transpose(0, 2, 1, 3)
    dcond = dcond.reshape(cond_slots, 2, 2, cond_width // 4)
    cond_keep = lax.dynamic_index_in_dim(dcond, side, 2, keepdims=False)
    cond_send = lax.dynamic_index_in_dim(dcond, 1 - side, 2, keepdims=False)
    dcond = cond_keep + swap(cond_send, "half")
    cond_keep = lax.dynamic_index_in_dim(dcond, seq, 1, keepdims=False)
    cond_send = lax.dynamic_index_in_dim(dcond, 1 - seq, 1, keepdims=False)
    cond_got = swap(cond_send, "seq")
    grad_cond = jnp.stack(
        [jnp.where(seq == 1, cond_got, cond_keep), jnp.where(seq == 1, cond_keep, cond_got)]
    )

    gain_grads = gain_grads[:, :3].T
    return (
        block_out,
        grad_input,
        grad_cond,
        gain_grads[0],
        gain_grads[1],
        gain_grads[2],
        grad_qkv,
        grad_out.T,
        grad_cq,
        grad_ckv,
        grad_co.T,
        grad_gate_up,
        grad_down.T,
    )


def pair_solution(mesh, sequences):
    dp, tensor = mesh.devices.shape
    finer = Mesh(mesh.devices.reshape(dp, sequences, tensor // sequences), ("dp", "seq", "half"))
    every = ("dp", "seq", "half")
    both = ("seq", "half")
    return jax.shard_map(
        pair_body,
        mesh=finer,
        in_specs=(
            P(every, None),
            P("dp", None, None),
            P("dp"),
            P("dp"),
            P("dp"),
            P("dp"),
            P("dp", None, both),
            P(both, "dp"),
            P("dp", both),
            P("dp", None, both),
            P(both, "dp"),
            P("dp", None, both),
            P(both, "dp"),
            P(every, None),
        ),
        out_specs=(
            P(every, None),
            P(every, None),
            P("dp", None, both),
            P("dp"),
            P("dp"),
            P("dp"),
            P("dp", None, both),
            P(both, "dp"),
            P("dp", both),
            P("dp", None, both),
            P(both, "dp"),
            P("dp", None, both),
            P(both, "dp"),
        ),
        check_vma=False,
    )


CHUNKS = 3
FLOPS = 1.15e9
TILE = 256
SLOTS = 144


def solution(mesh):
    dp, tensor = mesh.devices.shape

    def run(*args):
        block_in, cond_tokens, qkv, down = args[0], args[1], args[6], args[12]
        sequences = cond_tokens.shape[0] // dp
        fits = (
            sequences == 2
            and tensor == 4
            and dp == 8
            and qkv.shape[2] % (tensor * 128) == 0
            and (qkv.shape[0] // dp) % 64 == 0
            and down.shape[0] % (tensor * CHUNKS * TILE) == 0
            and qkv.shape[0] == 2 * cond_tokens.shape[2]
            and qkv.shape[2] == qkv.shape[0]
            and cond_tokens.shape[1] <= SLOTS
            and block_in.shape[0] == 1024 * cond_tokens.shape[0]
        )
        if fits:
            return pair_solution(mesh, sequences)(*args)
        return general_solution(mesh)(*args)

    return run
```

```python
import functools
import math

import jax
import jax.numpy as jnp
from jax import lax
from jax.experimental import pallas as pl
from jax.experimental.pallas import tpu as pltpu
from jax.sharding import Mesh
from jax.sharding import PartitionSpec as P

HD = 64


EPSILON = 1e-05
MASKED_SCORE = -1e30
BF = jnp.bfloat16
F32 = jnp.float32
NN = (((1,), (0,)), ((), ()))
NT = (((1,), (1,)), ((), ()))
VMEM_BYTES = 60 << 20
DP, TENSOR = "dp", "tensor"


def layer_norm(values, gain):
    centre = values - jnp.mean(values, axis=-1, keepdims=True)
    spread = jnp.mean(centre * centre, axis=-1, keepdims=True)
    return centre * lax.rsqrt(spread + EPSILON) * gain


def rotate(values, cosine, sine):
    quarter = cosine.shape[-1]
    first_part = values[..., :quarter]
    second_part = values[..., quarter : 2 * quarter]
    rest_part = values[..., 2 * quarter :]
    return jnp.concatenate(
        [
            first_part * cosine - second_part * sine,
            first_part * sine + second_part * cosine,
            rest_part,
        ],
        axis=-1,
    )


def rotate_back(grads, cosine, sine):
    quarter = cosine.shape[-1]
    first_part = grads[..., :quarter]
    second_part = grads[..., quarter : 2 * quarter]
    rest_part = grads[..., 2 * quarter :]
    return jnp.concatenate(
        [
            first_part * cosine + second_part * sine,
            second_part * cosine - first_part * sine,
            rest_part,
        ],
        axis=-1,
    )


def gated(gate_vals, up_vals):
    return jax.nn.silu(gate_vals) * up_vals


def rows_by_rows(left, right):
    return lax.dot_general(
        left, right, (((0,), (0,)), ((), ())), preferred_element_type=jnp.float32
    )


def times_transposed(left, right):
    return lax.dot_general(
        left, right, (((1,), (1,)), ((), ())), preferred_element_type=jnp.float32
    )


def attend_forward(query_rows, key_rows, value_rows, allowed):
    scores = jnp.einsum("qhd,khd->hqk", query_rows, key_rows, preferred_element_type=jnp.float32)
    scores = jnp.where(allowed[None, None, :], scores, MASKED_SCORE)
    top_score = jnp.max(scores, axis=-1, keepdims=True)
    weights = jnp.exp(scores - top_score)
    totals = jnp.sum(weights, axis=-1, keepdims=True)
    probs = weights / totals
    mixed = jnp.einsum(
        "hqk,khd->qhd", probs.astype(jnp.bfloat16), value_rows, preferred_element_type=jnp.float32
    )
    return (mixed.astype(jnp.bfloat16), top_score + jnp.log(totals))


def attend_backward(query_rows, key_rows, value_rows, allowed, log_total, grad_mixed):
    scores = jnp.einsum("qhd,khd->hqk", query_rows, key_rows, preferred_element_type=jnp.float32)
    scores = jnp.where(allowed[None, None, :], scores, MASKED_SCORE)
    probs = jnp.exp(scores - log_total)
    grad_probs = jnp.einsum(
        "qhd,khd->hqk", grad_mixed, value_rows, preferred_element_type=jnp.float32
    )
    grad_values = jnp.einsum(
        "hqk,qhd->khd", probs.astype(jnp.bfloat16), grad_mixed, preferred_element_type=jnp.float32
    )
    grad_scores = probs * (grad_probs - jnp.sum(probs * grad_probs, axis=-1, keepdims=True))
    grad_scores = grad_scores.astype(jnp.bfloat16)
    grad_query = jnp.einsum(
        "hqk,khd->qhd", grad_scores, key_rows, preferred_element_type=jnp.float32
    )
    grad_keys = jnp.einsum(
        "hqk,qhd->khd", grad_scores, query_rows, preferred_element_type=jnp.float32
    )
    return (grad_query, grad_keys, grad_values)


def general_body(
    block_in,
    cond_tokens,
    cond_count,
    norm1_gain,
    norm2_gain,
    norm3_gain,
    qkv_weight,
    attn_out_weight,
    cross_q_weight,
    cross_kv_weight,
    cross_out_weight,
    gate_up_weight,
    down_weight,
    out_cotangent,
):
    local_rows = block_in.shape[0]
    model_width = block_in.shape[1]
    group_rows = local_rows * lax.axis_size(TENSOR)
    seq_here = cond_tokens.shape[0]
    seq_length = group_rows // seq_here
    cond_slots = cond_tokens.shape[1]
    cond_width = cond_tokens.shape[2]
    head_cols = attn_out_weight.shape[0]
    heads_here = head_cols // HD
    hidden_here = down_weight.shape[0]
    gain_one, gain_two, gain_three, w_qkv, w_out, w_cq, w_ckv, w_co, w_gu, w_down = (
        lax.all_gather(norm1_gain, DP, axis=0, tiled=True),
        lax.all_gather(norm2_gain, DP, axis=0, tiled=True),
        lax.all_gather(norm3_gain, DP, axis=0, tiled=True),
        lax.all_gather(qkv_weight, DP, axis=0, tiled=True),
        lax.all_gather(attn_out_weight, DP, axis=1, tiled=True),
        lax.all_gather(cross_q_weight, DP, axis=0, tiled=True),
        lax.all_gather(cross_kv_weight, DP, axis=0, tiled=True),
        lax.all_gather(cross_out_weight, DP, axis=1, tiled=True),
        lax.all_gather(gate_up_weight, DP, axis=0, tiled=True),
        lax.all_gather(down_weight, DP, axis=1, tiled=True),
    )
    quarter = HD // 4
    positions = (jnp.arange(group_rows) % seq_length).astype(jnp.float32)
    inverse = 10000.0 ** (-jnp.arange(quarter).astype(jnp.float32) / quarter)
    angle_grid = positions[:, None] * inverse[None, :]
    cosine = jnp.cos(angle_grid)[:, None, :]
    sine = jnp.sin(angle_grid)[:, None, :]
    every_key = jnp.ones((seq_length,), dtype=jnp.bool_)
    valid_slots = jnp.arange(cond_slots)[None, :] < cond_count[:, None]

    def by_sequence(array):
        return array.reshape((seq_here, seq_length) + array.shape[1:])

    def spread_rows(local_part):
        return lax.all_gather(local_part, TENSOR, axis=0, tiled=True)

    def project_out(mixed_all, weight):
        return lax.psum_scatter(
            jnp.dot(mixed_all, weight, preferred_element_type=jnp.float32),
            TENSOR,
            scatter_dimension=0,
            tiled=True,
        )

    def spread_grads(local_part):
        return lax.all_gather(local_part, TENSOR, axis=0, tiled=True)

    def gather_back(grad_all, weight):
        return lax.psum_scatter(
            times_transposed(grad_all, weight), TENSOR, scatter_dimension=0, tiled=True
        )

    def self_forward(seq_parts):
        return attend_forward(seq_parts[0], seq_parts[1], seq_parts[2], every_key)

    def cross_forward(seq_parts):
        return attend_forward(seq_parts[0], seq_parts[1][:, 0], seq_parts[1][:, 1], seq_parts[2])

    def self_backward(seq_parts):
        return attend_backward(
            seq_parts[0], seq_parts[1], seq_parts[2], every_key, seq_parts[3], seq_parts[4]
        )

    def cross_backward(seq_parts):
        return attend_backward(
            seq_parts[0],
            seq_parts[1][:, 0],
            seq_parts[1][:, 1],
            seq_parts[2],
            seq_parts[3],
            seq_parts[4],
        )

    gain_first = gain_one.astype(jnp.float32)
    gain_second = gain_two.astype(jnp.float32)
    gain_third = gain_three.astype(jnp.float32)
    input_rows = block_in.astype(jnp.float32)
    first_all = spread_rows(layer_norm(input_rows, gain_first).astype(jnp.bfloat16))
    qkv_all = jnp.dot(
        first_all, w_qkv.reshape(model_width, 3 * head_cols), preferred_element_type=jnp.float32
    )
    qkv_all = qkv_all.reshape(group_rows, 3, heads_here, HD)
    query_rot = (rotate(qkv_all[:, 0], cosine, sine) * 0.125).astype(jnp.bfloat16)
    key_rot = rotate(qkv_all[:, 1], cosine, sine).astype(jnp.bfloat16)
    value_rows = qkv_all[:, 2].astype(jnp.bfloat16)
    self_mixed, self_lse = lax.map(
        self_forward, (by_sequence(query_rot), by_sequence(key_rot), by_sequence(value_rows))
    )
    self_flat = self_mixed.reshape(group_rows, head_cols)
    after_self = input_rows + project_out(self_flat, w_out)
    second_all = spread_rows(layer_norm(after_self, gain_second).astype(jnp.bfloat16))
    cross_query = (jnp.dot(second_all, w_cq, preferred_element_type=jnp.float32) * 0.125).astype(
        jnp.bfloat16
    )
    cross_query = cross_query.reshape(group_rows, heads_here, HD)
    cond_flat = cond_tokens.reshape(seq_here * cond_slots, cond_width)
    cross_kv = jnp.dot(
        cond_flat, w_ckv.reshape(cond_width, 2 * head_cols), preferred_element_type=jnp.float32
    )
    cross_kv = cross_kv.astype(jnp.bfloat16).reshape(seq_here, cond_slots, 2, heads_here, HD)
    cross_mixed, cross_lse = lax.map(
        cross_forward, (by_sequence(cross_query), cross_kv, valid_slots)
    )
    cross_flat = cross_mixed.reshape(group_rows, head_cols)
    after_cross = after_self + project_out(cross_flat, w_co)
    third_all = spread_rows(layer_norm(after_cross, gain_third).astype(jnp.bfloat16))
    gate_up = jnp.dot(
        third_all, w_gu.reshape(model_width, 2 * hidden_here), preferred_element_type=jnp.float32
    )
    gate_up = gate_up.reshape(group_rows, 2, hidden_here)
    gate_vals = gate_up[:, 0]
    up_vals = gate_up[:, 1]
    hidden = gated(gate_vals, up_vals).astype(jnp.bfloat16)
    block_out = (after_cross + project_out(hidden, w_down)).astype(jnp.bfloat16)
    gain_one, gain_two, gain_three, w_qkv, w_out, w_cq, w_ckv, w_co, w_gu, w_down = (
        lax.all_gather(norm1_gain, DP, axis=0, tiled=True),
        lax.all_gather(norm2_gain, DP, axis=0, tiled=True),
        lax.all_gather(norm3_gain, DP, axis=0, tiled=True),
        lax.all_gather(qkv_weight, DP, axis=0, tiled=True),
        lax.all_gather(attn_out_weight, DP, axis=1, tiled=True),
        lax.all_gather(cross_q_weight, DP, axis=0, tiled=True),
        lax.all_gather(cross_kv_weight, DP, axis=0, tiled=True),
        lax.all_gather(cross_out_weight, DP, axis=1, tiled=True),
        lax.all_gather(gate_up_weight, DP, axis=0, tiled=True),
        lax.all_gather(down_weight, DP, axis=1, tiled=True),
    )
    gain_first = gain_one.astype(jnp.float32)
    gain_second = gain_two.astype(jnp.float32)
    gain_third = gain_three.astype(jnp.float32)
    grad_top = out_cotangent.astype(jnp.float32)
    third_grads = spread_grads(out_cotangent)
    grad_hidden = times_transposed(third_grads, w_down)
    grad_down = rows_by_rows(hidden, third_grads)
    gated_out, gated_pull = jax.vjp(gated, gate_vals, up_vals)
    grad_gate, grad_up = gated_pull(grad_hidden)
    grad_gate_up = (
        jnp.stack([grad_gate, grad_up], axis=1)
        .astype(jnp.bfloat16)
        .reshape(group_rows, 2 * hidden_here)
    )
    grad_gu_weight = rows_by_rows(third_all, grad_gate_up).reshape(model_width, 2, hidden_here)
    grad_third = gather_back(grad_gate_up, w_gu.reshape(model_width, 2 * hidden_here))
    norm_out, norm_pull = jax.vjp(layer_norm, after_cross, gain_third)
    part_rows, grad_gain_third = norm_pull(grad_third)
    grad_cross_rows = grad_top + part_rows
    second_grads = spread_grads(grad_cross_rows.astype(jnp.bfloat16))
    grad_cross_mixed = times_transposed(second_grads, w_co).astype(jnp.bfloat16)
    grad_co_weight = rows_by_rows(cross_flat, second_grads)
    cross_gq, cross_gk, cross_gv = lax.map(
        cross_backward,
        (
            by_sequence(cross_query),
            cross_kv,
            valid_slots,
            cross_lse,
            by_sequence(grad_cross_mixed.reshape(group_rows, heads_here, HD)),
        ),
    )
    grad_cross_query = (cross_gq * 0.125).astype(jnp.bfloat16).reshape(group_rows, head_cols)
    grad_cross_kv = (
        jnp.stack([cross_gk, cross_gv], axis=2)
        .astype(jnp.bfloat16)
        .reshape(seq_here * cond_slots, 2 * head_cols)
    )
    grad_cq_weight = rows_by_rows(second_all, grad_cross_query)
    grad_ckv_weight = rows_by_rows(cond_flat, grad_cross_kv).reshape(cond_width, 2, head_cols)
    cond_partial = times_transposed(
        grad_cross_kv, w_ckv.reshape(cond_width, 2 * head_cols)
    ).reshape(seq_here, cond_slots, cond_width)
    grad_cond = lax.psum_scatter(cond_partial, TENSOR, scatter_dimension=2, tiled=True)
    grad_second = gather_back(grad_cross_query, w_cq)
    norm_out, norm_pull = jax.vjp(layer_norm, after_self, gain_second)
    part_rows, grad_gain_second = norm_pull(grad_second)
    grad_self_rows = grad_cross_rows + part_rows
    first_grads = spread_grads(grad_self_rows.astype(jnp.bfloat16))
    grad_self_mixed = times_transposed(first_grads, w_out).astype(jnp.bfloat16)
    grad_out_weight = rows_by_rows(self_flat, first_grads)
    self_gq, self_gk, self_gv = lax.map(
        self_backward,
        (
            by_sequence(query_rot),
            by_sequence(key_rot),
            by_sequence(value_rows),
            self_lse,
            by_sequence(grad_self_mixed.reshape(group_rows, heads_here, HD)),
        ),
    )
    grad_query = rotate_back(self_gq.reshape(group_rows, heads_here, HD) * 0.125, cosine, sine)
    grad_keys = rotate_back(self_gk.reshape(group_rows, heads_here, HD), cosine, sine)
    grad_values = self_gv.reshape(group_rows, heads_here, HD)
    grad_qkv_all = (
        jnp.stack([grad_query, grad_keys, grad_values], axis=1)
        .astype(jnp.bfloat16)
        .reshape(group_rows, 3 * head_cols)
    )
    grad_qkv_weight = rows_by_rows(first_all, grad_qkv_all).reshape(model_width, 3, head_cols)
    grad_first = gather_back(grad_qkv_all, w_qkv.reshape(model_width, 3 * head_cols))
    norm_out, norm_pull = jax.vjp(layer_norm, input_rows, gain_first)
    part_rows, grad_gain_first = norm_pull(grad_first)
    grad_input = grad_self_rows + part_rows
    owned = (
        lax.psum_scatter(grad_gain_first, DP, scatter_dimension=0, tiled=True),
        lax.psum_scatter(grad_gain_second, DP, scatter_dimension=0, tiled=True),
        lax.psum_scatter(grad_gain_third, DP, scatter_dimension=0, tiled=True),
        lax.psum_scatter(grad_qkv_weight, DP, scatter_dimension=0, tiled=True),
        lax.psum_scatter(grad_out_weight, DP, scatter_dimension=1, tiled=True),
        lax.psum_scatter(grad_cq_weight, DP, scatter_dimension=0, tiled=True),
        lax.psum_scatter(grad_ckv_weight, DP, scatter_dimension=0, tiled=True),
        lax.psum_scatter(grad_co_weight, DP, scatter_dimension=1, tiled=True),
        lax.psum_scatter(grad_gu_weight, DP, scatter_dimension=0, tiled=True),
        lax.psum_scatter(grad_down, DP, scatter_dimension=1, tiled=True),
    )
    gain_grads = lax.psum((owned[0], owned[1], owned[2]), TENSOR)
    return (
        block_out,
        grad_input,
        grad_cond,
        gain_grads[0],
        gain_grads[1],
        gain_grads[2],
        owned[3],
        owned[4],
        owned[5],
        owned[6],
        owned[7],
        owned[8],
        owned[9],
    )


def general_solution(mesh):
    return jax.shard_map(
        general_body,
        mesh=mesh,
        in_specs=(
            P((DP, TENSOR), None),
            P(DP, None, None),
            P(DP),
            P(DP),
            P(DP),
            P(DP),
            P(DP, None, TENSOR),
            P(TENSOR, DP),
            P(DP, TENSOR),
            P(DP, None, TENSOR),
            P(TENSOR, DP),
            P(DP, None, TENSOR),
            P(TENSOR, DP),
            P((DP, TENSOR), None),
        ),
        out_specs=(
            P((DP, TENSOR), None),
            P((DP, TENSOR), None),
            P(DP, None, TENSOR),
            P(DP),
            P(DP),
            P(DP),
            P(DP, None, TENSOR),
            P(TENSOR, DP),
            P(DP, TENSOR),
            P(DP, None, TENSOR),
            P(TENSOR, DP),
            P(DP, None, TENSOR),
            P(TENSOR, DP),
        ),
        check_vma=False,
    )


def dot(left, right, dims=NN):
    return lax.dot_general(left, right, dims, preferred_element_type=F32)


def iota(shape, axis):
    return lax.broadcasted_iota(jnp.int32, shape, axis)


def whole(shape):
    return pl.BlockSpec(shape, lambda *p: (0,) * len(shape), pipeline_mode=pl.Buffered(1))


def columns_of(rows, first=0):
    return pl.BlockSpec((rows, 128), lambda p, s: (0, first + p))


SCALAR = pl.BlockSpec(memory_space=pltpu.SMEM)


def shaped(shape, dtype):
    return jax.ShapeDtypeStruct(shape, dtype)


def call(kernel, grid, ins, outs, name, micros, scratch=(), after=(), scalars=None):
    lead = 0 if scalars is None else 1

    def without_after(*refs):
        kernel(*refs[: lead + len(ins)], *refs[lead + len(ins) + len(after) :])

    in_specs = [spec for spec, _ in ins] + [pl.BlockSpec(memory_space=pl.ANY)] * len(after)
    out_specs = [spec for spec, _ in outs]
    if lead:
        how = dict(
            grid_spec=pltpu.PrefetchScalarGridSpec(
                num_scalar_prefetch=1, grid=grid, in_specs=in_specs, out_specs=out_specs,
                scratch_shapes=list(scratch),
            )
        )
    else:
        how = dict(
            grid=grid, in_specs=in_specs, out_specs=out_specs, scratch_shapes=list(scratch)
        )
    return pl.pallas_call(
        without_after,
        **how,
        out_shape=[shape for _, shape in outs],
        compiler_params=pltpu.CompilerParams(vmem_limit_bytes=VMEM_BYTES),
        cost_estimate=pl.CostEstimate(
            flops=int(micros * FLOPS), bytes_accessed=0, transcendentals=0
        ),
        name=name,
    )(*([] if scalars is None else [scalars]), *[array for _, array in ins], *after)


def unravel(shard):
    size = 4 * shard
    source, target = iota((size, size), 0), iota((size, size), 1)
    z, core, at = source // (2 * shard), (source // shard) % 2, source % shard
    return jnp.where(core * 2 * shard + z * shard + at == target, 1.0, 0.0).astype(BF)


def put_in_order(values, turn, odd):
    size = turn.shape[0]
    own, other = [], []
    for at in range(0, values.shape[1], size):
        both = dot(values[:, at : at + size], turn)
        even, odds = both[:, : size // 2], both[:, size // 2 :]
        own.append(jnp.where(odd, odds, even))
        other.append(jnp.where(odd, even, odds))
    return jnp.concatenate(own + other, axis=1)


def put_back(values, turn, odd, parts):
    size = turn.shape[0]
    middle = values.shape[1] // 2
    result = []
    for at in range(0, middle, size // 2):
        own = values[:, at : at + size // 2]
        other = values[:, middle + at : middle + at + size // 2]
        both = jnp.concatenate(
            [jnp.where(odd, other, own), jnp.where(odd, own, other)], axis=1
        )
        total = None
        for _ in range(parts):
            term = both.astype(BF)
            moved = dot(term, turn, NT)
            total = moved if total is None else total + moved
            both = both - term.astype(F32)
        result.append(total)
    return jnp.concatenate(result, axis=1)


def hold(array, after):
    anywhere = pl.BlockSpec(memory_space=pl.ANY)
    return pl.pallas_call(
        lambda *refs: None,
        in_specs=[anywhere] * (1 + len(after)),
        out_specs=anywhere,
        out_shape=shaped(array.shape, array.dtype),
        input_output_aliases={0: 0},
        cost_estimate=pl.CostEstimate(flops=0, bytes_accessed=0, transcendentals=0),
        name="hold",
    )(array, *after)


def normalize(values):
    centre = values - jnp.mean(values, axis=-1, keepdims=True)
    scale = lax.rsqrt(jnp.mean(centre * centre, axis=-1, keepdims=True) + EPSILON)
    return centre * scale, scale


def normalize_back(grads, gain, normal, scale):
    inner = grads * gain
    return (
        inner
        - jnp.mean(inner, axis=-1, keepdims=True)
        - normal * jnp.mean(inner * normal, axis=-1, keepdims=True)
    ) * scale


def first_norm(ref, base, gains_ref, out_ref, across_ref):
    step = 256
    for at in range(0, ref.shape[0], step):
        normal, _ = normalize(ref[at : at + step, :].astype(F32))
        out = (normal * gains_ref[0:1, :]).astype(BF)
        out_ref[base + at : base + at + step, :] = out
        across_ref[:, base + at : base + at + step] = jnp.transpose(out)


QKV_CHAINS = (("z2", "y", "z1", "c"), ("z1", "z2", "y", "c"))
SQUARE_CHAINS = (
    ("x", "z1", "y", "z2", "c"),
    ("z2", "y", "x", "z1", "c"),
    ("z2", "z1", "x", "y", "c"),
    ("y", "z2", "z1", "x", "c"),
)
AXES = ("z2", "z1", "c", "y", "x")
STEPS = (
    "S0.0", "S3.0", "g0", "S2.0", "S1.0", "Q1.0", "g1", "tops", "S1.1", "Q0.0", "g2", "norm",
    "S0.1", "S3.1", "Q0.1", "in", "S2.1", "norms", "S1.2", "S0.2", "Q1.1", "pack", "S2.2",
    "S3.2", "Q1.2", "Q1.3", "Q0.2", "Q0.3", "S3.3", "S2.3", "S3.4", "S0.3", "S2.4", "S1.3",
    "S0.4", "S1.4",
)


def gather_kernel(
    qkv_ref, square_ref, gains_ref, rows_ref, tops_ref, gu_ref, down_ref,
    wq_ref, w0_ref, w1_ref, w2_ref, w3_ref,
    mine_ref, theirs_ref, tops_out, gains_out, first_ref, across_ref, turn_ref,
    *rest,
):
    *pack_refs, sum_ref, slot_ref, sends, receives, local_sems = rest
    dp, seq, side = (lax.axis_index(name) for name in ("dp", "seq", "half"))
    here = {"z2": dp // 4, "z1": (dp // 2) % 2, "c": dp % 2, "y": seq, "x": side}
    partners = {
        "z2": (dp + 4 - 8 * (dp // 4), seq, side),
        "z1": (dp + 2 - 4 * ((dp // 2) % 2), seq, side),
        "c": (dp + 1 - 2 * (dp % 2), seq, side),
        "y": (dp, 1 - seq, side),
        "x": (dp, seq, 1 - side),
    }
    barrier = pltpu.get_barrier_semaphore()
    for axis in AXES:
        pl.semaphore_signal(
            barrier, inc=1, device_id=partners[axis], device_id_type=pl.DeviceIdType.MESH
        )
    pl.semaphore_wait(barrier, len(AXES))
    count = [0]

    def send(source, target, axis):
        copy = pltpu.make_async_remote_copy(
            source, target, sends.at[count[0]], receives.at[count[0]],
            device_id=partners[axis], device_id_type=pl.DeviceIdType.MESH,
        )
        count[0] += 1
        copy.start()
        return copy

    chains = {}
    columns = qkv_ref.shape[1]
    cut = columns // 2 // 128 * 128 + 128
    for at, (order, low, high) in enumerate(
        ((QKV_CHAINS[0], 0, cut), (QKV_CHAINS[1], cut, columns))
    ):
        chains["Q%d" % at] = (wq_ref, qkv_ref, low, high, order, AXES[:4])
    wide = square_ref.shape[1] // 4
    for at, (order, ref) in enumerate(zip(SQUARE_CHAINS, (w0_ref, w1_ref, w2_ref, w3_ref))):
        chains["S%d" % at] = (ref, square_ref, at * wide, (at + 1) * wide, order, AXES)

    own_copies = {}

    def region(name, step):
        ref, _, low, high, order, axes = chains[name]
        grown = order[:step]
        index = tuple(slice(None) if axis in grown else here[axis] for axis in axes)
        if name[0] == "Q":
            index += (slice(None), slice(low, high))
        return ref.at[index]

    def begin(name, step):
        _, source, low, high, order, _ = chains[name]
        if step == 0:
            part = source.at[:, slice(low, high)]
            copy = pltpu.make_async_copy(part, region(name, 0), local_sems.at[len(own_copies)])
            copy.start()
            own_copies[name] = copy
            return send(part, region(name, 0), order[0])
        if step == 1:
            own_copies[name].wait()
        return send(region(name, step), region(name, step), order[step])

    flying = {}
    for event in STEPS:
        if event.endswith(".0"):
            flying[event[:2]] = begin(event[:2], 0)
    odd = here["c"] == 1
    turn_ref[...] = unravel(qkv_ref.shape[0])
    turn = turn_ref[...]
    mine_ref[...] = put_in_order(rows_ref[...], turn, odd).astype(BF)
    their_rows = send(mine_ref, theirs_ref, "x")
    sum_ref[...] = gains_ref[...]
    gain_axes = ("c", "z1", "z2")
    gain_copy = send(sum_ref, slot_ref.at[0], gain_axes[0])

    for event in STEPS:
        if event[0] == "g":
            at = int(event[1])
            gain_copy.wait()
            sum_ref[...] += slot_ref[at]
            if at < 2:
                gain_copy = send(sum_ref, slot_ref.at[at + 1], gain_axes[at + 1])
            else:
                gains_out[...] = put_in_order(sum_ref[...].astype(BF), turn, odd)
            continue
        if event == "tops":
            tops_out[...] = put_in_order(tops_ref[...], turn, odd).astype(BF)
            continue
        if event == "pack":
            pack_parts(gu_ref, down_ref, pack_refs)
            continue
        if event == "norm":
            first_norm(mine_ref, 0, gains_out, first_ref, across_ref)
            continue
        if event == "norms":
            first_norm(theirs_ref, theirs_ref.shape[0], gains_out, first_ref, across_ref)
            continue
        if event == "in":
            their_rows.wait()
            continue
        name, step = event.split(".")
        flying[name].wait()
        if int(step) + 1 < len(chains[name][4]):
            flying[name] = begin(name, int(step) + 1)


def pack_parts(gu_ref, down_ref, pack_refs):
    hidden = down_ref.shape[1]
    tiles = hidden // len(pack_refs) // TILE
    for i, pack_ref in enumerate(pack_refs):
        for j in range(tiles):
            at, low = 3 * j * TILE, (i * tiles + j) * TILE
            pack_ref[:, at : at + TILE] = gu_ref[:, low : low + TILE]
            pack_ref[:, at + TILE : at + 2 * TILE] = gu_ref[:, hidden + low : hidden + low + TILE]
            pack_ref[:, at + 2 * TILE : at + 3 * TILE] = down_ref[:, low : low + TILE]


def gather_first(qkv, square, gains, rows, tops, gate_up, down):
    anywhere, vmem = pl.BlockSpec(memory_space=pl.ANY), pl.BlockSpec(memory_space=pltpu.VMEM)
    shard = qkv.shape[0]
    wide = square.shape[1] // 4
    count, width = rows.shape
    copies = 4 * 2 + 5 * 4 + 1 + 3
    return pl.pallas_call(
        gather_kernel,
        in_specs=[anywhere, anywhere] + [vmem] * 5,
        out_specs=[anywhere] * 5 + [vmem] * (7 + CHUNKS),
        out_shape=[shaped((2, 2, 2, 2) + qkv.shape, BF)]
        + [shaped((2, 2, 2, 2, 2, shard, wide), BF)] * 4
        + [shaped(rows.shape, BF)] * 3
        + [shaped(gains.shape, F32), shaped((2 * count, width), BF), shaped((width, 2 * count), BF)]
        + [shaped((4 * shard, 4 * shard), BF)]
        + [shaped((shard, 3 * down.shape[1] // CHUNKS), BF)] * CHUNKS,
        scratch_shapes=[
            pltpu.VMEM(gains.shape, F32),
            pltpu.VMEM((3,) + gains.shape, F32),
            pltpu.SemaphoreType.DMA((copies,)),
            pltpu.SemaphoreType.DMA((copies,)),
            pltpu.SemaphoreType.DMA((6,)),
        ],
        compiler_params=pltpu.CompilerParams(
            vmem_limit_bytes=VMEM_BYTES, collective_id=0, has_side_effects=True
        ),
        name="gather_first",
    )(qkv, square, gains, rows, tops, gate_up, down)


def across_kernel(*refs):
    count = len(refs) // 2
    for source, target in zip(refs[:count], refs[count:]):
        step = 256
        for at in range(0, source.shape[0], step):
            target[:, at : at + step] = jnp.transpose(source[at : at + step, :])


def across(*arrays):
    shape = arrays[0].shape
    flipped = (shape[1], shape[0])
    return call(
        across_kernel, (1,),
        [(whole(shape), array) for array in arrays],
        [(whole(flipped), shaped(flipped, BF))] * len(arrays),
        "across", 3 * len(arrays),
    )


def rot(values, tables):
    cosine, sine_up, sine_down = tables
    return (
        values * cosine
        + pltpu.roll(values, 16, 1) * sine_up
        + pltpu.roll(values, 112, 1) * sine_down
    )


def rot_back(grads, tables):
    cosine, sine_up, sine_down = tables
    return (
        grads * cosine
        - pltpu.roll(grads, 16, 1) * sine_up
        - pltpu.roll(grads, 112, 1) * sine_down
    )


def rot_tables(positions):
    quarter = HD // 4
    feature = jnp.arange(2 * HD) % HD
    inverse = 10000.0 ** (-(feature % quarter).astype(F32) / quarter)
    angle_grid = positions.astype(F32)[:, None] * inverse[None, :]
    cosine, sine = jnp.cos(angle_grid), jnp.sin(angle_grid)
    first, second = (feature < quarter)[None], ((feature // quarter) == 1)[None]
    return (
        jnp.where(first | second, cosine, 1.0),
        jnp.where(second, sine, 0.0),
        jnp.where(first, -sine, 0.0),
    )


def to_rows(picks, columns):
    first = columns.astype(BF)
    rest = columns - first.astype(F32)
    second = rest.astype(BF)
    third = (rest - second.astype(F32)).astype(BF)
    return dot(picks, first, NT) + dot(picks, second, NT) + dot(picks, third, NT)


def self_forward_kernel(
    step, place_ref, rows_ref, own_ref, other_ref, c_ref, su_ref, sd_ref,
    q_ref, k_ref, v_ref, mine_ref, theirs_ref, lse_ref,
):
    count, width = rows_ref.shape
    half = width // 2
    own, other = own_ref[...].reshape(half, 384), other_ref[...].reshape(half, 384)
    qkv = dot(rows_ref[:, :half], own) + dot(rows_ref[:, half:], other)
    tables = (c_ref[...], su_ref[...], sd_ref[...])
    query = (rot(qkv[:, :128], tables) * 0.125).astype(BF)
    key = rot(qkv[:, 128:256], tables).astype(BF)
    value = qkv[:, 256:].astype(BF)
    q_ref[...] = query
    k_ref[...] = key
    v_ref[...] = value
    lane = iota((step, 128), 1)
    picks = jnp.where(iota((8, 128), 0) == iota((8, 128), 1), 1.0, 0.0).astype(BF)
    for at in range(0, count, step):
        part = query[at : at + step]
        mixed, logs = [], []
        for head in range(2):
            here = (lane // HD) == head
            scores = dot(jnp.where(here, part, jnp.zeros_like(part)), key, NT)
            top = jnp.max(scores, axis=1, keepdims=True)
            weights = jnp.exp(scores - top)
            total = jnp.sum(weights, axis=1, keepdims=True)
            mixed.append(dot(weights.astype(BF), value) * (1.0 / total))
            logs.append(top + jnp.log(total))
        out = jnp.where(lane < HD, mixed[0], mixed[1]).astype(BF)
        both = jnp.where(lane == 0, logs[0], jnp.where(lane == 1, logs[1], 0.0))
        lse_ref[0, :, at : at + step] = to_rows(picks, both)
        if at < count // 2:
            mine_ref[at : at + step, :] = out
        else:
            theirs_ref[at - count // 2 : at - count // 2 + step, :] = out


def self_weights(weights, first=0):
    shape = (weights.shape[0], 1, 1, weights.shape[3], 384)
    return [
        (pl.BlockSpec(shape, lambda p, s: (0, s[0], p % 2, 0, first // 2 + p // 2)), weights),
        (pl.BlockSpec(shape, lambda p, s: (0, 1 - s[0], p % 2, 0, first // 2 + p // 2)), weights),
    ]


def self_forward(place, rows, weights, tables, after=()):
    count, width = rows.shape
    wide = weights.shape[2] * weights.shape[4] // 3
    pairs = wide // 128
    return call(
        functools.partial(self_forward_kernel, 512),
        (pairs,),
        [(whole(rows.shape), rows)] + self_weights(weights)
        + [(whole((count, 128)), table) for table in tables],
        [(columns_of(count), shaped((count, wide), BF))] * 3
        + [(columns_of(count // 2), shaped((count // 2, wide), BF))] * 2
        + [(pl.BlockSpec((1, 8, count), lambda p, s: (p, 0, 0)), shaped((pairs, 8, count), F32))],
        "self_forward", 7 * pairs,
        after=after,
        scalars=place,
    )


def self_backward_kernel(
    step, begins, ends, place_ref, q_ref, k_ref, v_ref, mine_ref, theirs_ref, dmine_ref, dtheirs_ref, lse_ref,
    c_ref, su_ref, sd_ref, across_ref, own_ref, other_ref, *rest,
):
    if begins:
        gown_ref, gother_ref, *outs, qkv_ref, sum_ref = rest
    else:
        start_ref, gown_ref, gother_ref, *outs, qkv_ref, sum_ref = rest
    count = q_ref.shape[0]
    query = q_ref[...]
    grads = jnp.concatenate([dmine_ref[...], dtheirs_ref[...]], axis=0)
    mixed = jnp.concatenate([mine_ref[...], theirs_ref[...]], axis=0)
    picks = jnp.where((iota((8, 128), 1) // HD) == iota((8, 128), 0), 1.0, 0.0).astype(BF)
    delta = to_rows(picks, grads.astype(F32) * mixed.astype(F32))
    lane = iota((step, 128), 1)
    row = iota((128, step), 0)
    keys_across = jnp.transpose(k_ref[...].astype(F32)).astype(BF)
    query_across = jnp.zeros((128, count), F32)
    tables = (c_ref[...], su_ref[...], sd_ref[...])
    for at in range(0, count, step):
        here = slice(at, at + step)
        key, value = k_ref[here, :], v_ref[here, :]
        flipped = keys_across[:, here]
        dkeys, dvalues = [], []
        for head in range(2):
            inside = (lane // HD) == head
            scores = dot(jnp.where(inside, key, jnp.zeros_like(key)), query, NT)
            probs = jnp.exp(scores - lse_ref[0, head : head + 1, :])
            dprobs = dot(jnp.where(inside, value, jnp.zeros_like(value)), grads, NT)
            dscores = (probs * (dprobs - delta[head : head + 1, :])).astype(BF)
            dvalues.append(dot(probs.astype(BF), grads))
            dkeys.append(dot(dscores, query))
            picked = jnp.where((row // HD) == head, flipped, jnp.zeros_like(flipped))
            query_across = query_across + dot(picked, dscores)
        dkey = jnp.where(lane < HD, dkeys[0], dkeys[1])
        dvalue = jnp.where(lane < HD, dvalues[0], dvalues[1])
        qkv_ref[here, 128:256] = rot_back(dkey, [t[here] for t in tables]).astype(BF)
        qkv_ref[here, 256:384] = dvalue.astype(BF)
    dquery = jnp.transpose(query_across)
    qkv_ref[:, 0:128] = (rot_back(dquery, tables) * 0.125).astype(BF)

    first = pl.program_id(0) == 0
    last = pl.program_id(0) == pl.num_programs(0) - 1
    half = across_ref.shape[0] // 2
    own, other = own_ref[...].reshape(half, 384), other_ref[...].reshape(half, 384)
    both = qkv_ref[...]
    gown_ref[0] = dot(across_ref[:half, :], both).astype(BF)
    gother_ref[0] = dot(across_ref[half:, :], both).astype(BF)
    back = jnp.concatenate([dot(both, own, NT), dot(both, other, NT)], axis=1)

    @pl.when(first)
    def _():
        sum_ref[...] = back if begins else start_ref[...] + back

    @pl.when(jnp.logical_not(first))
    def _():
        sum_ref[...] += back

    @pl.when(last)
    def _():
        if ends:
            outs[0][...] = sum_ref[: count // 2, :].astype(BF)
            outs[1][...] = sum_ref[count // 2 :, :].astype(BF)
        else:
            outs[0][...] = sum_ref[...]


def self_backward(
    place, query, key, value, mine, theirs, dmine, dtheirs, lse, tables, flipped, weights, first, pairs,
    start, ends, after=(),
):
    count = query.shape[0]
    wide = 128 * pairs
    width = flipped.shape[0]
    out = pl.BlockSpec((1, width // 2, 384), lambda p, s: (p % 2, 0, p // 2))
    out_shape = (2, width // 2, 192 * pairs)
    rows, half = columns_of(count, first), columns_of(count // 2, first)
    half_rows = (count // 2, width)
    all_rows = (count, width)
    if ends:
        sums = [(whole(half_rows), shaped(half_rows, BF))] * 2
    else:
        sums = [(whole(all_rows), shaped(all_rows, F32))]
    starts = [] if start is None else [(whole(all_rows), start)]
    return call(
        functools.partial(self_backward_kernel, 512, start is None, ends),
        (pairs,),
        [(rows, array) for array in (query, key, value)]
        + [(half, array) for array in (mine, theirs, dmine, dtheirs)]
        + [(pl.BlockSpec((1, 8, count), lambda p, s: (first + p, 0, 0)), lse)]
        + [(whole((count, 128)), table) for table in tables]
        + [(whole(flipped.shape), flipped)] + self_weights(weights, first) + starts,
        [(out, shaped(out_shape, BF))] * 2 + sums,
        "self_backward", 13 * pairs,
        scratch=[pltpu.VMEM((count, 384), BF), pltpu.VMEM((count, width), F32)],
        after=after,
        scalars=place,
    )


def ffn_kernel(
    tile, carried, place_ref, mine_ref, theirs_ref, fmine_ref, ftheirs_ref,
    tmine_ref, ttheirs_ref, gmine_ref, gtheirs_ref, *rest,
):
    weight_refs, rest = rest[: len(rest) - 4 * carried - 8], rest[len(rest) - 4 * carried - 8 :]
    starts, rest = rest[: 4 * carried], rest[4 * carried :]
    ymine_ref, ytheirs_ref, dmine_ref, dtheirs_ref, gown_ref, gother_ref, y_ref, d_ref = rest
    rows, width = mine_ref.shape
    half = width // 2
    both = 2 * tile
    first = pl.program_id(0) == 0
    last = pl.program_id(0) == pl.num_programs(0) - 1

    @pl.when(first)
    def _():
        if carried:
            for part in range(2):
                y_ref[part] = starts[part][...].astype(F32)
                d_ref[part] = starts[2 + part][...].astype(F32)
        else:
            y_ref[...] = jnp.zeros_like(y_ref)
            d_ref[...] = jnp.zeros_like(d_ref)

    if len(weight_refs) == 2:
        own, other = (ref[...] for ref in weight_refs)
    else:
        nearer = pl.program_id(0) < pl.num_programs(0) // 2
        own = jnp.where(nearer, weight_refs[0][...], weight_refs[1][...])
        other = jnp.where(nearer, weight_refs[2][...], weight_refs[3][...])
    own, other = own.reshape(half, 3 * tile), other.reshape(half, 3 * tile)
    hidden_parts, dgate_up_parts = [], []
    for part, (ref, top_ref) in enumerate(((mine_ref, tmine_ref), (theirs_ref, ttheirs_ref))):
        gate_up = dot(ref[:, :half], own[:, :both]) + dot(ref[:, half:], other[:, :both])
        dhidden = dot(top_ref[:, :half], own[:, both:]) + dot(top_ref[:, half:], other[:, both:])
        gate, up = gate_up[:, :tile], gate_up[:, tile:]
        sigma = 1.0 / (1.0 + jnp.exp(-gate))
        silu = gate * sigma
        hidden = (silu * up).astype(BF)
        dup = (dhidden * silu).astype(BF)
        dgate = (dhidden * up * (sigma * (1.0 + gate * (1.0 - sigma)))).astype(BF)
        dgate_up = jnp.concatenate([dgate, dup], axis=1)
        y_ref[part, :, :half] += dot(hidden, own[:, both:], NT)
        y_ref[part, :, half:] += dot(hidden, other[:, both:], NT)
        d_ref[part, :, :half] += dot(dgate_up, own[:, :both], NT)
        d_ref[part, :, half:] += dot(dgate_up, other[:, :both], NT)
        hidden_parts.append(hidden)
        dgate_up_parts.append(dgate_up)
    for out, cut in ((gown_ref, slice(0, half)), (gother_ref, slice(half, width))):
        out[0, :, :both] = (
            dot(fmine_ref[cut, :], dgate_up_parts[0]) + dot(ftheirs_ref[cut, :], dgate_up_parts[1])
        ).astype(BF)
        out[0, :, both:] = (
            dot(gmine_ref[cut, :], hidden_parts[0]) + dot(gtheirs_ref[cut, :], hidden_parts[1])
        ).astype(BF)

    @pl.when(last)
    def _():
        ymine_ref[...] = y_ref[0].astype(BF)
        ytheirs_ref[...] = y_ref[1].astype(BF)
        dmine_ref[...] = d_ref[0].astype(BF)
        dtheirs_ref[...] = d_ref[1].astype(BF)


def ffn(place, rows, flipped, tops, tops_flipped, weights, tile, starts=(), after=()):
    count, width = rows[0].shape
    several = isinstance(weights, list)
    zs, shard, wide = weights[0].shape if several else (weights.shape[:1] + weights.shape[3:])
    half = zs * shard
    tiles = wide // (3 * tile)
    groups = 2
    if several:
        near = pl.BlockSpec((zs, shard, 3 * tile), lambda p, s: (0, 0, jnp.minimum(p, tiles - 1)))
        far = pl.BlockSpec((zs, shard, 3 * tile), lambda p, s: (0, 0, jnp.maximum(p - tiles, 0)))
        matrices = list(zip((near, far, near, far), weights))
    else:
        shape = (zs, 1, 1, shard, 3 * tile)
        own = pl.BlockSpec(shape, lambda p, s: (0, s[0], p // tiles, 0, p % tiles))
        other = pl.BlockSpec(shape, lambda p, s: (0, 1 - s[0], p // tiles, 0, p % tiles))
        matrices = [(own, weights), (other, weights)]
    block = pl.BlockSpec((1, half, 3 * tile), lambda p, s: (p // tiles, 0, p % tiles))
    out = shaped((groups, half, wide), BF)
    once, fixed = whole((count, width)), whole((width, count))
    return call(
        functools.partial(ffn_kernel, tile, len(starts) // 4),
        (groups * tiles,),
        [(once, a) for a in rows] + [(fixed, a) for a in flipped]
        + [(once, a) for a in tops] + [(fixed, a) for a in tops_flipped]
        + matrices + [(once, a) for a in starts],
        [(once, shaped((count, width), BF))] * 4 + [(block, out)] * 2,
        "feed_forward", 9 * groups * tiles,
        scratch=[pltpu.VMEM((2, count, width), F32)] * 2,
        after=after,
        scalars=place,
    )


def section(square, other):
    zs, _, ys, xs, shard, wide = square.shape
    return (
        pl.BlockSpec(
            (zs, 1, ys, xs, shard, wide),
            lambda *a: (0, 1 - a[-1][0] if other else a[-1][0], 0, 0, 0, 0),
            pipeline_mode=pl.Buffered(1),
        ),
        square,
    )


def sections(squares):
    return [section(squares[n], other) for n in (0, 1, 3) for other in (False, True)]


def weight_of(ref, x, y):
    zs, _, _, _, shard, wide = ref.shape
    return ref[:, 0, y, x].reshape(zs * shard, wide)


def cond_kernel(place_ref, cond_ref, own_ref, other_ref, key_ref, value_ref):
    shard = cond_ref.shape[1] // 8
    half = 4 * shard
    wide = own_ref.shape[-1]
    for x in range(2):
        for y in range(2):
            at = (2 * x + y) * wide
            for kind, out in ((0, key_ref), (1, value_ref)):
                total = None
                for part, ref in ((0, own_ref), (1, other_ref)):
                    weight = ref[:, 0, y, x, kind * shard : (kind + 1) * shard, :]
                    weight = weight.reshape(half, wide)
                    term = dot(cond_ref[:, part * half : (part + 1) * half], weight)
                    total = term if total is None else total + term
                out[:, at : at + wide] = total.astype(BF)


def cond_forward(place, cond, square):
    slots, width = cond.shape
    wide = 4 * square.shape[-1]
    return call(
        cond_kernel, (1,),
        [(whole(cond.shape), cond), section(square, False), section(square, True)],
        [(whole((slots, wide)), shaped((slots, wide), BF))] * 2,
        "cond_forward", 6,
        scalars=place,
    )


def beside(ref, y):
    return jnp.concatenate(
        [ref[:, at : at + 128] for at in range(y * 128, ref.shape[1], 256)], axis=1
    )


def middle_forward_kernel(
    place_ref, rows_ref, mine_ref, theirs_ref, gains_ref, key_ref, value_ref,
    out_own, out_other, cq_own, cq_other, co_own, co_other,
    x1_ref, second_ref, query_ref, mixed_ref, x2_ref, third_ref,
):
    rows, width = rows_ref.shape
    half = width // 2
    wide = out_own.shape[-1]
    slots = key_ref.shape[0]
    valid = iota((rows, slots), 1) < place_ref[3]
    lane = iota((rows, 128), 1)
    for out, cut in ((out_own, 0), (out_other, half)):
        total = rows_ref[:, cut : cut + half].astype(F32)
        for x in range(2):
            for y in range(2):
                mixed = jnp.where(
                    place_ref[2] == x, beside(mine_ref, y), beside(theirs_ref, y)
                )
                total += dot(mixed, weight_of(out, x, y), NT)
        x1_ref[:, cut : cut + half] = total
    normal, _ = normalize(x1_ref[...])
    second = (normal * gains_ref[1:2, :]).astype(BF)
    second_ref[...] = second
    for x in range(2):
        for y in range(2):
            at = (2 * x + y) * wide
            query = dot(second[:, :half], weight_of(cq_own, x, y)) + dot(
                second[:, half:], weight_of(cq_other, x, y)
            )
            query_ref[:, at : at + wide] = (query * 0.125).astype(BF)
    for at in range(0, 4 * wide, 128):
        query, key, value = (
            ref[:, at : at + 128] for ref in (query_ref, key_ref, value_ref)
        )
        mixed = []
        for head in range(2):
            part = jnp.where((lane // HD) == head, query, jnp.zeros_like(query))
            scores = jnp.where(valid, dot(part, key, NT), MASKED_SCORE)
            top = jnp.max(scores, axis=1, keepdims=True)
            weights = jnp.exp(scores - top)
            total = jnp.sum(weights, axis=1, keepdims=True)
            mixed.append(dot(weights.astype(BF), value) * (1.0 / total))
        mixed_ref[:, at : at + 128] = jnp.where(lane < HD, mixed[0], mixed[1]).astype(BF)
    for out, cut in ((co_own, 0), (co_other, half)):
        total = x1_ref[:, cut : cut + half]
        for x in range(2):
            for y in range(2):
                at = (2 * x + y) * wide
                total += dot(mixed_ref[:, at : at + wide], weight_of(out, x, y), NT)
        x2_ref[:, cut : cut + half] = total
    normal, _ = normalize(x2_ref[...])
    third_ref[...] = (normal * gains_ref[2:3, :]).astype(BF)


def middle_forward(place, rows, mine, theirs, gains, key, value, squares, after=()):
    full = whole(rows.shape)
    part = whole(mine.shape)
    cond = whole(key.shape)
    return call(
        middle_forward_kernel, (1,),
        [(full, rows), (part, mine), (part, theirs)]
        + [(whole(gains.shape), gains), (cond, key), (cond, value)] + sections(squares),
        [(full, shaped(rows.shape, dtype)) for dtype in (F32, BF, BF, BF, F32, BF)],
        "middle_forward", 26,
        after=after, scalars=place,
    )


def middle_backward_kernel(
    place_ref, d_ref, r_ref, top_ref, x2_ref, x1_ref, gains_ref,
    query_ref, key_ref, value_ref,
    out_own, out_other, cq_own, cq_other, co_own, co_other,
    dx1_ref, e2_ref, dquery_ref, dkey_ref, dvalue_ref, e1_ref, *refs,
):
    dmine_ref, dtheirs_ref, dmixed_ref = refs
    rows, width = x1_ref.shape
    half = width // 2
    wide = out_own.shape[-1]
    slots = key_ref.shape[0]
    grad_third = d_ref[...].astype(F32) + r_ref[...].astype(F32)
    normal, scale = normalize(x2_ref[...])
    dx2 = top_ref[...].astype(F32) + normalize_back(grad_third, gains_ref[2:3, :], normal, scale)
    dx1_ref[...] = dx2
    e2 = dx2.astype(BF)
    e2_ref[...] = e2
    for x in range(2):
        for y in range(2):
            at = (2 * x + y) * wide
            dmixed_ref[:, at : at + wide] = (
                dot(e2[:, :half], weight_of(co_own, x, y))
                + dot(e2[:, half:], weight_of(co_other, x, y))
            ).astype(BF)
    valid = iota((slots, rows), 0) < place_ref[3]
    lane = iota((slots, 128), 1)
    row = iota((128, slots), 0)
    for at in range(0, 4 * wide, 128):
        here = slice(at, at + 128)
        query, key, value, grads = (
            ref[:, here] for ref in (query_ref, key_ref, value_ref, dmixed_ref)
        )
        flipped = jnp.transpose(key.astype(F32)).astype(BF)
        dkeys, dvalues = [], []
        query_across = None
        for head in range(2):
            inside = (lane // HD) == head
            scores = dot(jnp.where(inside, key, jnp.zeros_like(key)), query, NT)
            scores = jnp.where(valid, scores, MASKED_SCORE)
            weights = jnp.exp(scores - jnp.max(scores, axis=0, keepdims=True))
            probs = weights * (1.0 / jnp.sum(weights, axis=0, keepdims=True))
            dprobs = dot(jnp.where(inside, value, jnp.zeros_like(value)), grads, NT)
            shared = jnp.sum(probs * dprobs, axis=0, keepdims=True)
            dscores = (probs * (dprobs - shared)).astype(BF)
            dvalues.append(dot(probs.astype(BF), grads))
            dkeys.append(dot(dscores, query))
            term = dot(jnp.where((row // HD) == head, flipped, jnp.zeros_like(flipped)), dscores)
            query_across = term if query_across is None else query_across + term
        dkey_ref[:, here] = jnp.where(lane < HD, dkeys[0], dkeys[1]).astype(BF)
        dvalue_ref[:, here] = jnp.where(lane < HD, dvalues[0], dvalues[1]).astype(BF)
        dquery_ref[:, here] = (jnp.transpose(query_across) * 0.125).astype(BF)
    parts = []
    for weight in (cq_own, cq_other):
        total = None
        for x in range(2):
            for y in range(2):
                at = (2 * x + y) * wide
                term = dot(dquery_ref[:, at : at + wide], weight_of(weight, x, y), NT)
                total = term if total is None else total + term
        parts.append(total)
    grad_second = jnp.concatenate(parts, axis=1)
    normal, scale = normalize(x1_ref[...])
    dx1 = dx1_ref[...] + normalize_back(grad_second, gains_ref[1:2, :], normal, scale)
    dx1_ref[...] = dx1
    e1 = dx1.astype(BF)
    e1_ref[...] = e1
    for y in range(2):
        first, second = (
            dot(e1[:, :half], weight_of(out_own, x, y))
            + dot(e1[:, half:], weight_of(out_other, x, y))
            for x in range(2)
        )
        low = place_ref[2] == 0
        for out, grads in (
            (dtheirs_ref, jnp.where(low, second, first).astype(BF)),
            (dmine_ref, jnp.where(low, first, second).astype(BF)),
        ):
            for j in range(wide // 128):
                at = (2 * j + y) * 128
                out[:, at : at + 128] = grads[:, j * 128 : (j + 1) * 128]


def middle_backward(
    place, d, r, top, x2, x1, gains, query, key, value, squares, after=()
):
    full = whole(x1.shape)
    rows, width = x1.shape
    part = (rows, width // 2)
    cond = whole(key.shape)
    return call(
        middle_backward_kernel, (1,),
        [(full, array) for array in (d, r, top, x2, x1)]
        + [(whole(gains.shape), gains), (full, query), (cond, key), (cond, value)]
        + sections(squares),
        [(full, shaped(x1.shape, F32)), (full, shaped(x1.shape, BF)), (full, shaped(x1.shape, BF))]
        + [(cond, shaped(key.shape, BF))] * 2
        + [(full, shaped(x1.shape, BF))]
        + [(whole(part), shaped(part, BF))] * 2,
        "middle_backward", 40,
        scratch=[pltpu.VMEM((rows, width), BF)],
        after=after,
        scalars=place,
    )


def middle_weights_kernel(
    pieces, place_ref, e1_ref, second_ref, dquery_ref, cond_ref, dkey_ref, dvalue_ref,
    e2_ref, mixed_ref, kv_own, kv_other, *rest,
):
    mine_refs, theirs_refs = rest[:pieces], rest[pieces : 2 * pieces]
    aown_ref, aother_ref, bown_ref, bother_ref, dcond_ref = rest[2 * pieces : 2 * pieces + 5]
    f1_ref, fsecond_ref, f2_ref, fcond_ref = rest[2 * pieces + 5 :]
    width = e1_ref.shape[1]
    half = width // 2
    wide = kv_own.shape[-1]
    shard = cond_ref.shape[1] // 8
    first = pl.program_id(0) == 0

    @pl.when(first)
    def _():
        for source, target in (
            (e1_ref, f1_ref), (second_ref, fsecond_ref), (e2_ref, f2_ref), (cond_ref, fcond_ref)
        ):
            target[...] = jnp.transpose(source[...])
        dcond_ref[...] = jnp.zeros_like(dcond_ref)

    from_theirs = pl.program_id(0) // 2 != place_ref[2]
    mixed = jnp.concatenate(
        [jnp.where(from_theirs, b[...], a[...]) for a, b in zip(mine_refs, theirs_refs)], axis=1
    )
    for part, (first_out, out, kv) in enumerate(
        ((aown_ref, bown_ref, kv_own), (aother_ref, bother_ref, kv_other))
    ):
        cut = slice(part * half, (part + 1) * half)
        first_out[0, 0, :, 0:wide] = dot(f1_ref[cut, :], mixed).astype(BF)
        first_out[0, 0, :, wide : 2 * wide] = dot(fsecond_ref[cut, :], dquery_ref[...]).astype(BF)
        out[0, 0, :, wide : 2 * wide] = dot(f2_ref[cut, :], mixed_ref[...]).astype(BF)
        weights = []
        for kind, grads in ((0, dkey_ref), (1, dvalue_ref)):
            at = part * 4 * shard
            both = dot(fcond_ref[at : at + 4 * shard, :], grads[...]).astype(BF)
            for z in range(4):
                low = (2 * z + kind) * shard
                out[0, 0, low : low + shard, 0:wide] = both[z * shard : (z + 1) * shard]
            weight = kv[:, 0, 0, 0, kind * shard : (kind + 1) * shard, :]
            weights.append(weight.reshape(4 * shard, wide))
        dcond_ref[:, part * 4 * shard : (part + 1) * 4 * shard] += dot(
            dkey_ref[...], weights[0], NT
        ) + dot(dvalue_ref[...], weights[1], NT)


def middle_weights(
    place, e1, mine, theirs, second, dquery, cond, dkey, dvalue, e2, mixed, square, after=()
):
    zs, _, _, _, square_shard, wide = square.shape
    rows, width = e1.shape
    slots = cond.shape[0]
    full = whole(e1.shape)
    block = pl.BlockSpec((rows, wide), lambda p, s: (0, p))
    pairs = [
        pl.BlockSpec((rows, 128), lambda p, s, j=j: (0, 2 * j + p % 2))
        for j in range(mine.shape[1] // 256)
    ]
    cond_block = pl.BlockSpec((slots, wide), lambda p, s: (0, p))
    shape = (zs, 1, 1, 1, square_shard, wide)
    own = pl.BlockSpec(shape, lambda p, s: (0, s[0], p % 2, p // 2, 0, 0))
    other = pl.BlockSpec(shape, lambda p, s: (0, 1 - s[0], p % 2, p // 2, 0, 0))
    out = pl.BlockSpec((1, 1, width // 2, 2 * wide), lambda p, s: (p // 2, p % 2, 0, 0))
    out_shape = (2, 2, width // 2, 2 * wide)
    return call(
        functools.partial(middle_weights_kernel, len(pairs)), (4,),
        [(full, e1), (full, second), (block, dquery)]
        + [(whole(cond.shape), cond), (cond_block, dkey), (cond_block, dvalue)]
        + [(full, e2), (block, mixed), (own, square), (other, square)]
        + [(pair, a) for a in (mine, theirs) for pair in pairs],
        [(out, shaped(out_shape, BF))] * 4 + [(whole(cond.shape), shaped(cond.shape, F32))],
        "middle_weights", 5,
        scratch=[pltpu.VMEM((width, rows), BF)] * 3 + [pltpu.VMEM((cond.shape[1], slots), BF)],
        after=after,
        scalars=place,
    )


def fold_kernel(place_ref, keep_ref, got_keep_ref, send_ref, got_send_ref, keep_out, send_out):
    send_out[...] = (send_ref[...].astype(F32) + got_send_ref[...].astype(F32)).astype(BF)
    keep_out[...] = (keep_ref[...].astype(F32) + got_keep_ref[...].astype(F32)).astype(BF)


def fold(place, bit, here, got, at):
    shape = here.shape
    before, after = math.prod(shape[:at]), math.prod(shape[at + 1 : -2])
    view = (before, 2, after) + shape[-2:]
    block = (1, 1, 1) + shape[-2:]
    keep = pl.BlockSpec(block, lambda a, b, s: (a, s[bit], b, 0, 0))
    send = pl.BlockSpec(block, lambda a, b, s: (a, 1 - s[bit], b, 0, 0))
    out = pl.BlockSpec(block, lambda a, b, s: (a, 0, b, 0, 0))
    out_shape = shaped((before, 1, after) + shape[-2:], BF)
    here, got = here.reshape(view), got.reshape(view)
    results = call(
        fold_kernel, (before, after),
        [(keep, here), (keep, got), (send, here), (send, got)],
        [(out, out_shape)] * 2,
        "fold", here.size * 1.3e-6, scalars=place,
    )
    left = shape[:at] + (1,) + shape[at + 1 :]
    return [array.reshape(left) for array in results]


def finish_ffn(weight_ref, sources, gu_ref, down_ref):
    chunks = len(sources) // 2
    tiles = sources[0].shape[1] // (3 * TILE)
    hidden = chunks * tiles * TILE
    total = jnp.zeros((weight_ref.shape[0], 1), F32)
    for i in range(chunks):
        keep, got = sources[2 * i], sources[2 * i + 1]
        for j in range(tiles):
            at = 3 * j * TILE
            target = (i * tiles + j) * TILE
            grads = keep[:, at : at + 3 * TILE].astype(F32) + got[:, at : at + 3 * TILE].astype(F32)
            for kind in range(2):
                cut = slice(kind * hidden + target, kind * hidden + target + TILE)
                part = grads[:, kind * TILE : (kind + 1) * TILE]
                gu_ref[:, cut] = part
                total += jnp.sum(part * weight_ref[:, cut].astype(F32), axis=1, keepdims=True)
            down_ref[:, target : target + TILE] = grads[:, 2 * TILE :]
    return total


SUM_CHAINS = {
    "A": ("z1", "y", "z2"),
    "B": ("x", "z2", "z1"),
    "Q0": ("z2", "y", "z1"),
    "Q1": ("y", "z1", "z2"),
}
SUM_STEPS = (
    "Q0.0", "Q1.0", "out", "A.1", "B.1", "Q0.1", "Q1.1", "A.2", "Q0.2", "B.2", "in", "Q1.2",
)


def scatter_kernel(
    queries, their_dx_ref, *refs,
):
    few = 12 + 2 * CHUNKS
    sources, refs, fetched = refs[:few], refs[few : len(refs) - few], refs[len(refs) - few :]
    dx_ref, gain_ref, qkv_weight, query_weight, ffn_weight, x2_ref, y_ref = fetched[:7]
    y_got_ref, turn_ref, rows_ref, gains_ref, dx1_ref, *ffn_refs = fetched[7:]
    inputs, refs = refs[: 4 + 2 * queries], refs[4 + 2 * queries :]
    outs, refs = refs[:10], refs[10:]
    block_ref, dinput_ref, out_ref, cq_ref, ckv_ref, co_ref, qkv_ref, norm_ref = outs[:8]
    dx_slot, norm_slot, refs = refs[0], refs[1], refs[2:]
    works, slots, refs = refs[: 2 + queries], refs[2 + queries : 5 * (2 + queries)], refs[5 * (2 + queries) :]
    sends, receives, local_sems = refs
    dp, seq, side = (lax.axis_index(name) for name in ("dp", "seq", "half"))
    here = {"z2": dp // 4, "z1": (dp // 2) % 2, "c": dp % 2, "y": seq, "x": side}
    partners = {
        "z2": (dp + 4 - 8 * (dp // 4), seq, side),
        "z1": (dp + 2 - 4 * ((dp // 2) % 2), seq, side),
        "c": (dp + 1 - 2 * (dp % 2), seq, side),
        "y": (dp, 1 - seq, side),
        "x": (dp, seq, 1 - side),
    }
    barrier = pltpu.get_barrier_semaphore()
    for axis in AXES:
        pl.semaphore_signal(
            barrier, inc=1, device_id=partners[axis], device_id_type=pl.DeviceIdType.MESH
        )
    pl.semaphore_wait(barrier, len(AXES))
    count = [0, 0]

    def send(source, target, axis):
        copy = pltpu.make_async_remote_copy(
            source, target, sends.at[count[0]], receives.at[count[0]],
            device_id=partners[axis], device_id_type=pl.DeviceIdType.MESH,
        )
        count[0] += 1
        copy.start()
        return copy

    def load(source, target):
        copy = pltpu.make_async_copy(source, target, local_sems.at[count[1]])
        count[1] += 1
        copy.start()
        return copy

    def add(target, source):
        target[...] = (target[...].astype(F32) + source[...].astype(F32)).astype(BF)

    names = ["A", "B"] + ["Q%d" % i for i in range(queries)]
    work = dict(zip(names, works))
    slot = {name: slots[4 * i : 4 * i + 4] for i, name in enumerate(names)}
    first = dict.fromkeys(names, "y")
    first["B"] = "x"
    flying = {}
    for i in range(queries):
        own, other = inputs[4 + 2 * i], inputs[5 + 2 * i]
        name = "Q%d" % i
        flying[name] = [load(own, work[name]), send(other, slot[name][0], "c")]
    for i, name in enumerate("AB"):
        flying[name] = [load(inputs[2 * i], work[name]), load(inputs[2 * i + 1], slot[name][0])]

    def part(name, step, goes):
        index = [slice(None)] * 3
        for at, axis in enumerate(SUM_CHAINS[name][: step + 1]):
            place = {"z2": 1, "z1": 2}.get(axis, 0)
            index[place] = 1 - here[axis] if goes and at == step else here[axis]
        return work[name].at[tuple(index)]

    def advance(name, step):
        for copy in flying[name]:
            copy.wait()
        add(work[name] if step == 0 else part(name, step - 1, False), slot[name][step])
        target = slot[name][step + 1]
        flying[name] = [send(part(name, step, True), target, SUM_CHAINS[name][step])]

    def end(name):
        for copy in flying[name]:
            copy.wait()
        return part(name, 2, False)[...].astype(F32) + slot[name][3][...].astype(F32)

    odd = here["c"] == 1
    fetches = [load(source, target) for source, target in zip(sources, fetched)]
    advance("A", 0)
    advance("B", 0)
    dx_copy = send(their_dx_ref, dx_slot, "x")
    for event in SUM_STEPS:
        if event == "out":
            for copy in fetches:
                copy.wait()
            total = x2_ref[...] + (y_ref[...].astype(F32) + y_got_ref[...].astype(F32))
            total = total.astype(BF).astype(F32)
            block_ref[...] = put_back(total, turn_ref[...], odd, 1).astype(BF)
            third = finish_ffn(ffn_weight, ffn_refs, *outs[8:])
        elif event == "in":
            dx_copy.wait()
            normal, scale = normalize(rows_ref[...].astype(F32))
            grads = dx_ref[...].astype(F32) + dx_slot[...].astype(F32)
            total = dx1_ref[...] + normalize_back(grads, gains_ref[0:1, :], normal, scale)
            dinput_ref[...] = put_back(total, turn_ref[...], odd, 2)
        else:
            name, step = event.split(".")
            advance(name, int(step))

    wide = cq_ref.shape[1]
    grads = end("A")
    out_ref[...] = grads[:, :wide]
    cq_ref[...] = grads[:, wide:]
    second = jnp.sum(grads[:, wide:] * query_weight[...].astype(F32), axis=1, keepdims=True)
    grads = end("B")
    ckv_ref[...] = grads[:, :wide]
    co_ref[...] = grads[:, wide:]
    total = jnp.zeros(second.shape, F32)
    j = 0
    for name in names[2:]:
        grads = end(name)
        for at in range(0, grads.shape[1], 384):
            for kind in range(3):
                cut = slice(kind * wide + j * 128, kind * wide + (j + 1) * 128)
                piece = grads[:, at + kind * 128 : at + (kind + 1) * 128]
                qkv_ref[kind, :, j * 128 : (j + 1) * 128] = piece
                total += jnp.sum(piece * qkv_weight[:, cut].astype(F32), axis=1, keepdims=True)
            j += 1
    lane = iota(norm_ref.shape, 1)
    norm_ref[...] = jnp.where(
        lane == 0,
        total / gain_ref[:, 0:1],
        jnp.where(lane == 1, second / gain_ref[:, 1:2], jnp.where(lane == 2, third / gain_ref[:, 2:3], 0.0)),
    )
    for at, axis in enumerate(("y", "x")):
        send(norm_ref, norm_slot.at[at], axis).wait()
        norm_ref[...] += norm_slot[at]


def scatter_last(
    dx, their_dx, gain_columns, qkv_weight, query_weight, ffn_weight, ffn_sums, x2, y, y_got, turn, rows, gains,
    dx1, squares, queries,
):
    anywhere, vmem = pl.BlockSpec(memory_space=pl.ANY), pl.BlockSpec(memory_space=pltpu.VMEM)
    shard, wide = query_weight.shape
    shapes = [a.shape for a, _ in squares] + [a.shape for a, _ in queries]
    assert all(shape[:3] == (2, 2, 2) for shape in shapes)
    few = [dx, gain_columns, qkv_weight, query_weight, ffn_weight, x2, y, y_got, turn, rows]
    few += [gains, dx1, *ffn_sums]
    many = [a for pair in (*squares, *queries) for a in pair]
    outs = [(x2.shape, BF), (x2.shape, F32), ((shard, wide), F32), ((shard, wide), F32)]
    outs += [((shard, wide), F32), ((shard, wide), F32), ((3, shard, wide), F32)]
    outs += [((shard, 128), F32), (ffn_weight.shape, F32), ((shard, ffn_weight.shape[1] // 2), F32)]
    slots = [pltpu.VMEM(shape[at:], BF) for shape in shapes for at in range(4)]
    copies = 1 + 2 + len(queries) * 4 + len(squares) * 3
    return pl.pallas_call(
        functools.partial(scatter_kernel, len(queries)),
        in_specs=[anywhere] * (1 + len(few) + len(many)),
        out_specs=[vmem] * len(outs),
        out_shape=[shaped(*out) for out in outs],
        scratch_shapes=[pltpu.VMEM(rows.shape, BF), pltpu.VMEM((2, shard, 128), F32)]
        + [pltpu.VMEM(shape, BF) for shape in shapes]
        + slots
        + [
            pltpu.SemaphoreType.DMA((copies,)),
            pltpu.SemaphoreType.DMA((copies,)),
            pltpu.SemaphoreType.DMA((4 + len(queries) + len(few),)),
        ]
        + [pltpu.VMEM(a.shape, a.dtype) for a in few],
        compiler_params=pltpu.CompilerParams(
            vmem_limit_bytes=63 << 20, collective_id=1, has_side_effects=True
        ),
        name="scatter_last",
    )(their_dx, *few, *many)


def swap(array, axis, bit=1):
    return lax.ppermute(array, axis, [(i, i ^ bit) for i in range(lax.axis_size(axis))])


def pair_body(
    block_in,
    cond_tokens,
    cond_count,
    norm1_gain,
    norm2_gain,
    norm3_gain,
    qkv_weight,
    attn_out_weight,
    cross_q_weight,
    cross_kv_weight,
    cross_out_weight,
    gate_up_weight,
    down_weight,
    out_cotangent,
):
    rows, width = block_in.shape
    shard = qkv_weight.shape[0]
    head_cols = attn_out_weight.shape[0]
    hidden_cols = down_weight.shape[0]
    cond_slots, cond_width = cond_tokens.shape[1:]
    cond_shard = cross_kv_weight.shape[0]
    dp = lax.axis_index("dp")
    seq = lax.axis_index("seq")
    side = lax.axis_index("half")
    z_size = lax.axis_size("dp") // 2
    core, z = dp % 2, dp // 2
    odd = core.astype(jnp.int32).reshape(1)
    half = width // 2
    pairs_here = head_cols // 128
    per_chunk = hidden_cols // CHUNKS
    z_bits = []
    bit = z_size // 2
    while bit:
        z_bits.append(bit)
        bit //= 2

    qkv_pack = jnp.concatenate(
        [
            qkv_weight[:, :, j * 128 : (j + 1) * 128].reshape(shard, 384)
            for j in range(pairs_here)
        ],
        axis=1,
    )
    square_pack = jnp.concatenate(
        [
            attn_out_weight.T,
            cross_q_weight,
            cross_kv_weight.transpose(1, 0, 2).reshape(shard, head_cols),
            cross_out_weight.T,
        ],
        axis=1,
    )
    gains = jnp.stack([norm1_gain, norm2_gain, norm3_gain]).astype(F32)
    gains = lax.dynamic_update_slice(jnp.zeros((8, width), F32), gains, (0, dp * shard))
    places = {"half": 0, "seq": 1, "own": 1}
    steps = {"half": ("half", 1, 2), "seq": ("seq", 1, 1), "own": ("seq", 1, 6)}
    for at, bit in enumerate(z_bits):
        name = "z%d" % bit
        places[name] = 2 + at
        steps[name] = ("dp", 2 * bit, 4 + at)
    far, near = "z%d" % z_bits[0], "z%d" % z_bits[-1]

    gate_up_flat = gate_up_weight.reshape(shard, 2 * hidden_cols)
    (
        wq, w0, w1, w2, w3, mine_in, theirs_in, top_grads, gains, first_all, first_across, turn,
        *packs,
    ) = gather_first(
        qkv_pack, square_pack, gains, block_in, out_cotangent, gate_up_flat, down_weight.T
    )
    wq = wq.reshape((z_size, 2, 2) + qkv_pack.shape)
    squares = [w.reshape((z_size, 2, 2, 2, shard, head_cols)) for w in (w0, w1, w2, w3)]
    place = jnp.stack([core, seq, side, cond_count[seq], z // 2, z % 2, 0 * z]).astype(jnp.int32)
    their_top = swap(top_grads, "half")
    ffn_weights = []
    for pack in packs[:-1]:
        gathered = lax.all_gather(pack, ("dp", "seq"))
        ffn_weights.append(gathered.reshape((z_size, 2, 2) + pack.shape))

    def over(array, name, after):
        axis, bit, which = steps[name]
        array = hold(array, after)
        got, upper = swap(array, axis, bit), place[which] == 1
        return jnp.stack([jnp.where(upper, got, array), jnp.where(upper, array, got)], axis=-3)

    slab = over(packs[-1], far, (gains,))

    class Way:
        def __init__(self, own, other, wide, order):
            full = (2 if wide else 1, 2) + (2,) * len(z_bits) + (shard, own.shape[-1])
            self.order = list(order)
            self.here = own.reshape(full)
            self.got = swap(other, "dp", 1).reshape(full)

        def step(self, after=(), late=()):
            step = self.order.pop(0)
            if late:
                self.here = hold(self.here, late)
            axis, bit, which = steps[step]
            self.here, send = fold(place, which, self.here, self.got, places[step])
            if after:
                send = hold(send, after)
            self.got = swap(send, axis, bit)
            return self.here

        def end(self):
            while self.order:
                self.step()
            shape = self.here.shape[-2:]
            return [self.here.reshape(shape), self.got.reshape(shape)]

    along = jnp.arange(rows)
    tables = rot_tables(jnp.concatenate([side * rows + along, (1 - side) * rows + along]))
    query, key, value, mine, theirs, lse = self_forward(place, first_all, wq, tables)
    theirs = hold(theirs, (their_top,))
    slab = over(slab, near, (lse,))
    mixed = swap(theirs, "half")

    my_cond = hold(cond_tokens[seq], (theirs,)).reshape(cond_slots, z_size, 2, cond_shard)
    swapped = jnp.where(core == 1, my_cond[:, :, ::-1], my_cond)
    my_cond = swapped.transpose(0, 2, 1, 3).reshape(cond_slots, cond_width)
    my_cond = jnp.pad(my_cond, ((0, SLOTS - cond_slots), (0, 0)))
    top_across, their_top_across = across(hold(top_grads, (theirs,)), their_top)
    cross_key, cross_value = cond_forward(place, my_cond, squares[2])
    x1, second, cross_query, cross_mixed, x2, third = middle_forward(
        place, mine_in, mine, mixed, gains, cross_key, cross_value, squares,
        (top_across, their_top_across),
    )
    slab = slab.reshape((z_size,) + slab.shape[2:])
    their_third = swap(third, "half")
    (third_across,) = across(third)
    (their_third_across,) = across(their_third)
    ffn_weights[0] = hold(ffn_weights[0], (their_third_across, third_across))
    sums, ways, after = (), [], (slab,)
    for i in range(CHUNKS):
        *sums, gown, gother = ffn(
            place,
            (third, their_third),
            (third_across, their_third_across),
            (top_grads, their_top),
            (top_across, their_top_across),
            ffn_weights[i],
            TILE,
            sums,
            after,
        )
        if i == 0:
            slab = hold(slab, (sums[2],))
            far_slab = swap(slab, "seq")
            slabs = [slab, far_slab]
            ffn_weights.append(slabs + [swap(s, "dp", 1) for s in slabs])
        else:
            arrived = [far_slab if i == 1 else ways[0].got]
            gother = hold(gother, arrived)
        order = (near, "own", far) if i == CHUNKS - 1 else ("seq", near, far)
        ways.append(Way(gown, gother, False, order))
        if i < CHUNKS - 1:
            after = (ways[i].step(((far_slab, ways[0].got)[i],)),)
    ymine, ytheirs, dmine, dtheirs = sums
    d_received = swap(hold(dtheirs, arrived), "half")

    after = [ways[0].step(), ways[2].step()]
    y_received = swap(hold(ytheirs, (d_received, *after)), "half")
    dx1, e2, dquery, dkey, dvalue, e1, dmine, dtheirs = middle_backward(
        place, dmine, d_received, top_grads, x2, x1, gains,
        cross_query, cross_key, cross_value, squares, after,
    )
    dtheirs = swap(dtheirs, "half")
    aown, aother, bown, bother, dcond = middle_weights(
        place, e1, mine, mixed, second, dquery, my_cond, dkey, dvalue, e2, cross_mixed, squares[2]
    )
    arrived = [way.got for way in ways] + [dtheirs, y_received]
    aother, bother = hold(aother, arrived), hold(bother, arrived)
    first_way = Way(aown, aother, True, ("half", "seq", near, far))
    second_way = Way(bown, bother, True, ("seq", "half", near, far))
    qkv_grads = []
    pairs = 2 * pairs_here
    after = [aother] + [way.step() for way in ways if way.order]
    running = None
    for first, several in ((0, 2), (2, pairs - 2)):
        gown, gother, *sums = self_backward(
            place, query, key, value, mine, theirs, dmine, dtheirs, lse, tables, first_across,
            wq, first, several, running, first > 0, after,
        )
        full = (2, 2, 2, shard, gown.shape[-1])
        qkv_grads.append((gown.reshape(full), gother.reshape(full)))
        running = sums[0]
        if first == 0:
            arrived = [way.got for way in ways] + [first_way.got, second_way.got]
            running = hold(running, arrived)
            dcond = hold(dcond, (running,))
            after = [way.step(late=(running,)) for way in ways if way.order]
            after += [first_way.step(late=(running,)), second_way.step(late=(running,))]
    rmine, rtheirs = sums
    rtheirs = hold(rtheirs, (first_way.got, second_way.got, ways[-1].got))
    gain_columns = [g.astype(F32).reshape(shard, 1) for g in (norm1_gain, norm2_gain, norm3_gain)]
    (
        block_out, grad_input, grad_out, grad_cq, grad_ckv, grad_co, grad_qkv, gain_grads,
        grad_gate_up, grad_down,
    ) = scatter_last(
        rmine, rtheirs, jnp.concatenate(gain_columns, axis=1),
        qkv_weight.reshape(shard, 3 * head_cols), cross_q_weight,
        gate_up_flat, [array for way in ways for array in way.end()],
        x2, ymine, y_received, turn, mine_in, gains, dx1,
        [
            tuple(a.reshape((2, 2, 2) + a.shape[-2:]) for a in (way.here, way.got))
            for way in (first_way, second_way)
        ],
        qkv_grads,
    )
    grad_ckv = grad_ckv.reshape(2, cond_shard, head_cols).transpose(1, 0, 2)
    grad_qkv = grad_qkv.transpose(1, 0, 2)
    grad_gate_up = grad_gate_up.reshape(shard, 2, hidden_cols)

    dcond = dcond[:cond_slots].reshape(cond_slots, 2, z_size, cond_shard)
    dcond = jnp.where(core == 1, dcond[:, ::-1], dcond).transpose(0, 2, 1, 3)
    dcond = dcond.reshape(cond_slots, 2, 2, cond_width // 4)
    cond_keep = lax.dynamic_index_in_dim(dcond, side, 2, keepdims=False)
    cond_send = lax.dynamic_index_in_dim(dcond, 1 - side, 2, keepdims=False)
    dcond = cond_keep + swap(cond_send, "half")
    cond_keep = lax.dynamic_index_in_dim(dcond, seq, 1, keepdims=False)
    cond_send = lax.dynamic_index_in_dim(dcond, 1 - seq, 1, keepdims=False)
    cond_got = swap(cond_send, "seq")
    grad_cond = jnp.stack(
        [jnp.where(seq == 1, cond_got, cond_keep), jnp.where(seq == 1, cond_keep, cond_got)]
    )

    gain_grads = gain_grads[:, :3].T
    return (
        block_out,
        grad_input,
        grad_cond,
        gain_grads[0],
        gain_grads[1],
        gain_grads[2],
        grad_qkv,
        grad_out.T,
        grad_cq,
        grad_ckv,
        grad_co.T,
        grad_gate_up,
        grad_down.T,
    )


def pair_solution(mesh, sequences):
    dp, tensor = mesh.devices.shape
    finer = Mesh(mesh.devices.reshape(dp, sequences, tensor // sequences), ("dp", "seq", "half"))
    every = ("dp", "seq", "half")
    both = ("seq", "half")
    return jax.shard_map(
        pair_body,
        mesh=finer,
        in_specs=(
            P(every, None),
            P("dp", None, None),
            P("dp"),
            P("dp"),
            P("dp"),
            P("dp"),
            P("dp", None, both),
            P(both, "dp"),
            P("dp", both),
            P("dp", None, both),
            P(both, "dp"),
            P("dp", None, both),
            P(both, "dp"),
            P(every, None),
        ),
        out_specs=(
            P(every, None),
            P(every, None),
            P("dp", None, both),
            P("dp"),
            P("dp"),
            P("dp"),
            P("dp", None, both),
            P(both, "dp"),
            P("dp", both),
            P("dp", None, both),
            P(both, "dp"),
            P("dp", None, both),
            P(both, "dp"),
        ),
        check_vma=False,
    )


CHUNKS = 3
FLOPS = 1.15e9
TILE = 256
SLOTS = 144


def solution(mesh):
    dp, tensor = mesh.devices.shape

    def run(*args):
        block_in, cond_tokens, qkv, down = args[0], args[1], args[6], args[12]
        sequences = cond_tokens.shape[0] // dp
        fits = (
            sequences == 2
            and tensor == 4
            and dp == 8
            and qkv.shape[2] % (tensor * 128) == 0
            and (qkv.shape[0] // dp) % 64 == 0
            and down.shape[0] % (tensor * CHUNKS * TILE) == 0
            and qkv.shape[0] == 2 * cond_tokens.shape[2]
            and qkv.shape[2] == qkv.shape[0]
            and cond_tokens.shape[1] <= SLOTS
            and block_in.shape[0] == 1024 * cond_tokens.shape[0]
        )
        if fits:
            return pair_solution(mesh, sequences)(*args)
        return general_solution(mesh)(*args)

    return run
```

```python
import functools
import math

import jax
import jax.numpy as jnp
from jax import lax
from jax.experimental import pallas as pl
from jax.experimental.pallas import tpu as pltpu
from jax.sharding import Mesh
from jax.sharding import PartitionSpec as P

HD = 64


EPSILON = 1e-05
MASKED_SCORE = -1e30
BF = jnp.bfloat16
F32 = jnp.float32
NN = (((1,), (0,)), ((), ()))
NT = (((1,), (1,)), ((), ()))
VMEM_BYTES = 60 << 20
DP, TENSOR = "dp", "tensor"


def layer_norm(values, gain):
    centre = values - jnp.mean(values, axis=-1, keepdims=True)
    spread = jnp.mean(centre * centre, axis=-1, keepdims=True)
    return centre * lax.rsqrt(spread + EPSILON) * gain


def rotate(values, cosine, sine):
    quarter = cosine.shape[-1]
    first_part = values[..., :quarter]
    second_part = values[..., quarter : 2 * quarter]
    rest_part = values[..., 2 * quarter :]
    return jnp.concatenate(
        [
            first_part * cosine - second_part * sine,
            first_part * sine + second_part * cosine,
            rest_part,
        ],
        axis=-1,
    )


def rotate_back(grads, cosine, sine):
    quarter = cosine.shape[-1]
    first_part = grads[..., :quarter]
    second_part = grads[..., quarter : 2 * quarter]
    rest_part = grads[..., 2 * quarter :]
    return jnp.concatenate(
        [
            first_part * cosine + second_part * sine,
            second_part * cosine - first_part * sine,
            rest_part,
        ],
        axis=-1,
    )


def gated(gate_vals, up_vals):
    return jax.nn.silu(gate_vals) * up_vals


def rows_by_rows(left, right):
    return lax.dot_general(
        left, right, (((0,), (0,)), ((), ())), preferred_element_type=jnp.float32
    )


def times_transposed(left, right):
    return lax.dot_general(
        left, right, (((1,), (1,)), ((), ())), preferred_element_type=jnp.float32
    )


def attend_forward(query_rows, key_rows, value_rows, allowed):
    scores = jnp.einsum("qhd,khd->hqk", query_rows, key_rows, preferred_element_type=jnp.float32)
    scores = jnp.where(allowed[None, None, :], scores, MASKED_SCORE)
    top_score = jnp.max(scores, axis=-1, keepdims=True)
    weights = jnp.exp(scores - top_score)
    totals = jnp.sum(weights, axis=-1, keepdims=True)
    probs = weights / totals
    mixed = jnp.einsum(
        "hqk,khd->qhd", probs.astype(jnp.bfloat16), value_rows, preferred_element_type=jnp.float32
    )
    return (mixed.astype(jnp.bfloat16), top_score + jnp.log(totals))


def attend_backward(query_rows, key_rows, value_rows, allowed, log_total, grad_mixed):
    scores = jnp.einsum("qhd,khd->hqk", query_rows, key_rows, preferred_element_type=jnp.float32)
    scores = jnp.where(allowed[None, None, :], scores, MASKED_SCORE)
    probs = jnp.exp(scores - log_total)
    grad_probs = jnp.einsum(
        "qhd,khd->hqk", grad_mixed, value_rows, preferred_element_type=jnp.float32
    )
    grad_values = jnp.einsum(
        "hqk,qhd->khd", probs.astype(jnp.bfloat16), grad_mixed, preferred_element_type=jnp.float32
    )
    grad_scores = probs * (grad_probs - jnp.sum(probs * grad_probs, axis=-1, keepdims=True))
    grad_scores = grad_scores.astype(jnp.bfloat16)
    grad_query = jnp.einsum(
        "hqk,khd->qhd", grad_scores, key_rows, preferred_element_type=jnp.float32
    )
    grad_keys = jnp.einsum(
        "hqk,qhd->khd", grad_scores, query_rows, preferred_element_type=jnp.float32
    )
    return (grad_query, grad_keys, grad_values)


def general_body(
    block_in,
    cond_tokens,
    cond_count,
    norm1_gain,
    norm2_gain,
    norm3_gain,
    qkv_weight,
    attn_out_weight,
    cross_q_weight,
    cross_kv_weight,
    cross_out_weight,
    gate_up_weight,
    down_weight,
    out_cotangent,
):
    local_rows = block_in.shape[0]
    model_width = block_in.shape[1]
    group_rows = local_rows * lax.axis_size(TENSOR)
    seq_here = cond_tokens.shape[0]
    seq_length = group_rows // seq_here
    cond_slots = cond_tokens.shape[1]
    cond_width = cond_tokens.shape[2]
    head_cols = attn_out_weight.shape[0]
    heads_here = head_cols // HD
    hidden_here = down_weight.shape[0]
    gain_one, gain_two, gain_three, w_qkv, w_out, w_cq, w_ckv, w_co, w_gu, w_down = (
        lax.all_gather(norm1_gain, DP, axis=0, tiled=True),
        lax.all_gather(norm2_gain, DP, axis=0, tiled=True),
        lax.all_gather(norm3_gain, DP, axis=0, tiled=True),
        lax.all_gather(qkv_weight, DP, axis=0, tiled=True),
        lax.all_gather(attn_out_weight, DP, axis=1, tiled=True),
        lax.all_gather(cross_q_weight, DP, axis=0, tiled=True),
        lax.all_gather(cross_kv_weight, DP, axis=0, tiled=True),
        lax.all_gather(cross_out_weight, DP, axis=1, tiled=True),
        lax.all_gather(gate_up_weight, DP, axis=0, tiled=True),
        lax.all_gather(down_weight, DP, axis=1, tiled=True),
    )
    quarter = HD // 4
    positions = (jnp.arange(group_rows) % seq_length).astype(jnp.float32)
    inverse = 10000.0 ** (-jnp.arange(quarter).astype(jnp.float32) / quarter)
    angle_grid = positions[:, None] * inverse[None, :]
    cosine = jnp.cos(angle_grid)[:, None, :]
    sine = jnp.sin(angle_grid)[:, None, :]
    every_key = jnp.ones((seq_length,), dtype=jnp.bool_)
    valid_slots = jnp.arange(cond_slots)[None, :] < cond_count[:, None]

    def by_sequence(array):
        return array.reshape((seq_here, seq_length) + array.shape[1:])

    def spread_rows(local_part):
        return lax.all_gather(local_part, TENSOR, axis=0, tiled=True)

    def project_out(mixed_all, weight):
        return lax.psum_scatter(
            jnp.dot(mixed_all, weight, preferred_element_type=jnp.float32),
            TENSOR,
            scatter_dimension=0,
            tiled=True,
        )

    def spread_grads(local_part):
        return lax.all_gather(local_part, TENSOR, axis=0, tiled=True)

    def gather_back(grad_all, weight):
        return lax.psum_scatter(
            times_transposed(grad_all, weight), TENSOR, scatter_dimension=0, tiled=True
        )

    def self_forward(seq_parts):
        return attend_forward(seq_parts[0], seq_parts[1], seq_parts[2], every_key)

    def cross_forward(seq_parts):
        return attend_forward(seq_parts[0], seq_parts[1][:, 0], seq_parts[1][:, 1], seq_parts[2])

    def self_backward(seq_parts):
        return attend_backward(
            seq_parts[0], seq_parts[1], seq_parts[2], every_key, seq_parts[3], seq_parts[4]
        )

    def cross_backward(seq_parts):
        return attend_backward(
            seq_parts[0],
            seq_parts[1][:, 0],
            seq_parts[1][:, 1],
            seq_parts[2],
            seq_parts[3],
            seq_parts[4],
        )

    gain_first = gain_one.astype(jnp.float32)
    gain_second = gain_two.astype(jnp.float32)
    gain_third = gain_three.astype(jnp.float32)
    input_rows = block_in.astype(jnp.float32)
    first_all = spread_rows(layer_norm(input_rows, gain_first).astype(jnp.bfloat16))
    qkv_all = jnp.dot(
        first_all, w_qkv.reshape(model_width, 3 * head_cols), preferred_element_type=jnp.float32
    )
    qkv_all = qkv_all.reshape(group_rows, 3, heads_here, HD)
    query_rot = (rotate(qkv_all[:, 0], cosine, sine) * 0.125).astype(jnp.bfloat16)
    key_rot = rotate(qkv_all[:, 1], cosine, sine).astype(jnp.bfloat16)
    value_rows = qkv_all[:, 2].astype(jnp.bfloat16)
    self_mixed, self_lse = lax.map(
        self_forward, (by_sequence(query_rot), by_sequence(key_rot), by_sequence(value_rows))
    )
    self_flat = self_mixed.reshape(group_rows, head_cols)
    after_self = input_rows + project_out(self_flat, w_out)
    second_all = spread_rows(layer_norm(after_self, gain_second).astype(jnp.bfloat16))
    cross_query = (jnp.dot(second_all, w_cq, preferred_element_type=jnp.float32) * 0.125).astype(
        jnp.bfloat16
    )
    cross_query = cross_query.reshape(group_rows, heads_here, HD)
    cond_flat = cond_tokens.reshape(seq_here * cond_slots, cond_width)
    cross_kv = jnp.dot(
        cond_flat, w_ckv.reshape(cond_width, 2 * head_cols), preferred_element_type=jnp.float32
    )
    cross_kv = cross_kv.astype(jnp.bfloat16).reshape(seq_here, cond_slots, 2, heads_here, HD)
    cross_mixed, cross_lse = lax.map(
        cross_forward, (by_sequence(cross_query), cross_kv, valid_slots)
    )
    cross_flat = cross_mixed.reshape(group_rows, head_cols)
    after_cross = after_self + project_out(cross_flat, w_co)
    third_all = spread_rows(layer_norm(after_cross, gain_third).astype(jnp.bfloat16))
    gate_up = jnp.dot(
        third_all, w_gu.reshape(model_width, 2 * hidden_here), preferred_element_type=jnp.float32
    )
    gate_up = gate_up.reshape(group_rows, 2, hidden_here)
    gate_vals = gate_up[:, 0]
    up_vals = gate_up[:, 1]
    hidden = gated(gate_vals, up_vals).astype(jnp.bfloat16)
    block_out = (after_cross + project_out(hidden, w_down)).astype(jnp.bfloat16)
    gain_one, gain_two, gain_three, w_qkv, w_out, w_cq, w_ckv, w_co, w_gu, w_down = (
        lax.all_gather(norm1_gain, DP, axis=0, tiled=True),
        lax.all_gather(norm2_gain, DP, axis=0, tiled=True),
        lax.all_gather(norm3_gain, DP, axis=0, tiled=True),
        lax.all_gather(qkv_weight, DP, axis=0, tiled=True),
        lax.all_gather(attn_out_weight, DP, axis=1, tiled=True),
        lax.all_gather(cross_q_weight, DP, axis=0, tiled=True),
        lax.all_gather(cross_kv_weight, DP, axis=0, tiled=True),
        lax.all_gather(cross_out_weight, DP, axis=1, tiled=True),
        lax.all_gather(gate_up_weight, DP, axis=0, tiled=True),
        lax.all_gather(down_weight, DP, axis=1, tiled=True),
    )
    gain_first = gain_one.astype(jnp.float32)
    gain_second = gain_two.astype(jnp.float32)
    gain_third = gain_three.astype(jnp.float32)
    grad_top = out_cotangent.astype(jnp.float32)
    third_grads = spread_grads(out_cotangent)
    grad_hidden = times_transposed(third_grads, w_down)
    grad_down = rows_by_rows(hidden, third_grads)
    gated_out, gated_pull = jax.vjp(gated, gate_vals, up_vals)
    grad_gate, grad_up = gated_pull(grad_hidden)
    grad_gate_up = (
        jnp.stack([grad_gate, grad_up], axis=1)
        .astype(jnp.bfloat16)
        .reshape(group_rows, 2 * hidden_here)
    )
    grad_gu_weight = rows_by_rows(third_all, grad_gate_up).reshape(model_width, 2, hidden_here)
    grad_third = gather_back(grad_gate_up, w_gu.reshape(model_width, 2 * hidden_here))
    norm_out, norm_pull = jax.vjp(layer_norm, after_cross, gain_third)
    part_rows, grad_gain_third = norm_pull(grad_third)
    grad_cross_rows = grad_top + part_rows
    second_grads = spread_grads(grad_cross_rows.astype(jnp.bfloat16))
    grad_cross_mixed = times_transposed(second_grads, w_co).astype(jnp.bfloat16)
    grad_co_weight = rows_by_rows(cross_flat, second_grads)
    cross_gq, cross_gk, cross_gv = lax.map(
        cross_backward,
        (
            by_sequence(cross_query),
            cross_kv,
            valid_slots,
            cross_lse,
            by_sequence(grad_cross_mixed.reshape(group_rows, heads_here, HD)),
        ),
    )
    grad_cross_query = (cross_gq * 0.125).astype(jnp.bfloat16).reshape(group_rows, head_cols)
    grad_cross_kv = (
        jnp.stack([cross_gk, cross_gv], axis=2)
        .astype(jnp.bfloat16)
        .reshape(seq_here * cond_slots, 2 * head_cols)
    )
    grad_cq_weight = rows_by_rows(second_all, grad_cross_query)
    grad_ckv_weight = rows_by_rows(cond_flat, grad_cross_kv).reshape(cond_width, 2, head_cols)
    cond_partial = times_transposed(
        grad_cross_kv, w_ckv.reshape(cond_width, 2 * head_cols)
    ).reshape(seq_here, cond_slots, cond_width)
    grad_cond = lax.psum_scatter(cond_partial, TENSOR, scatter_dimension=2, tiled=True)
    grad_second = gather_back(grad_cross_query, w_cq)
    norm_out, norm_pull = jax.vjp(layer_norm, after_self, gain_second)
    part_rows, grad_gain_second = norm_pull(grad_second)
    grad_self_rows = grad_cross_rows + part_rows
    first_grads = spread_grads(grad_self_rows.astype(jnp.bfloat16))
    grad_self_mixed = times_transposed(first_grads, w_out).astype(jnp.bfloat16)
    grad_out_weight = rows_by_rows(self_flat, first_grads)
    self_gq, self_gk, self_gv = lax.map(
        self_backward,
        (
            by_sequence(query_rot),
            by_sequence(key_rot),
            by_sequence(value_rows),
            self_lse,
            by_sequence(grad_self_mixed.reshape(group_rows, heads_here, HD)),
        ),
    )
    grad_query = rotate_back(self_gq.reshape(group_rows, heads_here, HD) * 0.125, cosine, sine)
    grad_keys = rotate_back(self_gk.reshape(group_rows, heads_here, HD), cosine, sine)
    grad_values = self_gv.reshape(group_rows, heads_here, HD)
    grad_qkv_all = (
        jnp.stack([grad_query, grad_keys, grad_values], axis=1)
        .astype(jnp.bfloat16)
        .reshape(group_rows, 3 * head_cols)
    )
    grad_qkv_weight = rows_by_rows(first_all, grad_qkv_all).reshape(model_width, 3, head_cols)
    grad_first = gather_back(grad_qkv_all, w_qkv.reshape(model_width, 3 * head_cols))
    norm_out, norm_pull = jax.vjp(layer_norm, input_rows, gain_first)
    part_rows, grad_gain_first = norm_pull(grad_first)
    grad_input = grad_self_rows + part_rows
    owned = (
        lax.psum_scatter(grad_gain_first, DP, scatter_dimension=0, tiled=True),
        lax.psum_scatter(grad_gain_second, DP, scatter_dimension=0, tiled=True),
        lax.psum_scatter(grad_gain_third, DP, scatter_dimension=0, tiled=True),
        lax.psum_scatter(grad_qkv_weight, DP, scatter_dimension=0, tiled=True),
        lax.psum_scatter(grad_out_weight, DP, scatter_dimension=1, tiled=True),
        lax.psum_scatter(grad_cq_weight, DP, scatter_dimension=0, tiled=True),
        lax.psum_scatter(grad_ckv_weight, DP, scatter_dimension=0, tiled=True),
        lax.psum_scatter(grad_co_weight, DP, scatter_dimension=1, tiled=True),
        lax.psum_scatter(grad_gu_weight, DP, scatter_dimension=0, tiled=True),
        lax.psum_scatter(grad_down, DP, scatter_dimension=1, tiled=True),
    )
    gain_grads = lax.psum((owned[0], owned[1], owned[2]), TENSOR)
    return (
        block_out,
        grad_input,
        grad_cond,
        gain_grads[0],
        gain_grads[1],
        gain_grads[2],
        owned[3],
        owned[4],
        owned[5],
        owned[6],
        owned[7],
        owned[8],
        owned[9],
    )


def general_solution(mesh):
    return jax.shard_map(
        general_body,
        mesh=mesh,
        in_specs=(
            P((DP, TENSOR), None),
            P(DP, None, None),
            P(DP),
            P(DP),
            P(DP),
            P(DP),
            P(DP, None, TENSOR),
            P(TENSOR, DP),
            P(DP, TENSOR),
            P(DP, None, TENSOR),
            P(TENSOR, DP),
            P(DP, None, TENSOR),
            P(TENSOR, DP),
            P((DP, TENSOR), None),
        ),
        out_specs=(
            P((DP, TENSOR), None),
            P((DP, TENSOR), None),
            P(DP, None, TENSOR),
            P(DP),
            P(DP),
            P(DP),
            P(DP, None, TENSOR),
            P(TENSOR, DP),
            P(DP, TENSOR),
            P(DP, None, TENSOR),
            P(TENSOR, DP),
            P(DP, None, TENSOR),
            P(TENSOR, DP),
        ),
        check_vma=False,
    )


def dot(left, right, dims=NN):
    return lax.dot_general(left, right, dims, preferred_element_type=F32)


def iota(shape, axis):
    return lax.broadcasted_iota(jnp.int32, shape, axis)


def whole(shape):
    return pl.BlockSpec(shape, lambda *p: (0,) * len(shape), pipeline_mode=pl.Buffered(1))


def columns_of(rows, first=0):
    return pl.BlockSpec((rows, 128), lambda p, s: (0, first + p))


SCALAR = pl.BlockSpec(memory_space=pltpu.SMEM)


def shaped(shape, dtype):
    return jax.ShapeDtypeStruct(shape, dtype)


def call(kernel, grid, ins, outs, name, micros, scratch=(), after=(), scalars=None):
    lead = 0 if scalars is None else 1

    def without_after(*refs):
        kernel(*refs[: lead + len(ins)], *refs[lead + len(ins) + len(after) :])

    in_specs = [spec for spec, _ in ins] + [pl.BlockSpec(memory_space=pl.ANY)] * len(after)
    out_specs = [spec for spec, _ in outs]
    if lead:
        how = dict(
            grid_spec=pltpu.PrefetchScalarGridSpec(
                num_scalar_prefetch=1, grid=grid, in_specs=in_specs, out_specs=out_specs,
                scratch_shapes=list(scratch),
            )
        )
    else:
        how = dict(
            grid=grid, in_specs=in_specs, out_specs=out_specs, scratch_shapes=list(scratch)
        )
    return pl.pallas_call(
        without_after,
        **how,
        out_shape=[shape for _, shape in outs],
        compiler_params=pltpu.CompilerParams(vmem_limit_bytes=VMEM_BYTES),
        cost_estimate=pl.CostEstimate(
            flops=int(micros * FLOPS), bytes_accessed=0, transcendentals=0
        ),
        name=name,
    )(*([] if scalars is None else [scalars]), *[array for _, array in ins], *after)


def unravel(shard):
    size = 4 * shard
    source, target = iota((size, size), 0), iota((size, size), 1)
    z, core, at = source // (2 * shard), (source // shard) % 2, source % shard
    return jnp.where(core * 2 * shard + z * shard + at == target, 1.0, 0.0).astype(BF)


def put_in_order(values, turn, odd):
    size = turn.shape[0]
    own, other = [], []
    for at in range(0, values.shape[1], size):
        both = dot(values[:, at : at + size], turn)
        even, odds = both[:, : size // 2], both[:, size // 2 :]
        own.append(jnp.where(odd, odds, even))
        other.append(jnp.where(odd, even, odds))
    return jnp.concatenate(own + other, axis=1)


def put_back(values, turn, odd, parts):
    size = turn.shape[0]
    middle = values.shape[1] // 2
    result = []
    for at in range(0, middle, size // 2):
        own = values[:, at : at + size // 2]
        other = values[:, middle + at : middle + at + size // 2]
        both = jnp.concatenate(
            [jnp.where(odd, other, own), jnp.where(odd, own, other)], axis=1
        )
        total = None
        for _ in range(parts):
            term = both.astype(BF)
            moved = dot(term, turn, NT)
            total = moved if total is None else total + moved
            both = both - term.astype(F32)
        result.append(total)
    return jnp.concatenate(result, axis=1)


def hold(array, after):
    anywhere = pl.BlockSpec(memory_space=pl.ANY)
    return pl.pallas_call(
        lambda *refs: None,
        in_specs=[anywhere] * (1 + len(after)),
        out_specs=anywhere,
        out_shape=shaped(array.shape, array.dtype),
        input_output_aliases={0: 0},
        cost_estimate=pl.CostEstimate(flops=0, bytes_accessed=0, transcendentals=0),
        name="hold",
    )(array, *after)


def normalize(values):
    centre = values - jnp.mean(values, axis=-1, keepdims=True)
    scale = lax.rsqrt(jnp.mean(centre * centre, axis=-1, keepdims=True) + EPSILON)
    return centre * scale, scale


def normalize_back(grads, gain, normal, scale):
    inner = grads * gain
    return (
        inner
        - jnp.mean(inner, axis=-1, keepdims=True)
        - normal * jnp.mean(inner * normal, axis=-1, keepdims=True)
    ) * scale


def first_norm(ref, base, gains_ref, out_ref, across_ref):
    step = 256
    for at in range(0, ref.shape[0], step):
        normal, _ = normalize(ref[at : at + step, :].astype(F32))
        out = (normal * gains_ref[0:1, :]).astype(BF)
        out_ref[base + at : base + at + step, :] = out
        across_ref[:, base + at : base + at + step] = jnp.transpose(out)


QKV_CHAINS = (("z2", "y", "z1", "c"), ("z1", "z2", "y", "c"))
SQUARE_CHAINS = (
    ("x", "z1", "y", "z2", "c"),
    ("z2", "y", "x", "z1", "c"),
    ("z2", "z1", "x", "y", "c"),
    ("y", "z2", "z1", "x", "c"),
)
AXES = ("z2", "z1", "c", "y", "x")
STEPS = (
    "S0.0", "S3.0", "g0", "S2.0", "S1.0", "Q1.0", "g1", "tops", "S1.1", "Q0.0", "g2", "norm",
    "S0.1", "S3.1", "Q0.1", "in", "S2.1", "norms", "S1.2", "S0.2", "Q1.1", "pack", "S2.2",
    "S3.2", "Q1.2", "Q1.3", "Q0.2", "Q0.3", "S3.3", "S2.3", "S3.4", "S0.3", "S2.4", "S1.3",
    "S0.4", "S1.4",
)


def gather_kernel(
    qkv_ref, square_ref, gains_ref, rows_ref, tops_ref, gu_ref, down_ref,
    wq_ref, w0_ref, w1_ref, w2_ref, w3_ref,
    mine_ref, theirs_ref, tops_out, gains_out, first_ref, across_ref, turn_ref,
    *rest,
):
    *pack_refs, sum_ref, slot_ref, sends, receives, local_sems = rest
    dp, seq, side = (lax.axis_index(name) for name in ("dp", "seq", "half"))
    here = {"z2": dp // 4, "z1": (dp // 2) % 2, "c": dp % 2, "y": seq, "x": side}
    partners = {
        "z2": (dp + 4 - 8 * (dp // 4), seq, side),
        "z1": (dp + 2 - 4 * ((dp // 2) % 2), seq, side),
        "c": (dp + 1 - 2 * (dp % 2), seq, side),
        "y": (dp, 1 - seq, side),
        "x": (dp, seq, 1 - side),
    }
    barrier = pltpu.get_barrier_semaphore()
    for axis in AXES:
        pl.semaphore_signal(
            barrier, inc=1, device_id=partners[axis], device_id_type=pl.DeviceIdType.MESH
        )
    pl.semaphore_wait(barrier, len(AXES))
    count = [0]

    def send(source, target, axis):
        copy = pltpu.make_async_remote_copy(
            source, target, sends.at[count[0]], receives.at[count[0]],
            device_id=partners[axis], device_id_type=pl.DeviceIdType.MESH,
        )
        count[0] += 1
        copy.start()
        return copy

    chains = {}
    columns = qkv_ref.shape[1]
    cut = columns // 2 // 128 * 128 + 128
    for at, (order, low, high) in enumerate(
        ((QKV_CHAINS[0], 0, cut), (QKV_CHAINS[1], cut, columns))
    ):
        chains["Q%d" % at] = (wq_ref, qkv_ref, low, high, order, AXES[:4])
    wide = square_ref.shape[1] // 4
    for at, (order, ref) in enumerate(zip(SQUARE_CHAINS, (w0_ref, w1_ref, w2_ref, w3_ref))):
        chains["S%d" % at] = (ref, square_ref, at * wide, (at + 1) * wide, order, AXES)

    own_copies = {}

    def region(name, step):
        ref, _, low, high, order, axes = chains[name]
        grown = order[:step]
        index = tuple(slice(None) if axis in grown else here[axis] for axis in axes)
        if name[0] == "Q":
            index += (slice(None), slice(low, high))
        return ref.at[index]

    def begin(name, step):
        _, source, low, high, order, _ = chains[name]
        if step == 0:
            part = source.at[:, slice(low, high)]
            copy = pltpu.make_async_copy(part, region(name, 0), local_sems.at[len(own_copies)])
            copy.start()
            own_copies[name] = copy
            return send(part, region(name, 0), order[0])
        if step == 1:
            own_copies[name].wait()
        return send(region(name, step), region(name, step), order[step])

    flying = {}
    for event in STEPS:
        if event.endswith(".0"):
            flying[event[:2]] = begin(event[:2], 0)
    odd = here["c"] == 1
    turn_ref[...] = unravel(qkv_ref.shape[0])
    turn = turn_ref[...]
    mine_ref[...] = put_in_order(rows_ref[...], turn, odd).astype(BF)
    their_rows = send(mine_ref, theirs_ref, "x")
    sum_ref[...] = gains_ref[...]
    gain_axes = ("c", "z1", "z2")
    gain_copy = send(sum_ref, slot_ref.at[0], gain_axes[0])

    for event in STEPS:
        if event[0] == "g":
            at = int(event[1])
            gain_copy.wait()
            sum_ref[...] += slot_ref[at]
            if at < 2:
                gain_copy = send(sum_ref, slot_ref.at[at + 1], gain_axes[at + 1])
            else:
                gains_out[...] = put_in_order(sum_ref[...].astype(BF), turn, odd)
            continue
        if event == "tops":
            tops_out[...] = put_in_order(tops_ref[...], turn, odd).astype(BF)
            continue
        if event == "pack":
            pack_parts(gu_ref, down_ref, pack_refs)
            continue
        if event == "norm":
            first_norm(mine_ref, 0, gains_out, first_ref, across_ref)
            continue
        if event == "norms":
            first_norm(theirs_ref, theirs_ref.shape[0], gains_out, first_ref, across_ref)
            continue
        if event == "in":
            their_rows.wait()
            continue
        name, step = event.split(".")
        flying[name].wait()
        if int(step) + 1 < len(chains[name][4]):
            flying[name] = begin(name, int(step) + 1)


def pack_parts(gu_ref, down_ref, pack_refs):
    hidden = down_ref.shape[1]
    tiles = hidden // len(pack_refs) // TILE
    for i, pack_ref in enumerate(pack_refs):
        for j in range(tiles):
            at, low = 3 * j * TILE, (i * tiles + j) * TILE
            pack_ref[:, at : at + TILE] = gu_ref[:, low : low + TILE]
            pack_ref[:, at + TILE : at + 2 * TILE] = gu_ref[:, hidden + low : hidden + low + TILE]
            pack_ref[:, at + 2 * TILE : at + 3 * TILE] = down_ref[:, low : low + TILE]


def gather_first(qkv, square, gains, rows, tops, gate_up, down):
    anywhere, vmem = pl.BlockSpec(memory_space=pl.ANY), pl.BlockSpec(memory_space=pltpu.VMEM)
    shard = qkv.shape[0]
    wide = square.shape[1] // 4
    count, width = rows.shape
    copies = 4 * 2 + 5 * 4 + 1 + 3
    return pl.pallas_call(
        gather_kernel,
        in_specs=[anywhere, anywhere] + [vmem] * 5,
        out_specs=[anywhere] * 5 + [vmem] * (7 + CHUNKS),
        out_shape=[shaped((2, 2, 2, 2) + qkv.shape, BF)]
        + [shaped((2, 2, 2, 2, 2, shard, wide), BF)] * 4
        + [shaped(rows.shape, BF)] * 3
        + [shaped(gains.shape, F32), shaped((2 * count, width), BF), shaped((width, 2 * count), BF)]
        + [shaped((4 * shard, 4 * shard), BF)]
        + [shaped((shard, 3 * down.shape[1] // CHUNKS), BF)] * CHUNKS,
        scratch_shapes=[
            pltpu.VMEM(gains.shape, F32),
            pltpu.VMEM((3,) + gains.shape, F32),
            pltpu.SemaphoreType.DMA((copies,)),
            pltpu.SemaphoreType.DMA((copies,)),
            pltpu.SemaphoreType.DMA((6,)),
        ],
        compiler_params=pltpu.CompilerParams(
            vmem_limit_bytes=VMEM_BYTES, collective_id=0, has_side_effects=True
        ),
        name="gather_first",
    )(qkv, square, gains, rows, tops, gate_up, down)


def across_kernel(*refs):
    count = len(refs) // 2
    for source, target in zip(refs[:count], refs[count:]):
        step = 256
        for at in range(0, source.shape[0], step):
            target[:, at : at + step] = jnp.transpose(source[at : at + step, :])


def across(*arrays):
    shape = arrays[0].shape
    flipped = (shape[1], shape[0])
    return call(
        across_kernel, (1,),
        [(whole(shape), array) for array in arrays],
        [(whole(flipped), shaped(flipped, BF))] * len(arrays),
        "across", 3 * len(arrays),
    )


def rot(values, tables):
    cosine, sine_up, sine_down = tables
    return (
        values * cosine
        + pltpu.roll(values, 16, 1) * sine_up
        + pltpu.roll(values, 112, 1) * sine_down
    )


def rot_back(grads, tables):
    cosine, sine_up, sine_down = tables
    return (
        grads * cosine
        - pltpu.roll(grads, 16, 1) * sine_up
        - pltpu.roll(grads, 112, 1) * sine_down
    )


def rot_tables(positions):
    quarter = HD // 4
    feature = jnp.arange(2 * HD) % HD
    inverse = 10000.0 ** (-(feature % quarter).astype(F32) / quarter)
    angle_grid = positions.astype(F32)[:, None] * inverse[None, :]
    cosine, sine = jnp.cos(angle_grid), jnp.sin(angle_grid)
    first, second = (feature < quarter)[None], ((feature // quarter) == 1)[None]
    return (
        jnp.where(first | second, cosine, 1.0),
        jnp.where(second, sine, 0.0),
        jnp.where(first, -sine, 0.0),
    )


def to_rows(picks, columns):
    first = columns.astype(BF)
    rest = columns - first.astype(F32)
    second = rest.astype(BF)
    third = (rest - second.astype(F32)).astype(BF)
    return dot(picks, first, NT) + dot(picks, second, NT) + dot(picks, third, NT)


def self_forward_kernel(
    step, place_ref, rows_ref, own_ref, other_ref, c_ref, su_ref, sd_ref,
    q_ref, k_ref, v_ref, mine_ref, theirs_ref, lse_ref,
):
    count, width = rows_ref.shape
    half = width // 2
    own, other = own_ref[...].reshape(half, 384), other_ref[...].reshape(half, 384)
    qkv = dot(rows_ref[:, :half], own) + dot(rows_ref[:, half:], other)
    tables = (c_ref[...], su_ref[...], sd_ref[...])
    query = (rot(qkv[:, :128], tables) * 0.125).astype(BF)
    key = rot(qkv[:, 128:256], tables).astype(BF)
    value = qkv[:, 256:].astype(BF)
    q_ref[...] = query
    k_ref[...] = key
    v_ref[...] = value
    lane = iota((step, 128), 1)
    picks = jnp.where(iota((8, 128), 0) == iota((8, 128), 1), 1.0, 0.0).astype(BF)
    for at in range(0, count, step):
        part = query[at : at + step]
        mixed, logs = [], []
        for head in range(2):
            here = (lane // HD) == head
            scores = dot(jnp.where(here, part, jnp.zeros_like(part)), key, NT)
            top = jnp.max(scores, axis=1, keepdims=True)
            weights = jnp.exp(scores - top)
            total = jnp.sum(weights, axis=1, keepdims=True)
            mixed.append(dot(weights.astype(BF), value) * (1.0 / total))
            logs.append(top + jnp.log(total))
        out = jnp.where(lane < HD, mixed[0], mixed[1]).astype(BF)
        both = jnp.where(lane == 0, logs[0], jnp.where(lane == 1, logs[1], 0.0))
        lse_ref[0, :, at : at + step] = to_rows(picks, both)
        if at < count // 2:
            mine_ref[at : at + step, :] = out
        else:
            theirs_ref[at - count // 2 : at - count // 2 + step, :] = out


def self_weights(weights, first=0):
    shape = (weights.shape[0], 1, 1, weights.shape[3], 384)
    return [
        (pl.BlockSpec(shape, lambda p, s: (0, s[0], p % 2, 0, first // 2 + p // 2)), weights),
        (pl.BlockSpec(shape, lambda p, s: (0, 1 - s[0], p % 2, 0, first // 2 + p // 2)), weights),
    ]


def self_forward(place, rows, weights, tables, after=()):
    count, width = rows.shape
    wide = weights.shape[2] * weights.shape[4] // 3
    pairs = wide // 128
    return call(
        functools.partial(self_forward_kernel, 512),
        (pairs,),
        [(whole(rows.shape), rows)] + self_weights(weights)
        + [(whole((count, 128)), table) for table in tables],
        [(columns_of(count), shaped((count, wide), BF))] * 3
        + [(columns_of(count // 2), shaped((count // 2, wide), BF))] * 2
        + [(pl.BlockSpec((1, 8, count), lambda p, s: (p, 0, 0)), shaped((pairs, 8, count), F32))],
        "self_forward", 7 * pairs,
        after=after,
        scalars=place,
    )


def self_backward_kernel(
    step, begins, ends, place_ref, q_ref, k_ref, v_ref, mine_ref, theirs_ref, dmine_ref, dtheirs_ref, lse_ref,
    c_ref, su_ref, sd_ref, across_ref, own_ref, other_ref, *rest,
):
    if begins:
        gown_ref, gother_ref, *outs, qkv_ref, sum_ref = rest
    else:
        start_ref, gown_ref, gother_ref, *outs, qkv_ref, sum_ref = rest
    count = q_ref.shape[0]
    query = q_ref[...]
    grads = jnp.concatenate([dmine_ref[...], dtheirs_ref[...]], axis=0)
    mixed = jnp.concatenate([mine_ref[...], theirs_ref[...]], axis=0)
    picks = jnp.where((iota((8, 128), 1) // HD) == iota((8, 128), 0), 1.0, 0.0).astype(BF)
    delta = to_rows(picks, grads.astype(F32) * mixed.astype(F32))
    lane = iota((step, 128), 1)
    row = iota((128, step), 0)
    keys_across = jnp.transpose(k_ref[...].astype(F32)).astype(BF)
    query_across = jnp.zeros((128, count), F32)
    tables = (c_ref[...], su_ref[...], sd_ref[...])
    for at in range(0, count, step):
        here = slice(at, at + step)
        key, value = k_ref[here, :], v_ref[here, :]
        flipped = keys_across[:, here]
        dkeys, dvalues = [], []
        for head in range(2):
            inside = (lane // HD) == head
            scores = dot(jnp.where(inside, key, jnp.zeros_like(key)), query, NT)
            probs = jnp.exp(scores - lse_ref[0, head : head + 1, :])
            dprobs = dot(jnp.where(inside, value, jnp.zeros_like(value)), grads, NT)
            dscores = (probs * (dprobs - delta[head : head + 1, :])).astype(BF)
            dvalues.append(dot(probs.astype(BF), grads))
            dkeys.append(dot(dscores, query))
            picked = jnp.where((row // HD) == head, flipped, jnp.zeros_like(flipped))
            query_across = query_across + dot(picked, dscores)
        dkey = jnp.where(lane < HD, dkeys[0], dkeys[1])
        dvalue = jnp.where(lane < HD, dvalues[0], dvalues[1])
        qkv_ref[here, 128:256] = rot_back(dkey, [t[here] for t in tables]).astype(BF)
        qkv_ref[here, 256:384] = dvalue.astype(BF)
    dquery = jnp.transpose(query_across)
    qkv_ref[:, 0:128] = (rot_back(dquery, tables) * 0.125).astype(BF)

    first = pl.program_id(0) == 0
    last = pl.program_id(0) == pl.num_programs(0) - 1
    half = across_ref.shape[0] // 2
    own, other = own_ref[...].reshape(half, 384), other_ref[...].reshape(half, 384)
    both = qkv_ref[...]
    gown_ref[0] = dot(across_ref[:half, :], both).astype(BF)
    gother_ref[0] = dot(across_ref[half:, :], both).astype(BF)
    back = jnp.concatenate([dot(both, own, NT), dot(both, other, NT)], axis=1)

    @pl.when(first)
    def _():
        sum_ref[...] = back if begins else start_ref[...] + back

    @pl.when(jnp.logical_not(first))
    def _():
        sum_ref[...] += back

    @pl.when(last)
    def _():
        if ends:
            outs[0][...] = sum_ref[: count // 2, :].astype(BF)
            outs[1][...] = sum_ref[count // 2 :, :].astype(BF)
        else:
            outs[0][...] = sum_ref[...]


def self_backward(
    place, query, key, value, mine, theirs, dmine, dtheirs, lse, tables, flipped, weights, first, pairs,
    start, ends, after=(),
):
    count = query.shape[0]
    wide = 128 * pairs
    width = flipped.shape[0]
    out = pl.BlockSpec((1, width // 2, 384), lambda p, s: (p % 2, 0, p // 2))
    out_shape = (2, width // 2, 192 * pairs)
    rows, half = columns_of(count, first), columns_of(count // 2, first)
    half_rows = (count // 2, width)
    all_rows = (count, width)
    if ends:
        sums = [(whole(half_rows), shaped(half_rows, BF))] * 2
    else:
        sums = [(whole(all_rows), shaped(all_rows, F32))]
    starts = [] if start is None else [(whole(all_rows), start)]
    return call(
        functools.partial(self_backward_kernel, 512, start is None, ends),
        (pairs,),
        [(rows, array) for array in (query, key, value)]
        + [(half, array) for array in (mine, theirs, dmine, dtheirs)]
        + [(pl.BlockSpec((1, 8, count), lambda p, s: (first + p, 0, 0)), lse)]
        + [(whole((count, 128)), table) for table in tables]
        + [(whole(flipped.shape), flipped)] + self_weights(weights, first) + starts,
        [(out, shaped(out_shape, BF))] * 2 + sums,
        "self_backward", 13 * pairs,
        scratch=[pltpu.VMEM((count, 384), BF), pltpu.VMEM((count, width), F32)],
        after=after,
        scalars=place,
    )


def ffn_kernel(
    tile, carried, place_ref, mine_ref, theirs_ref, fmine_ref, ftheirs_ref,
    tmine_ref, ttheirs_ref, gmine_ref, gtheirs_ref, *rest,
):
    weight_refs, rest = rest[: len(rest) - 4 * carried - 8], rest[len(rest) - 4 * carried - 8 :]
    starts, rest = rest[: 4 * carried], rest[4 * carried :]
    ymine_ref, ytheirs_ref, dmine_ref, dtheirs_ref, gown_ref, gother_ref, y_ref, d_ref = rest
    rows, width = mine_ref.shape
    half = width // 2
    both = 2 * tile
    first = pl.program_id(0) == 0
    last = pl.program_id(0) == pl.num_programs(0) - 1

    @pl.when(first)
    def _():
        if carried:
            for part in range(2):
                y_ref[part] = starts[part][...].astype(F32)
                d_ref[part] = starts[2 + part][...].astype(F32)
        else:
            y_ref[...] = jnp.zeros_like(y_ref)
            d_ref[...] = jnp.zeros_like(d_ref)

    if len(weight_refs) == 2:
        own, other = (ref[...] for ref in weight_refs)
    else:
        nearer = pl.program_id(0) < pl.num_programs(0) // 2
        own = jnp.where(nearer, weight_refs[0][...], weight_refs[1][...])
        other = jnp.where(nearer, weight_refs[2][...], weight_refs[3][...])
    own, other = own.reshape(half, 3 * tile), other.reshape(half, 3 * tile)
    hidden_parts, dgate_up_parts = [], []
    for part, (ref, top_ref) in enumerate(((mine_ref, tmine_ref), (theirs_ref, ttheirs_ref))):
        gate_up = dot(ref[:, :half], own[:, :both]) + dot(ref[:, half:], other[:, :both])
        dhidden = dot(top_ref[:, :half], own[:, both:]) + dot(top_ref[:, half:], other[:, both:])
        gate, up = gate_up[:, :tile], gate_up[:, tile:]
        sigma = 1.0 / (1.0 + jnp.exp(-gate))
        silu = gate * sigma
        hidden = (silu * up).astype(BF)
        dup = (dhidden * silu).astype(BF)
        dgate = (dhidden * up * (sigma * (1.0 + gate * (1.0 - sigma)))).astype(BF)
        dgate_up = jnp.concatenate([dgate, dup], axis=1)
        y_ref[part, :, :half] += dot(hidden, own[:, both:], NT)
        y_ref[part, :, half:] += dot(hidden, other[:, both:], NT)
        d_ref[part, :, :half] += dot(dgate_up, own[:, :both], NT)
        d_ref[part, :, half:] += dot(dgate_up, other[:, :both], NT)
        hidden_parts.append(hidden)
        dgate_up_parts.append(dgate_up)
    for out, cut in ((gown_ref, slice(0, half)), (gother_ref, slice(half, width))):
        out[0, :, :both] = (
            dot(fmine_ref[cut, :], dgate_up_parts[0]) + dot(ftheirs_ref[cut, :], dgate_up_parts[1])
        ).astype(BF)
        out[0, :, both:] = (
            dot(gmine_ref[cut, :], hidden_parts[0]) + dot(gtheirs_ref[cut, :], hidden_parts[1])
        ).astype(BF)

    @pl.when(last)
    def _():
        ymine_ref[...] = y_ref[0].astype(BF)
        ytheirs_ref[...] = y_ref[1].astype(BF)
        dmine_ref[...] = d_ref[0].astype(BF)
        dtheirs_ref[...] = d_ref[1].astype(BF)


def ffn(place, rows, flipped, tops, tops_flipped, weights, tile, starts=(), after=()):
    count, width = rows[0].shape
    several = isinstance(weights, list)
    zs, shard, wide = weights[0].shape if several else (weights.shape[:1] + weights.shape[3:])
    half = zs * shard
    tiles = wide // (3 * tile)
    groups = 2
    if several:
        near = pl.BlockSpec((zs, shard, 3 * tile), lambda p, s: (0, 0, jnp.minimum(p, tiles - 1)))
        far = pl.BlockSpec((zs, shard, 3 * tile), lambda p, s: (0, 0, jnp.maximum(p - tiles, 0)))
        matrices = list(zip((near, far, near, far), weights))
    else:
        shape = (zs, 1, 1, shard, 3 * tile)
        own = pl.BlockSpec(shape, lambda p, s: (0, s[0], p // tiles, 0, p % tiles))
        other = pl.BlockSpec(shape, lambda p, s: (0, 1 - s[0], p // tiles, 0, p % tiles))
        matrices = [(own, weights), (other, weights)]
    block = pl.BlockSpec((1, half, 3 * tile), lambda p, s: (p // tiles, 0, p % tiles))
    out = shaped((groups, half, wide), BF)
    once, fixed = whole((count, width)), whole((width, count))
    return call(
        functools.partial(ffn_kernel, tile, len(starts) // 4),
        (groups * tiles,),
        [(once, a) for a in rows] + [(fixed, a) for a in flipped]
        + [(once, a) for a in tops] + [(fixed, a) for a in tops_flipped]
        + matrices + [(once, a) for a in starts],
        [(once, shaped((count, width), BF))] * 4 + [(block, out)] * 2,
        "feed_forward", 9 * groups * tiles,
        scratch=[pltpu.VMEM((2, count, width), F32)] * 2,
        after=after,
        scalars=place,
    )


def section(square, other):
    zs, _, ys, xs, shard, wide = square.shape
    return (
        pl.BlockSpec(
            (zs, 1, ys, xs, shard, wide),
            lambda *a: (0, 1 - a[-1][0] if other else a[-1][0], 0, 0, 0, 0),
            pipeline_mode=pl.Buffered(1),
        ),
        square,
    )


def sections(squares):
    return [section(squares[n], other) for n in (0, 1, 3) for other in (False, True)]


def weight_of(ref, x, y):
    zs, _, _, _, shard, wide = ref.shape
    return ref[:, 0, y, x].reshape(zs * shard, wide)


def cond_kernel(place_ref, cond_ref, own_ref, other_ref, key_ref, value_ref):
    shard = cond_ref.shape[1] // 8
    half = 4 * shard
    wide = own_ref.shape[-1]
    for x in range(2):
        for y in range(2):
            at = (2 * x + y) * wide
            for kind, out in ((0, key_ref), (1, value_ref)):
                total = None
                for part, ref in ((0, own_ref), (1, other_ref)):
                    weight = ref[:, 0, y, x, kind * shard : (kind + 1) * shard, :]
                    weight = weight.reshape(half, wide)
                    term = dot(cond_ref[:, part * half : (part + 1) * half], weight)
                    total = term if total is None else total + term
                out[:, at : at + wide] = total.astype(BF)


def cond_forward(place, cond, square):
    slots, width = cond.shape
    wide = 4 * square.shape[-1]
    return call(
        cond_kernel, (1,),
        [(whole(cond.shape), cond), section(square, False), section(square, True)],
        [(whole((slots, wide)), shaped((slots, wide), BF))] * 2,
        "cond_forward", 6,
        scalars=place,
    )


def beside(ref, y):
    return jnp.concatenate(
        [ref[:, at : at + 128] for at in range(y * 128, ref.shape[1], 256)], axis=1
    )


def middle_forward_kernel(
    place_ref, rows_ref, mine_ref, theirs_ref, gains_ref, key_ref, value_ref,
    out_own, out_other, cq_own, cq_other, co_own, co_other,
    x1_ref, second_ref, query_ref, mixed_ref, x2_ref, third_ref,
):
    rows, width = rows_ref.shape
    half = width // 2
    wide = out_own.shape[-1]
    slots = key_ref.shape[0]
    valid = iota((rows, slots), 1) < place_ref[3]
    lane = iota((rows, 128), 1)
    for out, cut in ((out_own, 0), (out_other, half)):
        total = rows_ref[:, cut : cut + half].astype(F32)
        for x in range(2):
            for y in range(2):
                mixed = jnp.where(
                    place_ref[2] == x, beside(mine_ref, y), beside(theirs_ref, y)
                )
                total += dot(mixed, weight_of(out, x, y), NT)
        x1_ref[:, cut : cut + half] = total
    normal, _ = normalize(x1_ref[...])
    second = (normal * gains_ref[1:2, :]).astype(BF)
    second_ref[...] = second
    for x in range(2):
        for y in range(2):
            at = (2 * x + y) * wide
            query = dot(second[:, :half], weight_of(cq_own, x, y)) + dot(
                second[:, half:], weight_of(cq_other, x, y)
            )
            query_ref[:, at : at + wide] = (query * 0.125).astype(BF)
    for at in range(0, 4 * wide, 128):
        query, key, value = (
            ref[:, at : at + 128] for ref in (query_ref, key_ref, value_ref)
        )
        mixed = []
        for head in range(2):
            part = jnp.where((lane // HD) == head, query, jnp.zeros_like(query))
            scores = jnp.where(valid, dot(part, key, NT), MASKED_SCORE)
            top = jnp.max(scores, axis=1, keepdims=True)
            weights = jnp.exp(scores - top)
            total = jnp.sum(weights, axis=1, keepdims=True)
            mixed.append(dot(weights.astype(BF), value) * (1.0 / total))
        mixed_ref[:, at : at + 128] = jnp.where(lane < HD, mixed[0], mixed[1]).astype(BF)
    for out, cut in ((co_own, 0), (co_other, half)):
        total = x1_ref[:, cut : cut + half]
        for x in range(2):
            for y in range(2):
                at = (2 * x + y) * wide
                total += dot(mixed_ref[:, at : at + wide], weight_of(out, x, y), NT)
        x2_ref[:, cut : cut + half] = total
    normal, _ = normalize(x2_ref[...])
    third_ref[...] = (normal * gains_ref[2:3, :]).astype(BF)


def middle_forward(place, rows, mine, theirs, gains, key, value, squares, after=()):
    full = whole(rows.shape)
    part = whole(mine.shape)
    cond = whole(key.shape)
    return call(
        middle_forward_kernel, (1,),
        [(full, rows), (part, mine), (part, theirs)]
        + [(whole(gains.shape), gains), (cond, key), (cond, value)] + sections(squares),
        [(full, shaped(rows.shape, dtype)) for dtype in (F32, BF, BF, BF, F32, BF)],
        "middle_forward", 26,
        after=after, scalars=place,
    )


def middle_backward_kernel(
    place_ref, d_ref, r_ref, top_ref, x2_ref, x1_ref, gains_ref,
    query_ref, key_ref, value_ref,
    out_own, out_other, cq_own, cq_other, co_own, co_other,
    dx1_ref, e2_ref, dquery_ref, dkey_ref, dvalue_ref, e1_ref, *refs,
):
    dmine_ref, dtheirs_ref, dmixed_ref = refs
    rows, width = x1_ref.shape
    half = width // 2
    wide = out_own.shape[-1]
    slots = key_ref.shape[0]
    grad_third = d_ref[...].astype(F32) + r_ref[...].astype(F32)
    normal, scale = normalize(x2_ref[...])
    dx2 = top_ref[...].astype(F32) + normalize_back(grad_third, gains_ref[2:3, :], normal, scale)
    dx1_ref[...] = dx2
    e2 = dx2.astype(BF)
    e2_ref[...] = e2
    for x in range(2):
        for y in range(2):
            at = (2 * x + y) * wide
            dmixed_ref[:, at : at + wide] = (
                dot(e2[:, :half], weight_of(co_own, x, y))
                + dot(e2[:, half:], weight_of(co_other, x, y))
            ).astype(BF)
    valid = iota((slots, rows), 0) < place_ref[3]
    lane = iota((slots, 128), 1)
    row = iota((128, slots), 0)
    for at in range(0, 4 * wide, 128):
        here = slice(at, at + 128)
        query, key, value, grads = (
            ref[:, here] for ref in (query_ref, key_ref, value_ref, dmixed_ref)
        )
        flipped = jnp.transpose(key.astype(F32)).astype(BF)
        dkeys, dvalues = [], []
        query_across = None
        for head in range(2):
            inside = (lane // HD) == head
            scores = dot(jnp.where(inside, key, jnp.zeros_like(key)), query, NT)
            scores = jnp.where(valid, scores, MASKED_SCORE)
            weights = jnp.exp(scores - jnp.max(scores, axis=0, keepdims=True))
            probs = weights * (1.0 / jnp.sum(weights, axis=0, keepdims=True))
            dprobs = dot(jnp.where(inside, value, jnp.zeros_like(value)), grads, NT)
            shared = jnp.sum(probs * dprobs, axis=0, keepdims=True)
            dscores = (probs * (dprobs - shared)).astype(BF)
            dvalues.append(dot(probs.astype(BF), grads))
            dkeys.append(dot(dscores, query))
            term = dot(jnp.where((row // HD) == head, flipped, jnp.zeros_like(flipped)), dscores)
            query_across = term if query_across is None else query_across + term
        dkey_ref[:, here] = jnp.where(lane < HD, dkeys[0], dkeys[1]).astype(BF)
        dvalue_ref[:, here] = jnp.where(lane < HD, dvalues[0], dvalues[1]).astype(BF)
        dquery_ref[:, here] = (jnp.transpose(query_across) * 0.125).astype(BF)
    parts = []
    for weight in (cq_own, cq_other):
        total = None
        for x in range(2):
            for y in range(2):
                at = (2 * x + y) * wide
                term = dot(dquery_ref[:, at : at + wide], weight_of(weight, x, y), NT)
                total = term if total is None else total + term
        parts.append(total)
    grad_second = jnp.concatenate(parts, axis=1)
    normal, scale = normalize(x1_ref[...])
    dx1 = dx1_ref[...] + normalize_back(grad_second, gains_ref[1:2, :], normal, scale)
    dx1_ref[...] = dx1
    e1 = dx1.astype(BF)
    e1_ref[...] = e1
    for y in range(2):
        first, second = (
            dot(e1[:, :half], weight_of(out_own, x, y))
            + dot(e1[:, half:], weight_of(out_other, x, y))
            for x in range(2)
        )
        low = place_ref[2] == 0
        for out, grads in (
            (dtheirs_ref, jnp.where(low, second, first).astype(BF)),
            (dmine_ref, jnp.where(low, first, second).astype(BF)),
        ):
            for j in range(wide // 128):
                at = (2 * j + y) * 128
                out[:, at : at + 128] = grads[:, j * 128 : (j + 1) * 128]


def middle_backward(
    place, d, r, top, x2, x1, gains, query, key, value, squares, after=()
):
    full = whole(x1.shape)
    rows, width = x1.shape
    part = (rows, width // 2)
    cond = whole(key.shape)
    return call(
        middle_backward_kernel, (1,),
        [(full, array) for array in (d, r, top, x2, x1)]
        + [(whole(gains.shape), gains), (full, query), (cond, key), (cond, value)]
        + sections(squares),
        [(full, shaped(x1.shape, F32)), (full, shaped(x1.shape, BF)), (full, shaped(x1.shape, BF))]
        + [(cond, shaped(key.shape, BF))] * 2
        + [(full, shaped(x1.shape, BF))]
        + [(whole(part), shaped(part, BF))] * 2,
        "middle_backward", 40,
        scratch=[pltpu.VMEM((rows, width), BF)],
        after=after,
        scalars=place,
    )


def middle_weights_kernel(
    pieces, place_ref, e1_ref, second_ref, dquery_ref, cond_ref, dkey_ref, dvalue_ref,
    e2_ref, mixed_ref, kv_own, kv_other, *rest,
):
    mine_refs, theirs_refs = rest[:pieces], rest[pieces : 2 * pieces]
    aown_ref, aother_ref, bown_ref, bother_ref, dcond_ref = rest[2 * pieces : 2 * pieces + 5]
    f1_ref, fsecond_ref, f2_ref, fcond_ref = rest[2 * pieces + 5 :]
    width = e1_ref.shape[1]
    half = width // 2
    wide = kv_own.shape[-1]
    shard = cond_ref.shape[1] // 8
    first = pl.program_id(0) == 0

    @pl.when(first)
    def _():
        for source, target in (
            (e1_ref, f1_ref), (second_ref, fsecond_ref), (e2_ref, f2_ref), (cond_ref, fcond_ref)
        ):
            target[...] = jnp.transpose(source[...])
        dcond_ref[...] = jnp.zeros_like(dcond_ref)

    from_theirs = pl.program_id(0) // 2 != place_ref[2]
    mixed = jnp.concatenate(
        [jnp.where(from_theirs, b[...], a[...]) for a, b in zip(mine_refs, theirs_refs)], axis=1
    )
    for part, (first_out, out, kv) in enumerate(
        ((aown_ref, bown_ref, kv_own), (aother_ref, bother_ref, kv_other))
    ):
        cut = slice(part * half, (part + 1) * half)
        first_out[0, 0, :, 0:wide] = dot(f1_ref[cut, :], mixed).astype(BF)
        first_out[0, 0, :, wide : 2 * wide] = dot(fsecond_ref[cut, :], dquery_ref[...]).astype(BF)
        out[0, 0, :, wide : 2 * wide] = dot(f2_ref[cut, :], mixed_ref[...]).astype(BF)
        weights = []
        for kind, grads in ((0, dkey_ref), (1, dvalue_ref)):
            at = part * 4 * shard
            both = dot(fcond_ref[at : at + 4 * shard, :], grads[...]).astype(BF)
            for z in range(4):
                low = (2 * z + kind) * shard
                out[0, 0, low : low + shard, 0:wide] = both[z * shard : (z + 1) * shard]
            weight = kv[:, 0, 0, 0, kind * shard : (kind + 1) * shard, :]
            weights.append(weight.reshape(4 * shard, wide))
        dcond_ref[:, part * 4 * shard : (part + 1) * 4 * shard] += dot(
            dkey_ref[...], weights[0], NT
        ) + dot(dvalue_ref[...], weights[1], NT)


def middle_weights(
    place, e1, mine, theirs, second, dquery, cond, dkey, dvalue, e2, mixed, square, after=()
):
    zs, _, _, _, square_shard, wide = square.shape
    rows, width = e1.shape
    slots = cond.shape[0]
    full = whole(e1.shape)
    block = pl.BlockSpec((rows, wide), lambda p, s: (0, p))
    pairs = [
        pl.BlockSpec((rows, 128), lambda p, s, j=j: (0, 2 * j + p % 2))
        for j in range(mine.shape[1] // 256)
    ]
    cond_block = pl.BlockSpec((slots, wide), lambda p, s: (0, p))
    shape = (zs, 1, 1, 1, square_shard, wide)
    own = pl.BlockSpec(shape, lambda p, s: (0, s[0], p % 2, p // 2, 0, 0))
    other = pl.BlockSpec(shape, lambda p, s: (0, 1 - s[0], p % 2, p // 2, 0, 0))
    out = pl.BlockSpec((1, 1, width // 2, 2 * wide), lambda p, s: (p // 2, p % 2, 0, 0))
    out_shape = (2, 2, width // 2, 2 * wide)
    return call(
        functools.partial(middle_weights_kernel, len(pairs)), (4,),
        [(full, e1), (full, second), (block, dquery)]
        + [(whole(cond.shape), cond), (cond_block, dkey), (cond_block, dvalue)]
        + [(full, e2), (block, mixed), (own, square), (other, square)]
        + [(pair, a) for a in (mine, theirs) for pair in pairs],
        [(out, shaped(out_shape, BF))] * 4 + [(whole(cond.shape), shaped(cond.shape, F32))],
        "middle_weights", 5,
        scratch=[pltpu.VMEM((width, rows), BF)] * 3 + [pltpu.VMEM((cond.shape[1], slots), BF)],
        after=after,
        scalars=place,
    )


def fold_kernel(place_ref, keep_ref, got_keep_ref, send_ref, got_send_ref, keep_out, send_out):
    send_out[...] = (send_ref[...].astype(F32) + got_send_ref[...].astype(F32)).astype(BF)
    keep_out[...] = (keep_ref[...].astype(F32) + got_keep_ref[...].astype(F32)).astype(BF)


def fold(place, bit, here, got, at):
    shape = here.shape
    before, after = math.prod(shape[:at]), math.prod(shape[at + 1 : -2])
    view = (before, 2, after) + shape[-2:]
    group = 2 if after % 2 == 0 else 1
    block = (1, 1, group) + shape[-2:]
    keep = pl.BlockSpec(block, lambda a, b, s: (a, s[bit], b, 0, 0))
    send = pl.BlockSpec(block, lambda a, b, s: (a, 1 - s[bit], b, 0, 0))
    out = pl.BlockSpec(block, lambda a, b, s: (a, 0, b, 0, 0))
    out_shape = shaped((before, 1, after) + shape[-2:], BF)
    here, got = here.reshape(view), got.reshape(view)
    results = call(
        fold_kernel, (before, after // group),
        [(keep, here), (keep, got), (send, here), (send, got)],
        [(out, out_shape)] * 2,
        "fold", here.size * 1.3e-6, scalars=place,
    )
    left = shape[:at] + (1,) + shape[at + 1 :]
    return [array.reshape(left) for array in results]


def finish_ffn(weight_ref, sources, gu_ref, down_ref):
    chunks = len(sources) // 2
    tiles = sources[0].shape[1] // (3 * TILE)
    hidden = chunks * tiles * TILE
    total = jnp.zeros((weight_ref.shape[0], 1), F32)
    for i in range(chunks):
        keep, got = sources[2 * i], sources[2 * i + 1]
        for j in range(tiles):
            at = 3 * j * TILE
            target = (i * tiles + j) * TILE
            grads = keep[:, at : at + 3 * TILE].astype(F32) + got[:, at : at + 3 * TILE].astype(F32)
            for kind in range(2):
                cut = slice(kind * hidden + target, kind * hidden + target + TILE)
                part = grads[:, kind * TILE : (kind + 1) * TILE]
                gu_ref[:, cut] = part
                total += jnp.sum(part * weight_ref[:, cut].astype(F32), axis=1, keepdims=True)
            down_ref[:, target : target + TILE] = grads[:, 2 * TILE :]
    return total


SUM_CHAINS = {
    "A": ("z1", "y", "z2"),
    "B": ("x", "z2", "z1"),
    "Q0": ("z2", "y", "z1"),
    "Q1": ("y", "z1", "z2"),
}
SUM_STEPS = (
    "Q0.0", "Q1.0", "out", "A.1", "B.1", "Q0.1", "Q1.1", "A.2", "Q0.2", "B.2", "in", "Q1.2",
)


def scatter_kernel(
    queries, their_dx_ref, *refs,
):
    few = 12 + 2 * CHUNKS
    sources, refs, fetched = refs[:few], refs[few : len(refs) - few], refs[len(refs) - few :]
    dx_ref, gain_ref, qkv_weight, query_weight, ffn_weight, x2_ref, y_ref = fetched[:7]
    y_got_ref, turn_ref, rows_ref, gains_ref, dx1_ref, *ffn_refs = fetched[7:]
    inputs, refs = refs[: 4 + 2 * queries], refs[4 + 2 * queries :]
    outs, refs = refs[:10], refs[10:]
    block_ref, dinput_ref, out_ref, cq_ref, ckv_ref, co_ref, qkv_ref, norm_ref = outs[:8]
    dx_slot, norm_slot, refs = refs[0], refs[1], refs[2:]
    works, slots, refs = refs[: 2 + queries], refs[2 + queries : 5 * (2 + queries)], refs[5 * (2 + queries) :]
    sends, receives, local_sems = refs
    dp, seq, side = (lax.axis_index(name) for name in ("dp", "seq", "half"))
    here = {"z2": dp // 4, "z1": (dp // 2) % 2, "c": dp % 2, "y": seq, "x": side}
    partners = {
        "z2": (dp + 4 - 8 * (dp // 4), seq, side),
        "z1": (dp + 2 - 4 * ((dp // 2) % 2), seq, side),
        "c": (dp + 1 - 2 * (dp % 2), seq, side),
        "y": (dp, 1 - seq, side),
        "x": (dp, seq, 1 - side),
    }
    barrier = pltpu.get_barrier_semaphore()
    for axis in AXES:
        pl.semaphore_signal(
            barrier, inc=1, device_id=partners[axis], device_id_type=pl.DeviceIdType.MESH
        )
    pl.semaphore_wait(barrier, len(AXES))
    count = [0, 0]

    def send(source, target, axis):
        copy = pltpu.make_async_remote_copy(
            source, target, sends.at[count[0]], receives.at[count[0]],
            device_id=partners[axis], device_id_type=pl.DeviceIdType.MESH,
        )
        count[0] += 1
        copy.start()
        return copy

    def load(source, target):
        copy = pltpu.make_async_copy(source, target, local_sems.at[count[1]])
        count[1] += 1
        copy.start()
        return copy

    def add(target, source):
        target[...] = (target[...].astype(F32) + source[...].astype(F32)).astype(BF)

    names = ["A", "B"] + ["Q%d" % i for i in range(queries)]
    work = dict(zip(names, works))
    slot = {name: slots[4 * i : 4 * i + 4] for i, name in enumerate(names)}
    first = dict.fromkeys(names, "y")
    first["B"] = "x"
    flying = {}
    for i in range(queries):
        own, other = inputs[4 + 2 * i], inputs[5 + 2 * i]
        name = "Q%d" % i
        flying[name] = [load(own, work[name]), send(other, slot[name][0], "c")]
    for i, name in enumerate("AB"):
        flying[name] = [load(inputs[2 * i], work[name]), load(inputs[2 * i + 1], slot[name][0])]

    def part(name, step, goes):
        index = [slice(None)] * 3
        for at, axis in enumerate(SUM_CHAINS[name][: step + 1]):
            place = {"z2": 1, "z1": 2}.get(axis, 0)
            index[place] = 1 - here[axis] if goes and at == step else here[axis]
        return work[name].at[tuple(index)]

    def advance(name, step):
        for copy in flying[name]:
            copy.wait()
        add(work[name] if step == 0 else part(name, step - 1, False), slot[name][step])
        target = slot[name][step + 1]
        flying[name] = [send(part(name, step, True), target, SUM_CHAINS[name][step])]

    def end(name):
        for copy in flying[name]:
            copy.wait()
        return part(name, 2, False)[...].astype(F32) + slot[name][3][...].astype(F32)

    odd = here["c"] == 1
    fetches = [load(source, target) for source, target in zip(sources, fetched)]
    advance("A", 0)
    advance("B", 0)
    dx_copy = send(their_dx_ref, dx_slot, "x")
    for event in SUM_STEPS:
        if event == "out":
            for copy in fetches:
                copy.wait()
            total = x2_ref[...] + (y_ref[...].astype(F32) + y_got_ref[...].astype(F32))
            total = total.astype(BF).astype(F32)
            block_ref[...] = put_back(total, turn_ref[...], odd, 1).astype(BF)
            third = finish_ffn(ffn_weight, ffn_refs, *outs[8:])
        elif event == "in":
            dx_copy.wait()
            normal, scale = normalize(rows_ref[...].astype(F32))
            grads = dx_ref[...].astype(F32) + dx_slot[...].astype(F32)
            total = dx1_ref[...] + normalize_back(grads, gains_ref[0:1, :], normal, scale)
            dinput_ref[...] = put_back(total, turn_ref[...], odd, 2)
        else:
            name, step = event.split(".")
            advance(name, int(step))

    wide = cq_ref.shape[1]
    grads = end("A")
    out_ref[...] = grads[:, :wide]
    cq_ref[...] = grads[:, wide:]
    second = jnp.sum(grads[:, wide:] * query_weight[...].astype(F32), axis=1, keepdims=True)
    grads = end("B")
    ckv_ref[...] = grads[:, :wide]
    co_ref[...] = grads[:, wide:]
    total = jnp.zeros(second.shape, F32)
    j = 0
    for name in names[2:]:
        grads = end(name)
        for at in range(0, grads.shape[1], 384):
            for kind in range(3):
                cut = slice(kind * wide + j * 128, kind * wide + (j + 1) * 128)
                piece = grads[:, at + kind * 128 : at + (kind + 1) * 128]
                qkv_ref[kind, :, j * 128 : (j + 1) * 128] = piece
                total += jnp.sum(piece * qkv_weight[:, cut].astype(F32), axis=1, keepdims=True)
            j += 1
    lane = iota(norm_ref.shape, 1)
    norm_ref[...] = jnp.where(
        lane == 0,
        total / gain_ref[:, 0:1],
        jnp.where(lane == 1, second / gain_ref[:, 1:2], jnp.where(lane == 2, third / gain_ref[:, 2:3], 0.0)),
    )
    for at, axis in enumerate(("y", "x")):
        send(norm_ref, norm_slot.at[at], axis).wait()
        norm_ref[...] += norm_slot[at]


def scatter_last(
    dx, their_dx, gain_columns, qkv_weight, query_weight, ffn_weight, ffn_sums, x2, y, y_got, turn, rows, gains,
    dx1, squares, queries,
):
    anywhere, vmem = pl.BlockSpec(memory_space=pl.ANY), pl.BlockSpec(memory_space=pltpu.VMEM)
    shard, wide = query_weight.shape
    shapes = [a.shape for a, _ in squares] + [a.shape for a, _ in queries]
    assert all(shape[:3] == (2, 2, 2) for shape in shapes)
    few = [dx, gain_columns, qkv_weight, query_weight, ffn_weight, x2, y, y_got, turn, rows]
    few += [gains, dx1, *ffn_sums]
    many = [a for pair in (*squares, *queries) for a in pair]
    outs = [(x2.shape, BF), (x2.shape, F32), ((shard, wide), F32), ((shard, wide), F32)]
    outs += [((shard, wide), F32), ((shard, wide), F32), ((3, shard, wide), F32)]
    outs += [((shard, 128), F32), (ffn_weight.shape, F32), ((shard, ffn_weight.shape[1] // 2), F32)]
    slots = [pltpu.VMEM(shape[at:], BF) for shape in shapes for at in range(4)]
    copies = 1 + 2 + len(queries) * 4 + len(squares) * 3
    return pl.pallas_call(
        functools.partial(scatter_kernel, len(queries)),
        in_specs=[anywhere] * (1 + len(few) + len(many)),
        out_specs=[vmem] * len(outs),
        out_shape=[shaped(*out) for out in outs],
        scratch_shapes=[pltpu.VMEM(rows.shape, BF), pltpu.VMEM((2, shard, 128), F32)]
        + [pltpu.VMEM(shape, BF) for shape in shapes]
        + slots
        + [
            pltpu.SemaphoreType.DMA((copies,)),
            pltpu.SemaphoreType.DMA((copies,)),
            pltpu.SemaphoreType.DMA((4 + len(queries) + len(few),)),
        ]
        + [pltpu.VMEM(a.shape, a.dtype) for a in few],
        compiler_params=pltpu.CompilerParams(
            vmem_limit_bytes=63 << 20, collective_id=1, has_side_effects=True
        ),
        name="scatter_last",
    )(their_dx, *few, *many)


def swap(array, axis, bit=1):
    return lax.ppermute(array, axis, [(i, i ^ bit) for i in range(lax.axis_size(axis))])


def pair_body(
    block_in,
    cond_tokens,
    cond_count,
    norm1_gain,
    norm2_gain,
    norm3_gain,
    qkv_weight,
    attn_out_weight,
    cross_q_weight,
    cross_kv_weight,
    cross_out_weight,
    gate_up_weight,
    down_weight,
    out_cotangent,
):
    rows, width = block_in.shape
    shard = qkv_weight.shape[0]
    head_cols = attn_out_weight.shape[0]
    hidden_cols = down_weight.shape[0]
    cond_slots, cond_width = cond_tokens.shape[1:]
    cond_shard = cross_kv_weight.shape[0]
    dp = lax.axis_index("dp")
    seq = lax.axis_index("seq")
    side = lax.axis_index("half")
    z_size = lax.axis_size("dp") // 2
    core, z = dp % 2, dp // 2
    odd = core.astype(jnp.int32).reshape(1)
    half = width // 2
    pairs_here = head_cols // 128
    per_chunk = hidden_cols // CHUNKS
    z_bits = []
    bit = z_size // 2
    while bit:
        z_bits.append(bit)
        bit //= 2

    qkv_pack = jnp.concatenate(
        [
            qkv_weight[:, :, j * 128 : (j + 1) * 128].reshape(shard, 384)
            for j in range(pairs_here)
        ],
        axis=1,
    )
    square_pack = jnp.concatenate(
        [
            attn_out_weight.T,
            cross_q_weight,
            cross_kv_weight.transpose(1, 0, 2).reshape(shard, head_cols),
            cross_out_weight.T,
        ],
        axis=1,
    )
    gains = jnp.stack([norm1_gain, norm2_gain, norm3_gain]).astype(F32)
    gains = lax.dynamic_update_slice(jnp.zeros((8, width), F32), gains, (0, dp * shard))
    places = {"half": 0, "seq": 1, "own": 1}
    steps = {"half": ("half", 1, 2), "seq": ("seq", 1, 1), "own": ("seq", 1, 6)}
    for at, bit in enumerate(z_bits):
        name = "z%d" % bit
        places[name] = 2 + at
        steps[name] = ("dp", 2 * bit, 4 + at)
    far, near = "z%d" % z_bits[0], "z%d" % z_bits[-1]

    gate_up_flat = gate_up_weight.reshape(shard, 2 * hidden_cols)
    (
        wq, w0, w1, w2, w3, mine_in, theirs_in, top_grads, gains, first_all, first_across, turn,
        *packs,
    ) = gather_first(
        qkv_pack, square_pack, gains, block_in, out_cotangent, gate_up_flat, down_weight.T
    )
    wq = wq.reshape((z_size, 2, 2) + qkv_pack.shape)
    squares = [w.reshape((z_size, 2, 2, 2, shard, head_cols)) for w in (w0, w1, w2, w3)]
    place = jnp.stack([core, seq, side, cond_count[seq], z // 2, z % 2, 0 * z]).astype(jnp.int32)
    their_top = swap(top_grads, "half")
    ffn_weights = []
    for pack in packs[:-1]:
        gathered = lax.all_gather(pack, ("dp", "seq"))
        ffn_weights.append(gathered.reshape((z_size, 2, 2) + pack.shape))

    def over(array, name, after):
        axis, bit, which = steps[name]
        array = hold(array, after)
        got, upper = swap(array, axis, bit), place[which] == 1
        return jnp.stack([jnp.where(upper, got, array), jnp.where(upper, array, got)], axis=-3)

    slab = over(packs[-1], far, (gains,))

    class Way:
        def __init__(self, own, other, wide, order):
            full = (2 if wide else 1, 2) + (2,) * len(z_bits) + (shard, own.shape[-1])
            self.order = list(order)
            self.here = own.reshape(full)
            self.got = swap(other, "dp", 1).reshape(full)

        def step(self, after=(), late=()):
            step = self.order.pop(0)
            if late:
                self.here = hold(self.here, late)
            axis, bit, which = steps[step]
            self.here, send = fold(place, which, self.here, self.got, places[step])
            if after:
                send = hold(send, after)
            self.got = swap(send, axis, bit)
            return self.here

        def end(self):
            while self.order:
                self.step()
            shape = self.here.shape[-2:]
            return [self.here.reshape(shape), self.got.reshape(shape)]

    along = jnp.arange(rows)
    tables = rot_tables(jnp.concatenate([side * rows + along, (1 - side) * rows + along]))
    query, key, value, mine, theirs, lse = self_forward(place, first_all, wq, tables)
    theirs = hold(theirs, (their_top,))
    slab = over(slab, near, (lse,))
    mixed = swap(theirs, "half")

    my_cond = hold(cond_tokens[seq], (theirs,)).reshape(cond_slots, z_size, 2, cond_shard)
    swapped = jnp.where(core == 1, my_cond[:, :, ::-1], my_cond)
    my_cond = swapped.transpose(0, 2, 1, 3).reshape(cond_slots, cond_width)
    my_cond = jnp.pad(my_cond, ((0, SLOTS - cond_slots), (0, 0)))
    top_across, their_top_across = across(hold(top_grads, (theirs,)), their_top)
    cross_key, cross_value = cond_forward(place, my_cond, squares[2])
    x1, second, cross_query, cross_mixed, x2, third = middle_forward(
        place, mine_in, mine, mixed, gains, cross_key, cross_value, squares,
        (top_across, their_top_across),
    )
    slab = slab.reshape((z_size,) + slab.shape[2:])
    their_third = swap(third, "half")
    (third_across,) = across(third)
    (their_third_across,) = across(their_third)
    ffn_weights[0] = hold(ffn_weights[0], (their_third_across, third_across))
    sums, ways, after = (), [], (slab,)
    for i in range(CHUNKS):
        *sums, gown, gother = ffn(
            place,
            (third, their_third),
            (third_across, their_third_across),
            (top_grads, their_top),
            (top_across, their_top_across),
            ffn_weights[i],
            TILE,
            sums,
            after,
        )
        if i == 0:
            slab = hold(slab, (sums[2],))
            far_slab = swap(slab, "seq")
            slabs = [slab, far_slab]
            ffn_weights.append(slabs + [swap(s, "dp", 1) for s in slabs])
        else:
            arrived = [far_slab if i == 1 else ways[0].got]
            gother = hold(gother, arrived)
        order = (near, "own", far) if i == CHUNKS - 1 else ("seq", near, far)
        ways.append(Way(gown, gother, False, order))
        if i < CHUNKS - 1:
            after = (ways[i].step(((far_slab, ways[0].got)[i],)),)
    ymine, ytheirs, dmine, dtheirs = sums
    d_received = swap(hold(dtheirs, arrived), "half")

    after = [ways[0].step(), ways[2].step()]
    y_received = swap(hold(ytheirs, (d_received, *after)), "half")
    dx1, e2, dquery, dkey, dvalue, e1, dmine, dtheirs = middle_backward(
        place, dmine, d_received, top_grads, x2, x1, gains,
        cross_query, cross_key, cross_value, squares, after,
    )
    dtheirs = swap(dtheirs, "half")
    aown, aother, bown, bother, dcond = middle_weights(
        place, e1, mine, mixed, second, dquery, my_cond, dkey, dvalue, e2, cross_mixed, squares[2]
    )
    arrived = [way.got for way in ways] + [dtheirs, y_received]
    aother, bother = hold(aother, arrived), hold(bother, arrived)
    first_way = Way(aown, aother, True, ("half", "seq", near, far))
    second_way = Way(bown, bother, True, ("seq", "half", near, far))
    qkv_grads = []
    pairs = 2 * pairs_here
    after = [aother] + [way.step() for way in ways if way.order]
    running = None
    for first, several in ((0, 2), (2, pairs - 2)):
        gown, gother, *sums = self_backward(
            place, query, key, value, mine, theirs, dmine, dtheirs, lse, tables, first_across,
            wq, first, several, running, first > 0, after,
        )
        full = (2, 2, 2, shard, gown.shape[-1])
        qkv_grads.append((gown.reshape(full), gother.reshape(full)))
        running = sums[0]
        if first == 0:
            arrived = [way.got for way in ways] + [first_way.got, second_way.got]
            running = hold(running, arrived)
            dcond = hold(dcond, (running,))
            after = [way.step(late=(running,)) for way in ways if way.order]
            after += [first_way.step(late=(running,)), second_way.step(late=(running,))]
    rmine, rtheirs = sums
    rtheirs = hold(rtheirs, (first_way.got, second_way.got, ways[-1].got))
    gain_columns = [g.astype(F32).reshape(shard, 1) for g in (norm1_gain, norm2_gain, norm3_gain)]
    (
        block_out, grad_input, grad_out, grad_cq, grad_ckv, grad_co, grad_qkv, gain_grads,
        grad_gate_up, grad_down,
    ) = scatter_last(
        rmine, rtheirs, jnp.concatenate(gain_columns, axis=1),
        qkv_weight.reshape(shard, 3 * head_cols), cross_q_weight,
        gate_up_flat, [array for way in ways for array in way.end()],
        x2, ymine, y_received, turn, mine_in, gains, dx1,
        [
            tuple(a.reshape((2, 2, 2) + a.shape[-2:]) for a in (way.here, way.got))
            for way in (first_way, second_way)
        ],
        qkv_grads,
    )
    grad_ckv = grad_ckv.reshape(2, cond_shard, head_cols).transpose(1, 0, 2)
    grad_qkv = grad_qkv.transpose(1, 0, 2)
    grad_gate_up = grad_gate_up.reshape(shard, 2, hidden_cols)

    dcond = dcond[:cond_slots].reshape(cond_slots, 2, z_size, cond_shard)
    dcond = jnp.where(core == 1, dcond[:, ::-1], dcond).transpose(0, 2, 1, 3)
    dcond = dcond.reshape(cond_slots, 2, 2, cond_width // 4)
    cond_keep = lax.dynamic_index_in_dim(dcond, side, 2, keepdims=False)
    cond_send = lax.dynamic_index_in_dim(dcond, 1 - side, 2, keepdims=False)
    dcond = cond_keep + swap(cond_send, "half")
    cond_keep = lax.dynamic_index_in_dim(dcond, seq, 1, keepdims=False)
    cond_send = lax.dynamic_index_in_dim(dcond, 1 - seq, 1, keepdims=False)
    cond_got = swap(cond_send, "seq")
    grad_cond = jnp.stack(
        [jnp.where(seq == 1, cond_got, cond_keep), jnp.where(seq == 1, cond_keep, cond_got)]
    )

    gain_grads = gain_grads[:, :3].T
    return (
        block_out,
        grad_input,
        grad_cond,
        gain_grads[0],
        gain_grads[1],
        gain_grads[2],
        grad_qkv,
        grad_out.T,
        grad_cq,
        grad_ckv,
        grad_co.T,
        grad_gate_up,
        grad_down.T,
    )


def pair_solution(mesh, sequences):
    dp, tensor = mesh.devices.shape
    finer = Mesh(mesh.devices.reshape(dp, sequences, tensor // sequences), ("dp", "seq", "half"))
    every = ("dp", "seq", "half")
    both = ("seq", "half")
    return jax.shard_map(
        pair_body,
        mesh=finer,
        in_specs=(
            P(every, None),
            P("dp", None, None),
            P("dp"),
            P("dp"),
            P("dp"),
            P("dp"),
            P("dp", None, both),
            P(both, "dp"),
            P("dp", both),
            P("dp", None, both),
            P(both, "dp"),
            P("dp", None, both),
            P(both, "dp"),
            P(every, None),
        ),
        out_specs=(
            P(every, None),
            P(every, None),
            P("dp", None, both),
            P("dp"),
            P("dp"),
            P("dp"),
            P("dp", None, both),
            P(both, "dp"),
            P("dp", both),
            P("dp", None, both),
            P(both, "dp"),
            P("dp", None, both),
            P(both, "dp"),
        ),
        check_vma=False,
    )


CHUNKS = 3
FLOPS = 1.15e9
TILE = 256
SLOTS = 144


def solution(mesh):
    dp, tensor = mesh.devices.shape

    def run(*args):
        block_in, cond_tokens, qkv, down = args[0], args[1], args[6], args[12]
        sequences = cond_tokens.shape[0] // dp
        fits = (
            sequences == 2
            and tensor == 4
            and dp == 8
            and qkv.shape[2] % (tensor * 128) == 0
            and (qkv.shape[0] // dp) % 64 == 0
            and down.shape[0] % (tensor * CHUNKS * TILE) == 0
            and qkv.shape[0] == 2 * cond_tokens.shape[2]
            and qkv.shape[2] == qkv.shape[0]
            and cond_tokens.shape[1] <= SLOTS
            and block_in.shape[0] == 1024 * cond_tokens.shape[0]
        )
        if fits:
            return pair_solution(mesh, sequences)(*args)
        return general_solution(mesh)(*args)

    return run
```
